256 devices in a mesh: row: 8 (over z_hi, y), col: 32 (over z_lo, x, core).
Axes of the slice: x: 4, y: 4, z: 8 (z_hi: 2, z_lo: 4; z = z_hi * 4 + z_lo), core: 2. Of those that a mesh axis runs over, the one named last changes fastest.
Arguments:
- object_field: float32 [2, 4096, 16384], P(None, 'row', 'col'), may hold values from -6 to 6
- probe_field: float32 [2, 384, 384], replicated, may hold values from -6 to 6
- intensities: bfloat16 [8, 32, 6, 384, 384], P('row', 'col'), may hold values from 0 to 4
- positions: int32 [8, 32, 6, 2], replicated, may hold values from 0 to 511, as said below
- tile_counts: int32 [8, 32], replicated, may hold values from 1 to 6, as said below
Outputs:
- new_object: float32 [2, 4096, 16384], P(None, 'row', 'col')
- new_probe: float32 [2, 384, 384], replicated
The draws below stay inside these ranges and needn't reach their ends.
Inputs may be any that keep to these rules, and one draw needn't show every extreme that they name: Each entry is a row in 0 to 512 - 1 (first component) or a column in 0 to 512 - 1 (second) of the tile; only slots below the tile's count are scan positions. `tile_counts`: ragged scan positions a tile; some tile holds 6.
All inputs are finite; a program needn't handle non-finite values.
Results may differ from the reference program's by a relative error of at most 0.0061.
The reference program's roundings to bfloat16 on the way count: a program that leaves them out, or rounds other values in their place, can miss the bound.
Values may be sent and summed in bfloat16 or wider, within the bound.
No kernel may reach another device: no remote copies, remote signals or barrier semaphores. Data moves between devices by JAX's collectives and lax.ppermute only.
A program may use at most 128 MiB of HBM per device.

```python
import jax
import jax.numpy as jnp
from jax import lax

PS = 384
HALF = 192
TH = 512
TW = 512
PMAX = 6
GRID_R = 8
GRID_C = 32
NY = 4096
NX = 16384


def draw_positions(key, part):
    key = jax.random.fold_in(key, 11)
    first_key, second_key, third_key = jax.random.split(key, 3)
    row_values = jax.random.randint(first_key, (GRID_R, GRID_C, PMAX, 1), 0, TH, dtype=jnp.int32)
    col_values = jax.random.randint(second_key, (GRID_R, GRID_C, PMAX, 1), 0, TW, dtype=jnp.int32)
    table = jnp.concatenate([row_values, col_values], axis=3).reshape(GRID_R * GRID_C, PMAX, 2)
    picks = jax.random.randint(third_key, (2,), 0, GRID_R * GRID_C, dtype=jnp.int32)
    table = table.at[picks[0], 0].set(jnp.array([TH - 1, TW - 1], dtype=jnp.int32))
    table = table.at[picks[1], 1].set(jnp.zeros((2,), jnp.int32))
    return table.reshape(GRID_R, GRID_C, PMAX, 2)


def draw_tile_counts(key, part):
    key = jax.random.fold_in(key, 23)
    first_key, second_key, third_key = jax.random.split(key, 3)
    base_counts = jax.random.randint(first_key, (GRID_R * GRID_C,), 1, PMAX // 2 + 1, dtype=jnp.int32)
    heavy_draw = jax.random.randint(second_key, (GRID_R * GRID_C,), 0, 8, dtype=jnp.int32)
    counts_drawn = jnp.where(heavy_draw == 0, jnp.int32(PMAX), base_counts)
    chosen = jax.random.randint(third_key, (), 0, GRID_R * GRID_C, dtype=jnp.int32)
    counts_drawn = counts_drawn.at[chosen].set(jnp.int32(PMAX))
    return counts_drawn.reshape(GRID_R, GRID_C)


def steps_of(key, shape, cuts, smallest, high):
    def one(axis_at, parts):
        steps = jax.random.uniform(jax.random.fold_in(jax.random.fold_in(key, 6), axis_at), (parts,), jnp.float32, smallest / len(cuts), high / len(cuts))
        return jnp.repeat(jnp.exp(steps), shape[axis_at] // parts).reshape((-1,) + (1,) * (len(shape) - axis_at - 1))

    gain = one(*cuts[0])
    for cut in cuts[1:]:
        gain = gain * one(*cut)
    return gain


def bell_draw(stream_key, dims, scale, reach, pieces=(), kind=jnp.bfloat16):
    entries = scale * jax.random.normal(stream_key, dims, jnp.float32)
    if pieces:
        entries = entries * steps_of(stream_key, dims, pieces, -0.22, 0.18)
    return jnp.clip(entries, -reach, reach).astype(kind)


def setup_inputs(seed: int = 0) -> dict:
    key_list = jax.random.split(jax.random.key(seed), 6)
    object_field = bell_draw(key_list[0], (2, NY, NX), 0.7071, 6.0, ((1, 8), (2, 32)), jnp.float32)
    probe_field = bell_draw(key_list[1], (2, PS, PS), 0.7071, 6.0, (), jnp.float32)
    intensities = jnp.clip(4.0 * jax.random.uniform(key_list[2], (GRID_R, GRID_C, PMAX, PS, PS), jnp.float32) ** steps_of(key_list[2], (GRID_R, GRID_C, PMAX, PS, PS), ((0, 8), (1, 32)), -0.2, 0.2), 0.0, 4.0).astype(jnp.bfloat16)
    positions = draw_positions(jax.random.fold_in(key_list[5], 71), 0)
    tile_counts = draw_tile_counts(jax.random.fold_in(key_list[5], 71), 0)
    return dict(object_field=object_field, probe_field=probe_field, intensities=intensities, positions=positions, tile_counts=tile_counts)


OBJECT_REG = 0.1
PROBE_REG = 0.1
PROBE_RATE = 0.5
EPSILON = 1e-06

def dft_tables(length):
    rows_index = lax.iota(jnp.int32, length)
    product = rows_index[:, None] * rows_index[None, :] % length
    angles = product.astype(jnp.float32) * (2.0 * jnp.pi / length)
    norm_factor = 1.0 / jnp.sqrt(jnp.float32(length))
    cos_table = (jnp.cos(angles) * norm_factor).astype(jnp.bfloat16)
    sin_table = (-jnp.sin(angles) * norm_factor).astype(jnp.bfloat16)
    forward_mix = jnp.concatenate([jnp.concatenate([cos_table, sin_table], axis=1), jnp.concatenate([-sin_table, cos_table], axis=1)], axis=0)
    adjoint_mix = jnp.concatenate([jnp.concatenate([cos_table, -sin_table], axis=1), jnp.concatenate([sin_table, cos_table], axis=1)], axis=0)
    return (cos_table, sin_table, forward_mix, adjoint_mix)

def exit_wave(window, probe_field):
    probe_real = probe_field[0]
    probe_imaginary = probe_field[1]
    object_real = window[0]
    object_imaginary = window[1]
    return jnp.concatenate([probe_real * object_real - probe_imaginary * object_imaginary, probe_real * object_imaginary + probe_imaginary * object_real], axis=1).astype(jnp.bfloat16)

def wave_gradient(wave_in, intensity, tables):
    cos_table, sin_table, forward_mix, adjoint_mix = tables
    length = cos_table.shape[0]
    cos_part = jnp.dot(cos_table, wave_in, preferred_element_type=jnp.float32)
    sin_part = jnp.dot(sin_table, wave_in, preferred_element_type=jnp.float32)
    halfway = jnp.concatenate([cos_part[:, :length] - sin_part[:, length:], sin_part[:, :length] + cos_part[:, length:]], axis=1).astype(jnp.bfloat16)
    far_field = jnp.dot(halfway, forward_mix, preferred_element_type=jnp.float32)
    far_real = far_field[:, :length]
    far_imaginary = far_field[:, length:]
    misfit = far_real * far_real + far_imaginary * far_imaginary - intensity.astype(jnp.float32)
    residual_wave = jnp.concatenate([misfit * far_real, misfit * far_imaginary], axis=1).astype(jnp.bfloat16)
    cos_back = jnp.dot(cos_table, residual_wave, preferred_element_type=jnp.float32)
    sin_back = jnp.dot(sin_table, residual_wave, preferred_element_type=jnp.float32)
    returning = jnp.concatenate([cos_back[:, :length] + sin_back[:, length:], cos_back[:, length:] - sin_back[:, :length]], axis=1).astype(jnp.bfloat16)
    return jnp.dot(returning, adjoint_mix, preferred_element_type=jnp.float32)

def deposit_terms(window, probe_field, gradient):
    length = window.shape[1]
    grad_real = gradient[:, :length]
    grad_imaginary = gradient[:, length:]
    probe_real = probe_field[0]
    probe_imaginary = probe_field[1]
    object_real = window[0]
    object_imaginary = window[1]
    object_term = jnp.stack([probe_real * grad_real + probe_imaginary * grad_imaginary, probe_real * grad_imaginary - probe_imaginary * grad_real])
    probe_term = jnp.stack([object_real * grad_real + object_imaginary * grad_imaginary, object_real * grad_imaginary - object_imaginary * grad_real, object_real * object_real + object_imaginary * object_imaginary])
    return (object_term, probe_term)

def reference(object_field, probe_field, intensities, positions, tile_counts):
    tables = dft_tables(PS)
    padded = jnp.pad(object_field, ((0, 0), (HALF, HALF), (HALF, HALF)))
    slot_total = GRID_R * GRID_C * PMAX
    slot_ids = lax.iota(jnp.int32, slot_total)
    tile_ids = slot_ids // PMAX
    live_slot = slot_ids % PMAX < tile_counts.reshape(-1)[tile_ids]
    flat_positions = positions.reshape(slot_total, 2)
    top_rows = (tile_ids // GRID_C * TH + flat_positions[:, 0]).astype(jnp.int32)
    left_cols = (tile_ids % GRID_C * TW + flat_positions[:, 1]).astype(jnp.int32)
    flat_intensity = intensities.reshape(slot_total, PS, PS)
    probe_power = probe_field[0] * probe_field[0] + probe_field[1] * probe_field[1]
    zero_index = jnp.zeros((), jnp.int32)

    def visit(carried, scanned):
        top_row, left_col, is_live, intensity = scanned

        def active(inner):
            accumulated, probe_sum = inner
            corner = (zero_index, top_row, left_col)
            window = lax.dynamic_slice(padded, corner, (2, PS, PS))
            gradient = wave_gradient(exit_wave(window, probe_field), intensity, tables)
            object_term, probe_term = deposit_terms(window, probe_field, gradient)
            update = jnp.concatenate([object_term, probe_power[None]], axis=0)
            current = lax.dynamic_slice(accumulated, corner, (3, PS, PS))
            accumulated = lax.dynamic_update_slice(accumulated, current + update, corner)
            return (accumulated, probe_sum + probe_term)

        def passive(inner):
            return inner
        return (lax.cond(is_live, active, passive, carried), None)
    initial = (jnp.zeros((3, NY + PS, NX + PS), jnp.float32), jnp.zeros((3, PS, PS), jnp.float32))
    finals, ignored = lax.scan(visit, initial, (top_rows, left_cols, live_slot, flat_intensity))
    accumulated, probe_sum = finals
    field = accumulated[:, HALF:HALF + NY, HALF:HALF + NX]
    denominator = field[2] + OBJECT_REG * jnp.max(probe_power)
    new_object = object_field - field[:2] / denominator
    probe_denominator = probe_sum[2] + PROBE_REG * jnp.max(probe_sum[2])
    direction = probe_sum[:2] / probe_denominator
    spread = jnp.sqrt(jnp.mean(direction[0] * direction[0] + direction[1] * direction[1]) + EPSILON)
    new_probe = probe_field - PROBE_RATE * direction / spread
    return (new_object, new_probe)
```

```python
import functools

import jax
import jax.numpy as jnp
import ml_dtypes
import numpy as np
from jax import lax
from jax.experimental import pallas as pl
from jax.experimental.pallas import tpu as pltpu
from jax.sharding import PartitionSpec as P

OBJECT_REG = 0.1
PROBE_REG = 0.1
PROBE_RATE = 0.5
EPSILON = 1e-06

PS = 384
HALF = 192
TH = 512
TW = 512
PMAX = 6
EH = TH + PS
EW = TW + 512
CANVAS = 1280
TILES = 224
STEP = 32
F32 = jnp.float32
BF16 = jnp.bfloat16


def dft_blocks():
    index = np.arange(PS)
    product = (index[:, None] * index[None, :]) % PS
    angles = product.astype(np.float32) * np.float32(2.0 * np.pi / PS)
    norm = np.float32(1.0) / np.sqrt(np.float32(PS))
    cos = (np.cos(angles) * norm).astype(ml_dtypes.bfloat16)
    sin = (-np.sin(angles) * norm).astype(ml_dtypes.bfloat16)
    forward = np.block([[cos, sin], [-sin, cos]])
    adjoint = np.block([[cos, -sin], [sin, cos]])
    return forward, adjoint


def lane_parts(column):
    block = column // 128
    return block, column - block * 128


def rolled_out(blocks, shift, lanes):
    turned = [pltpu.roll(b, shift, axis=1) for b in blocks]
    keep = lanes >= shift
    zero = jnp.zeros_like(turned[0])
    return [
        jnp.where(keep, turned[0], zero),
        jnp.where(keep, turned[1], turned[0]),
        jnp.where(keep, turned[2], turned[1]),
        jnp.where(keep, zero, turned[2]),
    ]


def rolled_in(blocks, shift, lanes):
    turned = [pltpu.roll(b, (128 - shift) % 128, axis=1) for b in blocks]
    keep = lanes < 128 - shift
    return [jnp.where(keep, turned[k], turned[k + 1]) for k in range(3)]


def illumination_kernel(place, positions, counts, probe, out, canvas, power):
    for k in range(PS // STEP):
        rows = pl.ds(k * STEP, STEP)
        power[rows, :] = probe[0, rows, :] * probe[0, rows, :] + probe[1, rows, :] * probe[1, rows, :]
    for j in range(CANVAS // 128):
        canvas[j, pl.ds(PS, TH), :] = jnp.zeros((TH, 128), F32)
    lanes = lax.broadcasted_iota(jnp.int32, (STEP, 128), 1)
    grid_r, grid_c = 8, 32

    def tile(k, carry):
        down, across = k // 3 - 1, k % 3 - 1
        row, col = place[0] + down, place[1] + across
        inside = (row >= 0) & (row < grid_r) & (col >= 0) & (col < grid_c)
        owner = jnp.where(inside, row * grid_c + col, 0)
        count = jnp.where(inside, counts[owner], 0)

        def slot(s, inner):
            where = (owner * PMAX + s) * 2
            top = positions[where] + down * TH - HALF + PS
            left = positions[where + 1] + across * TW - HALF + PS
            meets = (top > 0) & (top < PS + TH) & (left > 0) & (left < PS + TW)

            @pl.when(meets)
            def _():
                block, shift = lane_parts(left)

                def chunk(c, deep):
                    rows = pl.ds(pl.multiple_of(c * STEP, STEP), STEP)
                    parts = rolled_out([power[rows, pl.ds(j * 128, 128)] for j in range(3)], shift, lanes)
                    for j in range(4):
                        canvas[block + j, pl.ds(top + c * STEP, STEP), :] += parts[j]
                    return deep

                lax.fori_loop(0, PS // STEP, chunk, 0)

            return inner

        return lax.fori_loop(0, count, slot, carry)

    lax.fori_loop(0, 9, tile, 0)
    floor = OBJECT_REG * jnp.max(power[...])
    for j in range(TW // 128):
        out[:, pl.ds(j * 128, 128)] = 1.0 / (canvas[PS // 128 + j, pl.ds(PS, TH), :] + floor)


def main_kernel(
    place, positions, counts, center, above, below, before, after, corners_before, corners_after,
    probe, intensity, forward, adjoint,
    field, rim_before, rim_after, rim_above, rim_below, sums,
    extended, total, wave, halfway, residual, returning, gradient, window, probe_sum,
):
    slots = place[0] * 32 + place[1]
    count = counts[slots]
    lanes = lax.broadcasted_iota(jnp.int32, (STEP, 128), 1)
    total[...] = jnp.zeros_like(total)
    probe_sum[...] = jnp.zeros_like(probe_sum)
    for p in range(2):
        for j in range(EW // 128):
            if 2 <= j < 6:
                middle, cols = center, pl.ds((j - 2) * 128, 128)
                over, under, low = above, below, 0
            else:
                cols = pl.ds(j % 2 * 128, 128)
                middle, over = (before, corners_before) if j < 2 else (after, corners_after)
                under, low = over, HALF
            extended[p, j, pl.ds(0, HALF), :] = over[p, pl.ds(0, HALF), cols].astype(F32)
            extended[p, j, pl.ds(HALF, TH), :] = middle[p, :, cols].astype(F32)
            extended[p, j, pl.ds(HALF + TH, HALF), :] = under[p, pl.ds(low, HALF), cols].astype(F32)

    def slot(s, carry):
        top = positions[(slots * PMAX + s) * 2]
        block, shift = lane_parts(positions[(slots * PMAX + s) * 2 + 1] + 64)

        def leave(c, inner):
            rows = pl.ds(pl.multiple_of(c * STEP, STEP), STEP)
            cells = []
            for p in range(2):
                found = [extended[p, block + j, pl.ds(top + c * STEP, STEP), :] for j in range(4)]
                cells.append(jnp.concatenate(rolled_in(found, shift, lanes), axis=1))
                window[p, rows, :] = cells[p]
            pr, pi = probe[0, rows, :], probe[1, rows, :]
            wave[rows, :] = (pr * cells[0] - pi * cells[1]).astype(BF16)
            wave[pl.ds(pl.multiple_of(PS + c * STEP, STEP), STEP), :] = (pr * cells[1] + pi * cells[0]).astype(BF16)
            return inner

        lax.fori_loop(0, PS // STEP, leave, 0)
        half = jnp.dot(adjoint[...], wave[...], preferred_element_type=F32).astype(BF16)
        halfway[:, pl.ds(0, PS)] = half[:PS]
        halfway[:, pl.ds(PS, PS)] = half[PS:]
        far = jnp.dot(halfway[...], forward[...], preferred_element_type=F32)
        far_r, far_i = far[:, :PS], far[:, PS:]
        misfit = far_r * far_r + far_i * far_i - intensity[s].astype(F32)
        residual[pl.ds(0, PS), :] = (misfit * far_r).astype(BF16)
        residual[pl.ds(PS, PS), :] = (misfit * far_i).astype(BF16)
        back = jnp.dot(forward[...], residual[...], preferred_element_type=F32).astype(BF16)
        returning[:, pl.ds(0, PS)] = back[:PS]
        returning[:, pl.ds(PS, PS)] = back[PS:]
        wave_back = jnp.dot(returning[...], adjoint[...], preferred_element_type=F32)
        gradient[...] = wave_back

        def deposit(c, inner):
            rows = pl.ds(pl.multiple_of(c * STEP, STEP), STEP)
            gr, gi = gradient[rows, pl.ds(0, PS)], gradient[rows, pl.ds(PS, PS)]
            pr, pi = probe[0, rows, :], probe[1, rows, :]
            wr, wi = window[0, rows, :], window[1, rows, :]
            for p, term in ((0, pr * gr + pi * gi), (1, pr * gi - pi * gr)):
                parts = rolled_out([term[:, j * 128 : (j + 1) * 128] for j in range(3)], shift, lanes)
                for j in range(4):
                    total[p, block + j, pl.ds(top + c * STEP, STEP), :] += parts[j]
            probe_sum[0, rows, :] += wr * gr + wi * gi
            probe_sum[1, rows, :] += wr * gi - wi * gr
            probe_sum[2, rows, :] += wr * wr + wi * wi
            return inner

        lax.fori_loop(0, PS // STEP, deposit, 0)
        return carry

    lax.fori_loop(0, count, slot, 0)
    for p in range(2):
        for j in range(EW // 128):
            if 2 <= j < 6:
                cols = pl.ds((j - 2) * 128, 128)
                field[p, :, cols] = total[p, j, pl.ds(HALF, TH), :]
                rim_above[p, :, cols] = total[p, j, pl.ds(0, HALF), :]
                rim_below[p, :, cols] = total[p, j, pl.ds(HALF + TH, HALF), :]
            else:
                rim = rim_before if j < 2 else rim_after
                rim[p, :, pl.ds(j % 2 * 128, 128)] = total[p, j].astype(BF16)
    at = 0
    for p in range(3):
        for k in range(PS // 16):
            for j in range(3):
                sums[at] = probe_sum[p, pl.ds(k * 16, 16), pl.ds(j * 128, 128)].astype(BF16)
                at += 1
    sums[pl.ds(at, TILES - at)] = jnp.zeros((TILES - at, 16, 128), BF16)


def object_kernel(center, field, from_before, from_after, from_above, from_below, weight, out):
    for k in range(TH // 64):
        rows = pl.ds(k * 64, 64)
        outer = pl.ds(HALF + k * 64, 64)
        for p in range(2):
            cells = field[p, rows, :]
            sides = [from_before[p, outer, :], from_after[p, outer, :]]
            cells = cells + jnp.concatenate(sides, axis=1).astype(F32)
            if k * 64 < HALF:
                cells = cells + from_above[p, rows, :].astype(F32)
            if k * 64 >= TH - HALF:
                cells = cells + from_below[p, pl.ds(k * 64 - TH + HALF, 64), :].astype(F32)
            out[p, rows, :] = center[p, rows, :] - cells * weight[rows, :]


def probe_kernel(sums, probe, out, planes):
    at = 0
    for p in range(3):
        for k in range(PS // 16):
            for j in range(3):
                planes[p, pl.ds(k * 16, 16), pl.ds(j * 128, 128)] = sums[at].astype(F32)
                at += 1
    floor = PROBE_REG * jnp.max(planes[2])
    square = jnp.zeros((STEP, PS), F32)
    for k in range(PS // STEP):
        rows = pl.ds(k * STEP, STEP)
        weight = 1.0 / (planes[2, rows, :] + floor)
        for p in range(2):
            direction = planes[p, rows, :] * weight
            planes[p, rows, :] = direction
            square = square + direction * direction
    spread = jnp.sqrt(jnp.sum(square) / (PS * PS) + EPSILON)
    for p in range(2):
        out[p] = probe[p] - PROBE_RATE * planes[p] / spread


SMEM = pl.BlockSpec(memory_space=pltpu.SMEM)
VMEM = pl.BlockSpec(memory_space=pltpu.VMEM)


def params(mib):
    return pltpu.CompilerParams(vmem_limit_bytes=mib << 20)


def shifted(value, axis, step):
    size = lax.axis_size(axis)
    low, high = max(0, -step), min(size, size - step)
    return lax.ppermute(value, axis, [(k, k + step) for k in range(low, high)])


def summed_everywhere(sums):
    core = lax.axis_index("col") % 2
    cols = lax.axis_size("col")
    groups = [list(range(c, cols, 2)) for c in range(2)]
    members = cols // 2
    partner = [(k, k ^ 1) for k in range(cols)]
    halves = sums.reshape(2, TILES // 2, 16, 128)
    kept = lax.dynamic_index_in_dim(halves, core, 0, keepdims=False)
    given = lax.dynamic_index_in_dim(halves, 1 - core, 0, keepdims=False)
    mine = (kept.astype(F32) + lax.ppermute(given, "col", partner).astype(F32)).astype(BF16)
    mine = mine.reshape(members, -1, 16, 128)
    parts = lax.all_to_all(mine, "col", 0, 0, axis_index_groups=groups)
    piece = jnp.sum(parts.astype(F32), axis=0).astype(BF16)
    rows = lax.axis_size("row")
    parts = lax.all_to_all(jnp.broadcast_to(piece[None], (rows,) + piece.shape), "row", 0, 0)
    piece = jnp.sum(parts.astype(F32), axis=0).astype(BF16)
    half = lax.all_to_all(
        jnp.broadcast_to(piece[None], (members,) + piece.shape), "col", 0, 0, axis_index_groups=groups
    ).reshape(TILES // 2, 16, 128)
    other = lax.ppermute(half, "col", partner)
    return jnp.where(core == 0, jnp.concatenate([half, other]), jnp.concatenate([other, half]))


def on_device(object_field, probe_field, intensities, positions, tile_counts):
    place = jnp.stack([lax.axis_index("row"), lax.axis_index("col")]).astype(jnp.int32)
    where = positions.reshape(-1)
    counts = tile_counts.reshape(-1)
    forward, adjoint = dft_blocks()
    rounded = object_field.astype(BF16)
    above = shifted(rounded[:, TH - HALF :, :], "row", 1)
    below = shifted(rounded[:, :HALF, :], "row", -1)
    before = shifted(rounded[:, :, TW - 256 :], "col", 1)
    after = shifted(rounded[:, :, :256], "col", -1)
    weight = pl.pallas_call(
        illumination_kernel,
        out_shape=jax.ShapeDtypeStruct((TH, TW), F32),
        in_specs=[SMEM, SMEM, SMEM, VMEM],
        out_specs=VMEM,
        scratch_shapes=[pltpu.VMEM((CANVAS // 128, CANVAS, 128), F32), pltpu.VMEM((PS, PS), F32)],
        compiler_params=params(24),
        cost_estimate=pl.CostEstimate(flops=20_000_000, bytes_accessed=20_000_000, transcendentals=0),
        name="illumination",
    )(place, where, counts, probe_field)
    corners = jnp.concatenate([above, below], axis=1)
    corners_before = shifted(corners[:, :, TW - 256 :], "col", 1)
    corners_after = shifted(corners[:, :, :256], "col", -1)
    like = jax.ShapeDtypeStruct
    field, rim_before, rim_after, rim_above, rim_below, sums = pl.pallas_call(
        main_kernel,
        out_shape=(
            like((2, TH, TW), F32),
            like((2, EH, 256), BF16),
            like((2, EH, 256), BF16),
            like((2, HALF, TW), F32),
            like((2, HALF, TW), F32),
            like((TILES, 16, 128), BF16),
        ),
        in_specs=[SMEM] * 3 + [VMEM] * 11,
        out_specs=(VMEM,) * 6,
        scratch_shapes=[
            pltpu.VMEM((2, EW // 128, EH, 128), F32),
            pltpu.VMEM((2, EW // 128, EH, 128), F32),
            pltpu.VMEM((2 * PS, PS), BF16),
            pltpu.VMEM((PS, 2 * PS), BF16),
            pltpu.VMEM((2 * PS, PS), BF16),
            pltpu.VMEM((PS, 2 * PS), BF16),
            pltpu.VMEM((PS, 2 * PS), F32),
            pltpu.VMEM((2, PS, PS), F32),
            pltpu.VMEM((3, PS, PS), F32),
        ],
        compiler_params=params(56),
        name="slots",
    )(
        place, where, counts, object_field, above, below, before, after, corners_before, corners_after,
        probe_field, intensities.reshape(PMAX, PS, PS), jnp.asarray(forward), jnp.asarray(adjoint),
    )
    from_before = shifted(rim_after, "col", 1)
    from_after = shifted(rim_before, "col", -1)
    up = rim_above + jnp.concatenate([from_before[:, :HALF], from_after[:, :HALF]], axis=2).astype(F32)
    down = rim_below + jnp.concatenate([from_before[:, HALF + TH :], from_after[:, HALF + TH :]], axis=2).astype(F32)
    from_below = shifted(up.astype(BF16), "row", -1)
    from_above = shifted(down.astype(BF16), "row", 1)
    everywhere = summed_everywhere(sums)
    new_object = pl.pallas_call(
        object_kernel,
        out_shape=like((2, TH, TW), F32),
        in_specs=[VMEM] * 7,
        out_specs=VMEM,
        compiler_params=params(24),
        cost_estimate=pl.CostEstimate(flops=4_000_000, bytes_accessed=12_000_000, transcendentals=0),
        name="new_object",
    )(object_field, field, from_before, from_after, from_above, from_below, weight)
    new_probe = pl.pallas_call(
        probe_kernel,
        out_shape=like((2, PS, PS), F32),
        in_specs=[VMEM] * 2,
        out_specs=VMEM,
        scratch_shapes=[pltpu.VMEM((3, PS, PS), F32)],
        compiler_params=params(24),
        name="new_probe",
    )(everywhere, probe_field)
    return (new_object, new_probe)


def solution(mesh):
    placed = (P(None, "row", "col"), P(), P("row", "col", None, None, None), P(), P())
    return jax.shard_map(
        on_device,
        mesh=mesh,
        in_specs=placed,
        out_specs=(P(None, "row", "col"), P()),
        check_vma=False,
    )
```

```python
import functools

import jax
import jax.numpy as jnp
import ml_dtypes
import numpy as np
from jax import lax
from jax.experimental import pallas as pl
from jax.experimental.pallas import tpu as pltpu
from jax.sharding import PartitionSpec as P

OBJECT_REG = 0.1
PROBE_REG = 0.1
PROBE_RATE = 0.5
EPSILON = 1e-06

PS = 384
HALF = 192
TH = 512
TW = 512
PMAX = 6
EH = TH + PS
EW = TW + 512
CANVAS = 1280
TILES = 224
STEP = 32
BAND = 96
F32 = jnp.float32
BF16 = jnp.bfloat16


def dft_blocks():
    index = np.arange(PS)
    product = (index[:, None] * index[None, :]) % PS
    angles = product.astype(np.float32) * np.float32(2.0 * np.pi / PS)
    norm = np.float32(1.0) / np.sqrt(np.float32(PS))
    cos = (np.cos(angles) * norm).astype(ml_dtypes.bfloat16)
    sin = (-np.sin(angles) * norm).astype(ml_dtypes.bfloat16)
    forward = np.block([[cos, sin], [-sin, cos]])
    adjoint = np.block([[cos, -sin], [sin, cos]])
    return forward, adjoint


def lane_parts(column):
    block = column // 128
    return block, column - block * 128


def rolled_out(blocks, shift, lanes):
    turned = [pltpu.roll(b, shift, axis=1) for b in blocks]
    keep = lanes >= shift
    zero = jnp.zeros_like(turned[0])
    return [
        jnp.where(keep, turned[0], zero),
        jnp.where(keep, turned[1], turned[0]),
        jnp.where(keep, turned[2], turned[1]),
        jnp.where(keep, zero, turned[2]),
    ]


def rolled_in(blocks, shift, lanes):
    turned = [pltpu.roll(b, (128 - shift) % 128, axis=1) for b in blocks]
    keep = lanes < 128 - shift
    return [jnp.where(keep, turned[k], turned[k + 1]) for k in range(3)]


def illumination_kernel(place, positions, counts, probe, out, canvas, power):
    power[0] = jnp.zeros((PS, 128), F32)
    power[4] = jnp.zeros((PS, 128), F32)
    for j in range(3):
        cols = pl.ds(j * 128, 128)
        power[j + 1] = probe[0, :, cols] * probe[0, :, cols] + probe[1, :, cols] * probe[1, :, cols]
    first, last = PS // 128, (PS + TW) // 128
    for j in range(first, last):
        canvas[j, pl.ds(PS, TH), :] = jnp.zeros((TH, 128), F32)
    lanes = lax.broadcasted_iota(jnp.int32, (BAND, 128), 1)
    grid_r, grid_c = 8, 32

    def tile(k, carry):
        down, across = k // 3 - 1, k % 3 - 1
        row, col = place[0] + down, place[1] + across
        inside = (row >= 0) & (row < grid_r) & (col >= 0) & (col < grid_c)
        owner = jnp.where(inside, row * grid_c + col, 0)
        count = jnp.where(inside, counts[owner], 0)

        def slot(s, inner):
            where = (owner * PMAX + s) * 2
            top = positions[where] + down * TH - HALF + PS
            left = positions[where + 1] + across * TW - HALF + PS
            meets = (top > 0) & (top < PS + TH) & (left > 0) & (left < PS + TW)

            @pl.when(meets)
            def _():
                block, shift = lane_parts(left)
                low = jnp.maximum(PS - top, 0) // BAND
                high = (jnp.minimum(PS + TH - top, PS) + BAND - 1) // BAND

                def column(j, wide):
                    def band(c, deep):
                        rows = pl.ds(pl.multiple_of(c * BAND, BAND), BAND)
                        here = pltpu.roll(power[j - block + 1, rows, :], shift, axis=1)
                        past = pltpu.roll(power[j - block, rows, :], shift, axis=1)
                        canvas[j, pl.ds(top + c * BAND, BAND), :] += jnp.where(lanes >= shift, here, past)
                        return deep

                    return lax.fori_loop(low, high, band, wide)

                lax.fori_loop(jnp.maximum(block, first), jnp.minimum(block + 4, last), column, 0)

            return inner

        return lax.fori_loop(0, count, slot, carry)

    lax.fori_loop(0, 9, tile, 0)
    floor = OBJECT_REG * jnp.max(power[...])
    for j in range(TW // 128):
        out[:, pl.ds(j * 128, 128)] = 1.0 / (canvas[first + j, pl.ds(PS, TH), :] + floor)


def main_kernel(
    place, positions, counts, center, above, below, before, after, corners_before, corners_after,
    probe, intensity, forward, adjoint,
    field, rim_before, rim_after, rim_above, rim_below, kept, given,
    extended, total, wave, halfway, residual, returning, gradient, window, probe_sum,
):
    slots = place[0] * 32 + place[1]
    count = counts[slots]
    lanes = lax.broadcasted_iota(jnp.int32, (STEP, 128), 1)
    total[...] = jnp.zeros_like(total)
    probe_sum[...] = jnp.zeros_like(probe_sum)
    for p in range(2):
        for j in range(EW // 128):
            if 2 <= j < 6:
                middle, cols = center, pl.ds((j - 2) * 128, 128)
                over, under, low = above, below, 0
            else:
                cols = pl.ds(j % 2 * 128, 128)
                middle, over = (before, corners_before) if j < 2 else (after, corners_after)
                under, low = over, HALF
            extended[p, j, pl.ds(0, HALF), :] = over[p, pl.ds(0, HALF), cols].astype(F32)
            extended[p, j, pl.ds(HALF, TH), :] = middle[p, :, cols].astype(F32)
            extended[p, j, pl.ds(HALF + TH, HALF), :] = under[p, pl.ds(low, HALF), cols].astype(F32)

    def slot(s, carry):
        top = positions[(slots * PMAX + s) * 2]
        block, shift = lane_parts(positions[(slots * PMAX + s) * 2 + 1] + 64)

        def leave(c, inner):
            rows = pl.ds(pl.multiple_of(c * STEP, STEP), STEP)
            cells = []
            for p in range(2):
                found = [extended[p, block + j, pl.ds(top + c * STEP, STEP), :] for j in range(4)]
                cells.append(jnp.concatenate(rolled_in(found, shift, lanes), axis=1))
                window[p, rows, :] = cells[p]
            pr, pi = probe[0, rows, :], probe[1, rows, :]
            wave[rows, :] = (pr * cells[0] - pi * cells[1]).astype(BF16)
            wave[pl.ds(pl.multiple_of(PS + c * STEP, STEP), STEP), :] = (pr * cells[1] + pi * cells[0]).astype(BF16)
            return inner

        lax.fori_loop(0, PS // STEP, leave, 0)
        half = jnp.dot(adjoint[...], wave[...], preferred_element_type=F32).astype(BF16)
        halfway[:, pl.ds(0, PS)] = half[:PS]
        halfway[:, pl.ds(PS, PS)] = half[PS:]
        far = jnp.dot(halfway[...], forward[...], preferred_element_type=F32)
        far_r, far_i = far[:, :PS], far[:, PS:]
        misfit = far_r * far_r + far_i * far_i - intensity[s].astype(F32)
        residual[pl.ds(0, PS), :] = (misfit * far_r).astype(BF16)
        residual[pl.ds(PS, PS), :] = (misfit * far_i).astype(BF16)
        back = jnp.dot(forward[...], residual[...], preferred_element_type=F32).astype(BF16)
        returning[:, pl.ds(0, PS)] = back[:PS]
        returning[:, pl.ds(PS, PS)] = back[PS:]
        wave_back = jnp.dot(returning[...], adjoint[...], preferred_element_type=F32)
        gradient[...] = wave_back

        def deposit(c, inner):
            rows = pl.ds(pl.multiple_of(c * STEP, STEP), STEP)
            gr, gi = gradient[rows, pl.ds(0, PS)], gradient[rows, pl.ds(PS, PS)]
            pr, pi = probe[0, rows, :], probe[1, rows, :]
            wr, wi = window[0, rows, :], window[1, rows, :]
            for p, term in ((0, pr * gr + pi * gi), (1, pr * gi - pi * gr)):
                parts = rolled_out([term[:, j * 128 : (j + 1) * 128] for j in range(3)], shift, lanes)
                for j in range(4):
                    total[p, block + j, pl.ds(top + c * STEP, STEP), :] += parts[j]
            probe_sum[0, rows, :] += wr * gr + wi * gi
            probe_sum[1, rows, :] += wr * gi - wi * gr
            probe_sum[2, rows, :] += wr * wr + wi * wi
            return inner

        lax.fori_loop(0, PS // STEP, deposit, 0)
        return carry

    lax.fori_loop(0, count, slot, 0)
    for p in range(2):
        for j in range(EW // 128):
            if 2 <= j < 6:
                cols = pl.ds((j - 2) * 128, 128)
                field[p, :, cols] = total[p, j, pl.ds(HALF, TH), :]
                rim_above[p, :, cols] = total[p, j, pl.ds(0, HALF), :]
                rim_below[p, :, cols] = total[p, j, pl.ds(HALF + TH, HALF), :]
            else:
                rim = rim_before if j < 2 else rim_after
                rim[p, :, pl.ds(j % 2 * 128, 128)] = total[p, j].astype(BF16)
    for core in range(2):

        @pl.when(place[1] % 2 == core)
        def _():
            for ref, half, kind in ((kept, core, F32), (given, 1 - core, BF16)):
                for at in range(TILES // 2):
                    found = half * (TILES // 2) + at
                    if found < 216:
                        p, k, j = found // 72, found // 3 % 24, found % 3
                        ref[at] = probe_sum[p, pl.ds(k * 16, 16), pl.ds(j * 128, 128)].astype(kind)
                    else:
                        ref[at] = jnp.zeros((16, 128), kind)


def object_kernel(center, field, from_before, from_after, from_above, from_below, weight, out):
    for k in range(TH // 64):
        rows = pl.ds(k * 64, 64)
        outer = pl.ds(HALF + k * 64, 64)
        for p in range(2):
            cells = field[p, rows, :]
            sides = [from_before[p, outer, :], from_after[p, outer, :]]
            cells = cells + jnp.concatenate(sides, axis=1).astype(F32)
            if k * 64 < HALF:
                cells = cells + from_above[p, rows, :].astype(F32)
            if k * 64 >= TH - HALF:
                cells = cells + from_below[p, pl.ds(k * 64 - TH + HALF, 64), :].astype(F32)
            out[p, rows, :] = center[p, rows, :] - cells * weight[rows, :]


def probe_kernel(place, half, other, probe, out, sums, planes):
    core = place[1] % 2
    sums[pl.ds(core * (TILES // 2), TILES // 2)] = half[...]
    sums[pl.ds((1 - core) * (TILES // 2), TILES // 2)] = other[...]
    at = 0
    for p in range(3):
        for k in range(PS // 16):
            for j in range(3):
                planes[p, pl.ds(k * 16, 16), pl.ds(j * 128, 128)] = sums[at].astype(F32)
                at += 1
    floor = PROBE_REG * jnp.max(planes[2])
    square = jnp.zeros((STEP, PS), F32)
    for k in range(PS // STEP):
        rows = pl.ds(k * STEP, STEP)
        weight = 1.0 / (planes[2, rows, :] + floor)
        for p in range(2):
            direction = planes[p, rows, :] * weight
            planes[p, rows, :] = direction
            square = square + direction * direction
    spread = jnp.sqrt(jnp.sum(square) / (PS * PS) + EPSILON)
    for p in range(2):
        out[p] = probe[p] - PROBE_RATE * planes[p] / spread


SMEM = pl.BlockSpec(memory_space=pltpu.SMEM)
VMEM = pl.BlockSpec(memory_space=pltpu.VMEM)


def params(mib):
    return pltpu.CompilerParams(vmem_limit_bytes=mib << 20)


def shifted(value, axis, step):
    size = lax.axis_size(axis)
    low, high = max(0, -step), min(size, size - step)
    return lax.ppermute(value, axis, [(k, k + step) for k in range(low, high)])


def on_device(object_field, probe_field, intensities, positions, tile_counts):
    place = jnp.stack([lax.axis_index("row"), lax.axis_index("col")]).astype(jnp.int32)
    where = positions.reshape(-1)
    counts = tile_counts.reshape(-1)
    forward, adjoint = dft_blocks()
    rounded = object_field.astype(BF16)
    above = shifted(rounded[:, TH - HALF :, :], "row", 1)
    below = shifted(rounded[:, :HALF, :], "row", -1)
    before = shifted(rounded[:, :, TW - 256 :], "col", 1)
    after = shifted(rounded[:, :, :256], "col", -1)
    weight = pl.pallas_call(
        illumination_kernel,
        out_shape=jax.ShapeDtypeStruct((TH, TW), F32),
        in_specs=[SMEM, SMEM, SMEM, VMEM],
        out_specs=VMEM,
        scratch_shapes=[pltpu.VMEM((CANVAS // 128, CANVAS, 128), F32), pltpu.VMEM((5, PS, 128), F32)],
        compiler_params=params(24),
        cost_estimate=pl.CostEstimate(flops=20_000_000, bytes_accessed=20_000_000, transcendentals=0),
        name="illumination",
    )(place, where, counts, probe_field)
    corners = jnp.concatenate([above, below], axis=1)
    corners_before = shifted(corners[:, :, TW - 256 :], "col", 1)
    corners_after = shifted(corners[:, :, :256], "col", -1)
    corners_before, corners_after, weight = lax.optimization_barrier((corners_before, corners_after, weight))
    like = jax.ShapeDtypeStruct
    field, rim_before, rim_after, rim_above, rim_below, kept, given = pl.pallas_call(
        main_kernel,
        out_shape=(
            like((2, TH, TW), F32),
            like((2, EH, 256), BF16),
            like((2, EH, 256), BF16),
            like((2, HALF, TW), F32),
            like((2, HALF, TW), F32),
            like((TILES // 2, 16, 128), F32),
            like((TILES // 2, 16, 128), BF16),
        ),
        in_specs=[SMEM] * 3 + [VMEM] * 11,
        out_specs=(VMEM,) * 7,
        scratch_shapes=[
            pltpu.VMEM((2, EW // 128, EH, 128), F32),
            pltpu.VMEM((2, EW // 128, EH, 128), F32),
            pltpu.VMEM((2 * PS, PS), BF16),
            pltpu.VMEM((PS, 2 * PS), BF16),
            pltpu.VMEM((2 * PS, PS), BF16),
            pltpu.VMEM((PS, 2 * PS), BF16),
            pltpu.VMEM((PS, 2 * PS), F32),
            pltpu.VMEM((2, PS, PS), F32),
            pltpu.VMEM((3, PS, PS), F32),
        ],
        compiler_params=params(56),
        name="slots",
    )(
        place, where, counts, object_field, above, below, before, after, corners_before, corners_after,
        probe_field, intensities.reshape(PMAX, PS, PS), jnp.asarray(forward), jnp.asarray(adjoint),
    )
    core = place[1] % 2
    cols, rows = lax.axis_size("col"), lax.axis_size("row")
    groups = [list(range(c, cols, 2)) for c in range(2)]
    members = cols // 2
    partner = [(k, k ^ 1) for k in range(cols)]
    arrived = lax.ppermute(given, "col", partner)
    from_before = shifted(rim_after, "col", 1)
    from_after = shifted(rim_before, "col", -1)
    mine = (kept + arrived.astype(F32)).astype(BF16).reshape(members, -1, 16, 128)
    parts = lax.all_to_all(mine, "col", 0, 0, axis_index_groups=groups)
    up = rim_above + jnp.concatenate([from_before[:, :HALF], from_after[:, :HALF]], axis=2).astype(F32)
    down = rim_below + jnp.concatenate([from_before[:, HALF + TH :], from_after[:, HALF + TH :]], axis=2).astype(F32)
    parts, up, down = lax.optimization_barrier((parts, up.astype(BF16), down.astype(BF16)))
    from_below = shifted(up, "row", -1)
    from_above = shifted(down, "row", 1)
    piece = jnp.sum(parts.astype(F32), axis=0).astype(BF16)
    parts = lax.all_to_all(jnp.broadcast_to(piece[None], (rows,) + piece.shape), "row", 0, 0)
    piece = jnp.sum(parts.astype(F32), axis=0).astype(BF16)
    half = lax.all_to_all(
        jnp.broadcast_to(piece[None], (members,) + piece.shape), "col", 0, 0, axis_index_groups=groups
    ).reshape(TILES // 2, 16, 128)
    new_object = pl.pallas_call(
        object_kernel,
        out_shape=like((2, TH, TW), F32),
        in_specs=[VMEM] * 7,
        out_specs=VMEM,
        compiler_params=params(24),
        cost_estimate=pl.CostEstimate(flops=4_000_000, bytes_accessed=12_000_000, transcendentals=0),
        name="new_object",
    )(object_field, field, from_before, from_after, from_above, from_below, weight)
    half, new_object = lax.optimization_barrier((half, new_object))
    other = lax.ppermute(half, "col", partner)
    new_probe = pl.pallas_call(
        probe_kernel,
        out_shape=like((2, PS, PS), F32),
        in_specs=[SMEM, VMEM, VMEM, VMEM],
        out_specs=VMEM,
        scratch_shapes=[pltpu.VMEM((TILES, 16, 128), BF16), pltpu.VMEM((3, PS, PS), F32)],
        compiler_params=params(24),
        name="new_probe",
    )(place, half, other, probe_field)
    return (new_object, new_probe)


def solution(mesh):
    placed = (P(None, "row", "col"), P(), P("row", "col", None, None, None), P(), P())
    return jax.shard_map(
        on_device,
        mesh=mesh,
        in_specs=placed,
        out_specs=(P(None, "row", "col"), P()),
        check_vma=False,
    )
```

```python
import functools

import jax
import jax.numpy as jnp
import ml_dtypes
import numpy as np
from jax import lax
from jax.experimental import pallas as pl
from jax.experimental.pallas import tpu as pltpu
from jax.sharding import PartitionSpec as P

OBJECT_REG = 0.1
PROBE_REG = 0.1
PROBE_RATE = 0.5
EPSILON = 1e-06

PS = 384
HALF = 192
TH = 512
TW = 512
PMAX = 6
EH = TH + PS
EW = TW + 512
CANVAS = 1280
TILES = 224
STEP = 128
BAND = 96
PART = 64
F32 = jnp.float32
BF16 = jnp.bfloat16


def dft_blocks():
    index = np.arange(PS)
    product = (index[:, None] * index[None, :]) % PS
    angles = product.astype(np.float32) * np.float32(2.0 * np.pi / PS)
    norm = np.float32(1.0) / np.sqrt(np.float32(PS))
    cos = (np.cos(angles) * norm).astype(ml_dtypes.bfloat16)
    sin = (-np.sin(angles) * norm).astype(ml_dtypes.bfloat16)
    forward = np.block([[cos, sin], [-sin, cos]])
    order = np.arange(2 * PS).reshape(2, 3, 128).transpose(1, 0, 2).reshape(-1)
    return forward[:, order]


def lane_parts(column):
    block = column // 128
    return block, column - block * 128


def rolled_out(blocks, shift, lanes):
    turned = [pltpu.roll(b, shift, axis=1) for b in blocks]
    keep = lanes >= shift
    zero = jnp.zeros_like(turned[0])
    return [
        jnp.where(keep, turned[0], zero),
        jnp.where(keep, turned[1], turned[0]),
        jnp.where(keep, turned[2], turned[1]),
        jnp.where(keep, zero, turned[2]),
    ]


def rolled_in(blocks, shift, lanes):
    turned = [pltpu.roll(b, (128 - shift) % 128, axis=1) for b in blocks]
    keep = lanes < 128 - shift
    return [jnp.where(keep, turned[k], turned[k + 1]) for k in range(3)]


def illumination_kernel(place, positions, counts, probe, out, canvas, power):
    power[0] = jnp.zeros((PS, 128), F32)
    power[4] = jnp.zeros((PS, 128), F32)
    for j in range(3):
        cols = pl.ds(j * 128, 128)
        power[j + 1] = probe[0, :, cols] * probe[0, :, cols] + probe[1, :, cols] * probe[1, :, cols]
    first, last = PS // 128, (PS + TW) // 128
    for j in range(first, last):
        canvas[j, pl.ds(PS, TH), :] = jnp.zeros((TH, 128), F32)
    lanes = lax.broadcasted_iota(jnp.int32, (BAND, 128), 1)
    grid_r, grid_c = 8, 32

    def tile(k, carry):
        down, across = k // 3 - 1, k % 3 - 1
        row, col = place[0] + down, place[1] + across
        inside = (row >= 0) & (row < grid_r) & (col >= 0) & (col < grid_c)
        owner = jnp.where(inside, row * grid_c + col, 0)
        count = jnp.where(inside, counts[owner], 0)

        def slot(s, inner):
            where = (owner * PMAX + s) * 2
            top = positions[where] + down * TH - HALF + PS
            left = positions[where + 1] + across * TW - HALF + PS
            meets = (top > 0) & (top < PS + TH) & (left > 0) & (left < PS + TW)

            @pl.when(meets)
            def _():
                block, shift = lane_parts(left)
                low = jnp.maximum(PS - top, 0) // BAND
                high = (jnp.minimum(PS + TH - top, PS) + BAND - 1) // BAND

                def column(j, wide):
                    def band(c, deep):
                        rows = pl.ds(pl.multiple_of(c * BAND, BAND), BAND)
                        here = pltpu.roll(power[j - block + 1, rows, :], shift, axis=1)
                        past = pltpu.roll(power[j - block, rows, :], shift, axis=1)
                        canvas[j, pl.ds(top + c * BAND, BAND), :] += jnp.where(lanes >= shift, here, past)
                        return deep

                    return lax.fori_loop(low, high, band, wide)

                lax.fori_loop(jnp.maximum(block, first), jnp.minimum(block + 4, last), column, 0)

            return inner

        return lax.fori_loop(0, count, slot, carry)

    lax.fori_loop(0, 9, tile, 0)
    floor = OBJECT_REG * jnp.max(power[...])
    for j in range(TW // 128):
        out[:, pl.ds(j * 128, 128)] = 1.0 / (canvas[first + j, pl.ds(PS, TH), :] + floor)


def main_kernel(
    place, positions, counts, center, above, below, before, after, corners_before, corners_after,
    probe_in, intensity_in, forward_in,
    field, rim_before, rim_after, rim_above, rim_below, kept, given,
    extended, total, wave, halfway, residual, returning, turned, window, probe_sum,
    probe, intensity, forward, adjoint, copied, slot_copied,
):
    slots = place[0] * 32 + place[1]
    count = counts[slots]

    def inward(s):
        return pltpu.make_async_copy(intensity_in.at[s], intensity.at[s], slot_copied.at[s])

    pairs = [(probe_in, probe), (forward_in, forward)]
    for p in range(2):
        for j in range(4):
            pairs.append((center.at[p, :, pl.ds(j * 128, 128)], extended.at[p, j + 2, pl.ds(HALF, TH), :]))
    copies = [pltpu.make_async_copy(a, b, copied.at[k]) for k, (a, b) in enumerate(pairs)]
    for copy in copies:
        copy.start()
    lax.fori_loop(0, count, lambda s, carry: (inward(s).start(), carry)[1], 0)
    total[...] = jnp.zeros_like(total)
    probe_sum[...] = jnp.zeros_like(probe_sum)
    for p in range(2):
        for j in range(EW // 128):
            if 2 <= j < 6:
                cols = pl.ds((j - 2) * 128, 128)
                over, under, low = above, below, 0
            else:
                cols = pl.ds(j % 2 * 128, 128)
                middle, over = (before, corners_before) if j < 2 else (after, corners_after)
                under, low = over, HALF
                extended[p, j, pl.ds(HALF, TH), :] = middle[p, :, cols].astype(F32)
            extended[p, j, pl.ds(0, HALF), :] = over[p, pl.ds(0, HALF), cols].astype(F32)
            extended[p, j, pl.ds(HALF + TH, HALF), :] = under[p, pl.ds(low, HALF), cols].astype(F32)
    for copy in copies:
        copy.wait()
    for k in range(2):
        for j in range(6):
            here = (pl.ds(k * PS, PS), pl.ds(j * 128, 128))
            adjoint[here] = forward[here] if k == j % 2 else -forward[here]

    def place_of(s):
        top = positions[(slots * PMAX + s) * 2]
        return (top,) + lane_parts(positions[(slots * PMAX + s) * 2 + 1] + 64)

    def leave(s, k):
        top, block, shift = place_of(s)
        lanes = lax.broadcasted_iota(jnp.int32, (PART, 128), 1)
        for at in range(k * 128, (k + 1) * 128, PART):
            rows = pl.ds(at, PART)
            cells = []
            for p in range(2):
                found = [extended[p, block + j, pl.ds(top + at, PART), :] for j in range(4)]
                cells.append(jnp.concatenate(rolled_in(found, shift, lanes), axis=1))
                window[s % 2, p, rows, :] = cells[p]
            pr, pi = probe[0, rows, :], probe[1, rows, :]
            wave[pl.ds(k * 128 + at, PART), :] = (pr * cells[0] - pi * cells[1]).astype(BF16)
            wave[pl.ds(k * 128 + at + 128, PART), :] = (pr * cells[1] + pi * cells[0]).astype(BF16)

    for k in range(3):
        leave(0, k)

    def slot(s, carry):
        top, block, shift = place_of(s)
        half = jnp.dot(adjoint[...], wave[...], preferred_element_type=F32).astype(BF16)
        halfway[:, pl.ds(0, PS)] = half[:PS]
        halfway[:, pl.ds(PS, PS)] = half[PS:]
        inward(s).wait()
        for j in range(3):
            cols = pl.ds(j * 128, 128)
            far = jnp.dot(halfway[...], forward[:, pl.ds(j * 256, 256)], preferred_element_type=F32)
            far_r, far_i = far[:, :128], far[:, 128:]
            misfit = far_r * far_r + far_i * far_i - intensity[s, :, cols].astype(F32)
            real, imaginary = (misfit * far_r).astype(BF16), (misfit * far_i).astype(BF16)
            for k in range(3):
                residual[pl.ds(k * 256, 128), cols] = real[k * 128 : (k + 1) * 128]
                residual[pl.ds(k * 256 + 128, 128), cols] = imaginary[k * 128 : (k + 1) * 128]
            leave(jnp.minimum(s + 1, count - 1), j)
        back = jnp.dot(forward[...], residual[...], preferred_element_type=F32).astype(BF16)
        returning[:, pl.ds(0, PS)] = back[:PS]
        returning[:, pl.ds(PS, PS)] = back[PS:]
        lanes = lax.broadcasted_iota(jnp.int32, (PART, 128), 1)
        for j in range(3):
            cols = pl.ds(j * 128, 128)
            gradient = jnp.dot(returning[...], adjoint[:, pl.ds(j * 256, 256)], preferred_element_type=F32)
            for k in range(PS // PART):
                rows = pl.ds(k * PART, PART)
                gr, gi = gradient[k * PART : (k + 1) * PART, :128], gradient[k * PART : (k + 1) * PART, 128:]
                pr, pi = probe[0, rows, cols], probe[1, rows, cols]
                wr, wi = window[s % 2, 0, rows, cols], window[s % 2, 1, rows, cols]
                for p, term in ((0, pr * gr + pi * gi), (1, pr * gi - pi * gr)):
                    term = pltpu.roll(term, shift, axis=1)
                    past = turned[p, rows, :] if j else jnp.zeros_like(term)
                    total[p, block + j, pl.ds(top + k * PART, PART), :] += jnp.where(lanes >= shift, term, past)
                    if j < 2:
                        turned[p, rows, :] = term
                    else:
                        total[p, block + 3, pl.ds(top + k * PART, PART), :] += jnp.where(lanes < shift, term, 0.0)
                probe_sum[0, rows, cols] += wr * gr + wi * gi
                probe_sum[1, rows, cols] += wr * gi - wi * gr
                probe_sum[2, rows, cols] += wr * wr + wi * wi
        return carry

    lax.fori_loop(0, count, slot, 0)
    pairs = []
    for p in range(2):
        for j in range(4):
            cols = pl.ds(j * 128, 128)
            pairs.append((total.at[p, j + 2, pl.ds(HALF, TH), :], field.at[p, :, cols]))
            pairs.append((total.at[p, j + 2, pl.ds(0, HALF), :], rim_above.at[p, :, cols]))
            pairs.append((total.at[p, j + 2, pl.ds(HALF + TH, HALF), :], rim_below.at[p, :, cols]))
    copies = [pltpu.make_async_copy(a, b, copied.at[k]) for k, (a, b) in enumerate(pairs)]
    for copy in copies:
        copy.start()
    for p in range(2):
        for j in (0, 1, 6, 7):
            rim = rim_before if j < 2 else rim_after
            rim[p, :, pl.ds(j % 2 * 128, 128)] = total[p, j].astype(BF16)
    for core in range(2):

        @pl.when(place[1] % 2 == core)
        def _():
            for ref, half, kind in ((kept, core, F32), (given, 1 - core, BF16)):
                for at in range(TILES // 2):
                    found = half * (TILES // 2) + at
                    if found < 216:
                        p, k, j = found // 72, found // 3 % 24, found % 3
                        ref[at] = probe_sum[p, pl.ds(k * 16, 16), pl.ds(j * 128, 128)].astype(kind)
                    else:
                        ref[at] = jnp.zeros((16, 128), kind)

    for copy in copies:
        copy.wait()


def object_kernel(center, field, from_before, from_after, from_above, from_below, weight, out):
    for k in range(TH // 64):
        rows = pl.ds(k * 64, 64)
        outer = pl.ds(HALF + k * 64, 64)
        for p in range(2):
            cells = field[p, rows, :]
            sides = [from_before[p, outer, :], from_after[p, outer, :]]
            cells = cells + jnp.concatenate(sides, axis=1).astype(F32)
            if k * 64 < HALF:
                cells = cells + from_above[p, rows, :].astype(F32)
            if k * 64 >= TH - HALF:
                cells = cells + from_below[p, pl.ds(k * 64 - TH + HALF, 64), :].astype(F32)
            out[p, rows, :] = center[p, rows, :] - cells * weight[rows, :]


def probe_kernel(place, half, other, probe, out, sums, planes):
    core = place[1] % 2
    sums[pl.ds(core * (TILES // 2), TILES // 2)] = half[...]
    sums[pl.ds((1 - core) * (TILES // 2), TILES // 2)] = other[...]
    at = 0
    for p in range(3):
        for k in range(PS // 16):
            for j in range(3):
                planes[p, pl.ds(k * 16, 16), pl.ds(j * 128, 128)] = sums[at].astype(F32)
                at += 1
    floor = PROBE_REG * jnp.max(planes[2])
    square = jnp.zeros((STEP, PS), F32)
    for k in range(PS // STEP):
        rows = pl.ds(k * STEP, STEP)
        weight = 1.0 / (planes[2, rows, :] + floor)
        for p in range(2):
            direction = planes[p, rows, :] * weight
            planes[p, rows, :] = direction
            square = square + direction * direction
    spread = jnp.sqrt(jnp.sum(square) / (PS * PS) + EPSILON)
    for p in range(2):
        out[p] = probe[p] - PROBE_RATE * planes[p] / spread


SMEM = pl.BlockSpec(memory_space=pltpu.SMEM)
VMEM = pl.BlockSpec(memory_space=pltpu.VMEM)
ANY = pl.BlockSpec(memory_space=pl.ANY)


def params(mib):
    return pltpu.CompilerParams(vmem_limit_bytes=mib << 20)


def shifted(value, axis, step):
    size = lax.axis_size(axis)
    low, high = max(0, -step), min(size, size - step)
    return lax.ppermute(value, axis, [(k, k + step) for k in range(low, high)])


def slots_call(*arrays):
    like = jax.ShapeDtypeStruct
    forward = dft_blocks()
    return pl.pallas_call(
        main_kernel,
        out_shape=(
            like((2, TH, TW), F32),
            like((2, EH, 256), BF16),
            like((2, EH, 256), BF16),
            like((2, HALF, TW), F32),
            like((2, HALF, TW), F32),
            like((TILES // 2, 16, 128), F32),
            like((TILES // 2, 16, 128), BF16),
        ),
        in_specs=[SMEM] * 3 + [ANY] + [VMEM] * 6 + [ANY] * 3,
        out_specs=(ANY, VMEM, VMEM, ANY, ANY, VMEM, VMEM),
        scratch_shapes=[
            pltpu.VMEM((2, EW // 128, EH, 128), F32),
            pltpu.VMEM((2, EW // 128, EH, 128), F32),
            pltpu.VMEM((2 * PS, PS), BF16),
            pltpu.VMEM((PS, 2 * PS), BF16),
            pltpu.VMEM((2 * PS, PS), BF16),
            pltpu.VMEM((PS, 2 * PS), BF16),
            pltpu.VMEM((2, PS, 128), F32),
            pltpu.VMEM((2, 2, PS, PS), F32),
            pltpu.VMEM((3, PS, PS), F32),
            pltpu.VMEM((2, PS, PS), F32),
            pltpu.VMEM((PMAX, PS, PS), BF16),
            pltpu.VMEM((2 * PS, 2 * PS), BF16),
            pltpu.VMEM((2 * PS, 2 * PS), BF16),
            pltpu.SemaphoreType.DMA((24,)),
            pltpu.SemaphoreType.DMA((PMAX,)),
        ],
        compiler_params=params(40),
        name="slots",
    )(*arrays, jnp.asarray(forward))


def on_device(object_field, probe_field, intensities, positions, tile_counts):
    place = jnp.stack([lax.axis_index("row"), lax.axis_index("col")]).astype(jnp.int32)
    where = positions.reshape(-1)
    counts = tile_counts.reshape(-1)
    rounded = object_field.astype(BF16)
    above = shifted(rounded[:, TH - HALF :, :], "row", 1)
    below = shifted(rounded[:, :HALF, :], "row", -1)
    before = shifted(rounded[:, :, TW - 256 :], "col", 1)
    after = shifted(rounded[:, :, :256], "col", -1)
    weight = pl.pallas_call(
        illumination_kernel,
        out_shape=jax.ShapeDtypeStruct((TH, TW), F32),
        in_specs=[SMEM, SMEM, SMEM, VMEM],
        out_specs=VMEM,
        scratch_shapes=[pltpu.VMEM((CANVAS // 128, CANVAS, 128), F32), pltpu.VMEM((5, PS, 128), F32)],
        compiler_params=params(24),
        cost_estimate=pl.CostEstimate(flops=20_000_000, bytes_accessed=20_000_000, transcendentals=0),
        name="illumination",
    )(place, where, counts, probe_field)
    above, below, weight = lax.optimization_barrier((above, below, weight))
    corners = jnp.concatenate([above, below], axis=1)
    corners_before = shifted(corners[:, :, TW - 256 :], "col", 1)
    corners_after = shifted(corners[:, :, :256], "col", -1)
    like = jax.ShapeDtypeStruct
    field, rim_before, rim_after, rim_above, rim_below, kept, given = slots_call(
        place, where, counts, object_field, above, below, before, after, corners_before, corners_after,
        probe_field, intensities.reshape(PMAX, PS, PS),
    )
    core = place[1] % 2
    cols, rows = lax.axis_size("col"), lax.axis_size("row")
    groups = [list(range(c, cols, 2)) for c in range(2)]
    members = cols // 2
    partner = [(k, k ^ 1) for k in range(cols)]
    arrived = lax.ppermute(given, "col", partner)
    mine = (kept + arrived.astype(F32)).astype(BF16).reshape(members, -1, 16, 128)
    mine, rim_before, rim_after = lax.optimization_barrier((mine, rim_before, rim_after))
    from_before = shifted(rim_after, "col", 1)
    from_after = shifted(rim_before, "col", -1)
    parts = lax.all_to_all(mine, "col", 0, 0, axis_index_groups=groups)
    up = rim_above + jnp.concatenate([from_before[:, :HALF], from_after[:, :HALF]], axis=2).astype(F32)
    down = rim_below + jnp.concatenate([from_before[:, HALF + TH :], from_after[:, HALF + TH :]], axis=2).astype(F32)
    parts, up, down = lax.optimization_barrier((parts, up.astype(BF16), down.astype(BF16)))
    from_below = shifted(up, "row", -1)
    from_above = shifted(down, "row", 1)
    piece = jnp.sum(parts.astype(F32), axis=0).astype(BF16)
    parts = lax.all_to_all(jnp.broadcast_to(piece[None], (rows,) + piece.shape), "row", 0, 0)
    parts, from_below, from_above = lax.optimization_barrier((parts, from_below, from_above))
    piece = jnp.sum(parts.astype(F32), axis=0).astype(BF16)
    half = lax.all_to_all(
        jnp.broadcast_to(piece[None], (members,) + piece.shape), "col", 0, 0, axis_index_groups=groups
    ).reshape(TILES // 2, 16, 128)
    new_object = pl.pallas_call(
        object_kernel,
        out_shape=like((2, TH, TW), F32),
        in_specs=[VMEM] * 7,
        out_specs=VMEM,
        compiler_params=params(24),
        cost_estimate=pl.CostEstimate(flops=4_000_000, bytes_accessed=12_000_000, transcendentals=0),
        name="new_object",
    )(object_field, field, from_before, from_after, from_above, from_below, weight)
    half, new_object = lax.optimization_barrier((half, new_object))
    other = lax.ppermute(half, "col", partner)
    new_probe = pl.pallas_call(
        probe_kernel,
        out_shape=like((2, PS, PS), F32),
        in_specs=[SMEM, VMEM, VMEM, VMEM],
        out_specs=VMEM,
        scratch_shapes=[pltpu.VMEM((TILES, 16, 128), BF16), pltpu.VMEM((3, PS, PS), F32)],
        compiler_params=params(24),
        name="new_probe",
    )(place, half, other, probe_field)
    return (new_object, new_probe)


def solution(mesh):
    placed = (P(None, "row", "col"), P(), P("row", "col", None, None, None), P(), P())
    return jax.shard_map(
        on_device,
        mesh=mesh,
        in_specs=placed,
        out_specs=(P(None, "row", "col"), P()),
        check_vma=False,
    )
```

```python
import functools

import jax
import jax.numpy as jnp
import ml_dtypes
import numpy as np
from jax import lax
from jax.experimental import pallas as pl
from jax.experimental.pallas import tpu as pltpu
from jax.sharding import PartitionSpec as P

OBJECT_REG = 0.1
PROBE_REG = 0.1
PROBE_RATE = 0.5
EPSILON = 1e-06

PS = 384
HALF = 192
TH = 512
TW = 512
PMAX = 6
EH = TH + PS
EW = TW + 512
CANVAS = 1280
USED = 108
BLOCKS = 112
STEP = 128
BAND = 96
PART = 64
F32 = jnp.float32
BF16 = jnp.bfloat16


def dft_blocks():
    index = np.arange(PS)
    product = (index[:, None] * index[None, :]) % PS
    angles = product.astype(np.float32) * np.float32(2.0 * np.pi / PS)
    norm = np.float32(1.0) / np.sqrt(np.float32(PS))
    cos = (np.cos(angles) * norm).astype(ml_dtypes.bfloat16)
    sin = (-np.sin(angles) * norm).astype(ml_dtypes.bfloat16)
    forward = np.block([[cos, sin], [-sin, cos]])
    order = np.arange(2 * PS).reshape(2, 3, 128).transpose(1, 0, 2).reshape(-1)
    return forward[:, order]


def lane_parts(column):
    block = column // 128
    return block, column - block * 128


def rolled_out(blocks, shift, lanes):
    turned = [pltpu.roll(b, shift, axis=1) for b in blocks]
    keep = lanes >= shift
    zero = jnp.zeros_like(turned[0])
    return [
        jnp.where(keep, turned[0], zero),
        jnp.where(keep, turned[1], turned[0]),
        jnp.where(keep, turned[2], turned[1]),
        jnp.where(keep, zero, turned[2]),
    ]


def rolled_in(blocks, shift, lanes):
    turned = [pltpu.roll(b, (128 - shift) % 128, axis=1) for b in blocks]
    keep = lanes < 128 - shift
    return [jnp.where(keep, turned[k], turned[k + 1]) for k in range(3)]


def illumination_kernel(place, positions, counts, probe, out, canvas, power):
    for j in range(3):
        cols = pl.ds(j * 128, 128)
        power[j] = probe[0, :, cols] * probe[0, :, cols] + probe[1, :, cols] * probe[1, :, cols]
    first, last = PS // 128, (PS + TW) // 128
    for j in range(first, last):
        canvas[j, pl.ds(PS, TH), :] = jnp.zeros((TH, 128), F32)
    lanes = lax.broadcasted_iota(jnp.int32, (BAND, 128), 1)
    grid_r, grid_c = 8, 32

    def tile(k, carry):
        down, across = k // 3 - 1, k % 3 - 1
        row, col = place[0] + down, place[1] + across
        inside = (row >= 0) & (row < grid_r) & (col >= 0) & (col < grid_c)
        owner = jnp.where(inside, row * grid_c + col, 0)
        count = jnp.where(inside, counts[owner], 0)

        def slot(s, inner):
            where = (owner * PMAX + s) * 2
            top = positions[where] + down * TH - HALF + PS
            left = positions[where + 1] + across * TW - HALF + PS
            meets = (top > 0) & (top < PS + TH) & (left > 0) & (left < PS + TW)

            @pl.when(meets)
            def _():
                block, shift = lane_parts(left)
                low = jnp.maximum(PS - top, 0) // BAND
                high = (jnp.minimum(PS + TH - top, PS) + BAND - 1) // BAND

                def band(c, deep):
                    rows = pl.ds(pl.multiple_of(c * BAND, BAND), BAND)
                    parts = rolled_out([power[j, rows, :] for j in range(3)], shift, lanes)
                    for j in range(4):
                        canvas[block + j, pl.ds(top + c * BAND, BAND), :] += parts[j]
                    return deep

                lax.fori_loop(low, high, band, 0)

            return inner

        return lax.fori_loop(0, count, slot, carry)

    lax.fori_loop(0, 9, tile, 0)
    floor = OBJECT_REG * jnp.max(power[...])
    for j in range(TW // 128):
        out[:, pl.ds(j * 128, 128)] = 1.0 / (canvas[first + j, pl.ds(PS, TH), :] + floor)


def main_kernel(
    place, positions, counts, center, above_in, below_in, before_in, after_in, corners_before_in, corners_after_in,
    probe_in, intensity_in, forward_in,
    field, rim_above, rim_below, side_before, side_after, kept, given,
    extended, total, wave, halfway, residual, returning, turned, window, probe_sum,
    probe, intensity, forward, adjoint, above, below, before, after, corners_before, corners_after,
    copied, slot_copied,
):
    slots = place[0] * 32 + place[1]
    count = counts[slots]

    def inward(s):
        return pltpu.make_async_copy(intensity_in.at[s], intensity.at[s], slot_copied.at[s])

    pairs = [(above_in, above), (below_in, below), (before_in, before), (after_in, after)]
    pairs += [(corners_before_in, corners_before), (corners_after_in, corners_after)]
    pairs += [(probe_in, probe), (forward_in, forward)]
    for p in range(2):
        for j in range(4):
            pairs.append((center.at[p, :, pl.ds(j * 128, 128)], extended.at[p, j + 2, pl.ds(HALF, TH), :]))
    copies = [pltpu.make_async_copy(a, b, copied.at[k]) for k, (a, b) in enumerate(pairs)]
    for copy in copies:
        copy.start()
    lax.fori_loop(0, count, lambda s, carry: (inward(s).start(), carry)[1], 0)
    total[...] = jnp.zeros_like(total)
    probe_sum[...] = jnp.zeros_like(probe_sum)
    for copy in copies[:6]:
        copy.wait()
    for p in range(2):
        for j in range(EW // 128):
            if 2 <= j < 6:
                cols = pl.ds((j - 2) * 128, 128)
                over, under, low = above, below, 0
            else:
                cols = pl.ds(j % 2 * 128, 128)
                middle, over = (before, corners_before) if j < 2 else (after, corners_after)
                under, low = over, HALF
                extended[p, j, pl.ds(HALF, TH), :] = middle[p, :, cols].astype(F32)
            extended[p, j, pl.ds(0, HALF), :] = over[p, pl.ds(0, HALF), cols].astype(F32)
            extended[p, j, pl.ds(HALF + TH, HALF), :] = under[p, pl.ds(low, HALF), cols].astype(F32)
    for copy in copies[6:]:
        copy.wait()
    for k in range(2):
        for j in range(6):
            here = (pl.ds(k * PS, PS), pl.ds(j * 128, 128))
            adjoint[here] = forward[here] if k == j % 2 else -forward[here]

    def place_of(s):
        top = positions[(slots * PMAX + s) * 2]
        return (top,) + lane_parts(positions[(slots * PMAX + s) * 2 + 1] + 64)

    def leave(s, k):
        top, block, shift = place_of(s)
        lanes = lax.broadcasted_iota(jnp.int32, (PART, 128), 1)
        for at in range(k * 128, (k + 1) * 128, PART):
            rows = pl.ds(at, PART)
            cells = []
            for p in range(2):
                found = [extended[p, block + j, pl.ds(top + at, PART), :] for j in range(4)]
                cells.append(jnp.concatenate(rolled_in(found, shift, lanes), axis=1))
                window[s % 2, p, rows, :] = cells[p]
            pr, pi = probe[0, rows, :], probe[1, rows, :]
            wave[pl.ds(k * 128 + at, PART), :] = (pr * cells[0] - pi * cells[1]).astype(BF16)
            wave[pl.ds(k * 128 + at + 128, PART), :] = (pr * cells[1] + pi * cells[0]).astype(BF16)

    for k in range(3):
        leave(0, k)

    def slot(s, carry):
        top, block, shift = place_of(s)
        half = jnp.dot(adjoint[...], wave[...], preferred_element_type=F32).astype(BF16)
        halfway[:, pl.ds(0, PS)] = half[:PS]
        halfway[:, pl.ds(PS, PS)] = half[PS:]
        inward(s).wait()
        for j in range(3):
            cols = pl.ds(j * 128, 128)
            far = jnp.dot(halfway[...], forward[:, pl.ds(j * 256, 256)], preferred_element_type=F32)
            far_r, far_i = far[:, :128], far[:, 128:]
            misfit = far_r * far_r + far_i * far_i - intensity[s, :, cols].astype(F32)
            real, imaginary = (misfit * far_r).astype(BF16), (misfit * far_i).astype(BF16)
            for k in range(3):
                residual[pl.ds(k * 256, 128), cols] = real[k * 128 : (k + 1) * 128]
                residual[pl.ds(k * 256 + 128, 128), cols] = imaginary[k * 128 : (k + 1) * 128]
            leave(jnp.minimum(s + 1, count - 1), j)
        back = jnp.dot(forward[...], residual[...], preferred_element_type=F32).astype(BF16)
        returning[:, pl.ds(0, PS)] = back[:PS]
        returning[:, pl.ds(PS, PS)] = back[PS:]
        lanes = lax.broadcasted_iota(jnp.int32, (PART, 128), 1)
        for j in range(3):
            cols = pl.ds(j * 128, 128)
            gradient = jnp.dot(returning[...], adjoint[:, pl.ds(j * 256, 256)], preferred_element_type=F32)
            for k in range(PS // PART):
                rows = pl.ds(k * PART, PART)
                gr, gi = gradient[k * PART : (k + 1) * PART, :128], gradient[k * PART : (k + 1) * PART, 128:]
                pr, pi = probe[0, rows, cols], probe[1, rows, cols]
                wr, wi = window[s % 2, 0, rows, cols], window[s % 2, 1, rows, cols]
                for p, term in ((0, pr * gr + pi * gi), (1, pr * gi - pi * gr)):
                    term = pltpu.roll(term, shift, axis=1)
                    past = turned[p, rows, :] if j else jnp.zeros_like(term)
                    total[p, block + j, pl.ds(top + k * PART, PART), :] += jnp.where(lanes >= shift, term, past)
                    if j < 2:
                        turned[p, rows, :] = term
                    else:
                        total[p, block + 3, pl.ds(top + k * PART, PART), :] += jnp.where(lanes < shift, term, 0.0)
                probe_sum[0, rows, cols] += wr * gr + wi * gi
                probe_sum[1, rows, cols] += wr * gi - wi * gr
                probe_sum[2, rows, cols] += wr * wr + wi * wi
        return carry

    lax.fori_loop(0, count, slot, 0)
    pairs = []
    for p in range(2):
        for j in range(4):
            cols = pl.ds(j * 128, 128)
            pairs.append((total.at[p, j + 2, pl.ds(HALF, TH), :], field.at[p, :, cols]))
    copies = [pltpu.make_async_copy(a, b, copied.at[k]) for k, (a, b) in enumerate(pairs)]
    for copy in copies:
        copy.start()
    lanes = lax.broadcasted_iota(jnp.int32, (HALF, 128), 1)
    for p in range(2):
        for rim, rows in ((rim_above, pl.ds(0, HALF)), (rim_below, pl.ds(HALF + TH, HALF))):
            rim[p, :, pl.ds(0, 128)] = jnp.where(lanes < 64, total[p, 7, rows, :], total[p, 0, rows, :]).astype(BF16)
            for j in range(1, 7):
                rim[p, :, pl.ds(j * 128, 128)] = total[p, j, rows, :].astype(BF16)
        for j in range(2):
            cols = pl.ds(j * 128, 128)
            side_before[p, :, cols] = total[p, j, pl.ds(HALF, TH), :].astype(BF16)
            side_after[p, :, cols] = total[p, j + 6, pl.ds(HALF, TH), :].astype(BF16)
    for core in range(2):

        @pl.when(place[1] % 2 == core)
        def _():
            for ref, half, kind in ((kept, core, BF16), (given, 1 - core, BF16)):
                for at in range(BLOCKS):
                    if at < USED:
                        found = half * USED + at
                        p, k, j = found // 72, found // 3 % 24, found % 3
                        ref[at] = probe_sum[p, pl.ds(k * 16, 16), pl.ds(j * 128, 128)].astype(kind)
                    else:
                        ref[at] = jnp.zeros((16, 128), kind)

    for copy in copies:
        copy.wait()


def total_kernel(pieces, out):
    total = pieces[0].astype(F32)
    for k in range(1, pieces.shape[0]):
        total = total + pieces[k].astype(F32)
    for k in range(out.shape[0]):
        out[k] = total.astype(BF16)


def sides_kernel(from_above, from_below, side_before, side_after, earlier, before, after):
    del earlier
    lanes = lax.broadcasted_iota(jnp.int32, (HALF, 128), 1)
    first, second, middle = pl.ds(0, 128), pl.ds(128, 128), pl.ds(HALF, TH - 2 * HALF)
    for p in range(2):
        before[p, middle, :] = side_before[p, middle, :]
        after[p, middle, :] = side_after[p, middle, :]
        for source, rows in ((from_above, pl.ds(0, HALF)), (from_below, pl.ds(TH - HALF, HALF))):
            shared = source[p, :, first].astype(F32)
            outer = jnp.where(lanes >= 64, shared, 0.0)
            before[p, rows, first] = (side_before[p, rows, first].astype(F32) + outer).astype(BF16)
            inner = source[p, :, second].astype(F32)
            before[p, rows, second] = (side_before[p, rows, second].astype(F32) + inner).astype(BF16)
            inner = source[p, :, pl.ds(768, 128)].astype(F32)
            after[p, rows, first] = (side_after[p, rows, first].astype(F32) + inner).astype(BF16)
            outer = jnp.where(lanes < 64, shared, 0.0)
            after[p, rows, second] = (side_after[p, rows, second].astype(F32) + outer).astype(BF16)


def object_kernel(center, field, from_before, from_after, from_above, from_below, weight, out):
    for k in range(TH // 64):
        rows = pl.ds(k * 64, 64)
        center_cols = pl.ds(256, TW)
        for p in range(2):
            cells = field[p, rows, :]
            sides = [from_before[p, rows, :], from_after[p, rows, :]]
            cells = cells + jnp.concatenate(sides, axis=1).astype(F32)
            if k * 64 < HALF:
                cells = cells + from_above[p, rows, center_cols].astype(F32)
            if k * 64 >= TH - HALF:
                cells = cells + from_below[p, pl.ds(k * 64 - TH + HALF, 64), center_cols].astype(F32)
            out[p, rows, :] = center[p, rows, :] - cells * weight[rows, :]


def probe_kernel(place, half, other, probe, out, sums, planes):
    core = place[1] % 2
    sums[core] = half[...]
    sums[1 - core] = other[...]
    for found in range(2 * USED):
        p, k, j = found // 72, found // 3 % 24, found % 3
        planes[p, pl.ds(k * 16, 16), pl.ds(j * 128, 128)] = sums[found // USED, found % USED].astype(F32)
    floor = PROBE_REG * jnp.max(planes[2])
    square = jnp.zeros((STEP, PS), F32)
    for k in range(PS // STEP):
        rows = pl.ds(k * STEP, STEP)
        weight = 1.0 / (planes[2, rows, :] + floor)
        for p in range(2):
            direction = planes[p, rows, :] * weight
            planes[p, rows, :] = direction
            square = square + direction * direction
    spread = jnp.sqrt(jnp.sum(square) / (PS * PS) + EPSILON)
    for p in range(2):
        out[p] = probe[p] - PROBE_RATE * planes[p] / spread


SMEM = pl.BlockSpec(memory_space=pltpu.SMEM)
VMEM = pl.BlockSpec(memory_space=pltpu.VMEM)
ANY = pl.BlockSpec(memory_space=pl.ANY)


def params(mib):
    return pltpu.CompilerParams(vmem_limit_bytes=mib << 20)


def shifted(value, axis, step):
    size = lax.axis_size(axis)
    low, high = max(0, -step), min(size, size - step)
    return lax.ppermute(value, axis, [(k, k + step) for k in range(low, high)])


def slots_call(*arrays):
    like = jax.ShapeDtypeStruct
    forward = dft_blocks()
    return pl.pallas_call(
        main_kernel,
        out_shape=(
            like((2, TH, TW), F32),
            like((2, HALF, 896), BF16),
            like((2, HALF, 896), BF16),
            like((2, TH, 256), BF16),
            like((2, TH, 256), BF16),
            like((BLOCKS, 16, 128), BF16),
            like((BLOCKS, 16, 128), BF16),
        ),
        in_specs=[SMEM] * 3 + [ANY] * 10,
        out_specs=(ANY,) + (VMEM,) * 6,
        scratch_shapes=[
            pltpu.VMEM((2, EW // 128, EH, 128), F32),
            pltpu.VMEM((2, EW // 128, EH, 128), F32),
            pltpu.VMEM((2 * PS, PS), BF16),
            pltpu.VMEM((PS, 2 * PS), BF16),
            pltpu.VMEM((2 * PS, PS), BF16),
            pltpu.VMEM((PS, 2 * PS), BF16),
            pltpu.VMEM((2, PS, 128), F32),
            pltpu.VMEM((2, 2, PS, PS), F32),
            pltpu.VMEM((3, PS, PS), F32),
            pltpu.VMEM((2, PS, PS), F32),
            pltpu.VMEM((PMAX, PS, PS), BF16),
            pltpu.VMEM((2 * PS, 2 * PS), BF16),
            pltpu.VMEM((2 * PS, 2 * PS), BF16),
            pltpu.VMEM((2, HALF, TW), BF16),
            pltpu.VMEM((2, HALF, TW), BF16),
            pltpu.VMEM((2, TH, 256), BF16),
            pltpu.VMEM((2, TH, 256), BF16),
            pltpu.VMEM((2, PS, 256), BF16),
            pltpu.VMEM((2, PS, 256), BF16),
            pltpu.SemaphoreType.DMA((16,)),
            pltpu.SemaphoreType.DMA((PMAX,)),
        ],
        compiler_params=params(60),
        name="slots",
    )(*arrays, jnp.asarray(forward))


def on_device(object_field, probe_field, intensities, positions, tile_counts):
    place = jnp.stack([lax.axis_index("row"), lax.axis_index("col")]).astype(jnp.int32)
    where = positions.reshape(-1)
    counts = tile_counts.reshape(-1)
    above = shifted(object_field[:, TH - HALF :, :].astype(BF16), "row", 1)
    below = shifted(object_field[:, :HALF, :].astype(BF16), "row", -1)
    before = shifted(object_field[:, :, TW - 256 :].astype(BF16), "col", 1)
    after = shifted(object_field[:, :, :256].astype(BF16), "col", -1)
    weight = pl.pallas_call(
        illumination_kernel,
        out_shape=jax.ShapeDtypeStruct((TH, TW), F32),
        in_specs=[SMEM, SMEM, SMEM, VMEM],
        out_specs=VMEM,
        scratch_shapes=[pltpu.VMEM((CANVAS // 128, CANVAS, 128), F32), pltpu.VMEM((3, PS, 128), F32)],
        compiler_params=params(60),
        cost_estimate=pl.CostEstimate(flops=20_000_000, bytes_accessed=20_000_000, transcendentals=0),
        name="illumination",
    )(place, where, counts, probe_field)
    above, below, weight = lax.optimization_barrier((above, below, weight))
    corners = jnp.concatenate([above, below], axis=1)
    corners_before = shifted(corners[:, :, TW - 256 :], "col", 1)
    corners_after = shifted(corners[:, :, :256], "col", -1)
    like = jax.ShapeDtypeStruct
    field, rim_above, rim_below, side_before, side_after, kept, given = slots_call(
        place, where, counts, object_field, above, below, before, after, corners_before, corners_after,
        probe_field, intensities.reshape(PMAX, PS, PS),
    )
    core = place[1] % 2
    cols, rows = lax.axis_size("col"), lax.axis_size("row")
    device = np.arange(rows * cols).reshape(2, 4, 4, 4, 2)
    plane = device.transpose(0, 2, 4, 1, 3).reshape(-1, 16).tolist()
    line = device.transpose(1, 3, 4, 0, 2).reshape(-1, 8).tolist()
    partner = [(k, k ^ 1) for k in range(cols)]

    def exchanged(pieces, groups):
        return lax.all_to_all(pieces, ("row", "col"), 0, 0, axis_index_groups=groups)

    def total_of(pieces, times):
        return pl.pallas_call(
            total_kernel,
            out_shape=like((times,) + pieces.shape[1:], BF16),
            in_specs=[VMEM],
            out_specs=VMEM,
            cost_estimate=pl.CostEstimate(flops=3_000_000_000, bytes_accessed=0, transcendentals=0),
            name="total",
        )(pieces)

    arrived = lax.ppermute(given, "col", partner)
    mine = (kept.astype(F32) + arrived.astype(F32)).astype(BF16)
    mine, rim_above, rim_below = lax.optimization_barrier((mine, rim_above, rim_below))
    from_below = shifted(rim_above, "row", -1)
    from_above = shifted(rim_below, "row", 1)
    parts = exchanged(mine.reshape(16, -1, 16, 128), plane)
    sums = total_of(parts, 8)
    parts = exchanged(sums, line)
    side_before, side_after = pl.pallas_call(
        sides_kernel,
        out_shape=(like((2, TH, 256), BF16),) * 2,
        in_specs=[VMEM] * 4 + [ANY],
        out_specs=(VMEM,) * 2,
        compiler_params=params(60),
        cost_estimate=pl.CostEstimate(flops=0, bytes_accessed=0, transcendentals=0),
        name="sides",
    )(from_above, from_below, side_before, side_after, sums)
    from_before = shifted(side_after, "col", 1)
    from_after = shifted(side_before, "col", -1)
    half = exchanged(total_of(parts, 16), plane).reshape(BLOCKS, 16, 128)
    new_object = pl.pallas_call(
        object_kernel,
        out_shape=like((2, TH, TW), F32),
        in_specs=[VMEM] * 7,
        out_specs=VMEM,
        compiler_params=params(60),
        cost_estimate=pl.CostEstimate(flops=40_000_000_000, bytes_accessed=12_000_000, transcendentals=0),
        name="new_object",
    )(object_field, field, from_before, from_after, from_above, from_below, weight)
    half, new_object = lax.optimization_barrier((half, new_object))
    other = lax.ppermute(half, "col", partner)
    new_probe = pl.pallas_call(
        probe_kernel,
        out_shape=like((2, PS, PS), F32),
        in_specs=[SMEM, VMEM, VMEM, VMEM],
        out_specs=VMEM,
        scratch_shapes=[pltpu.VMEM((2, BLOCKS, 16, 128), BF16), pltpu.VMEM((3, PS, PS), F32)],
        compiler_params=params(60),
        name="new_probe",
    )(place, half, other, probe_field)
    return (new_object, new_probe)


def solution(mesh):
    placed = (P(None, "row", "col"), P(), P("row", "col", None, None, None), P(), P())
    return jax.shard_map(
        on_device,
        mesh=mesh,
        in_specs=placed,
        out_specs=(P(None, "row", "col"), P()),
        check_vma=False,
    )
```

```python
import functools

import jax
import jax.numpy as jnp
import ml_dtypes
import numpy as np
from jax import lax
from jax.experimental import pallas as pl
from jax.experimental.pallas import tpu as pltpu
from jax.sharding import PartitionSpec as P

OBJECT_REG = 0.1
PROBE_REG = 0.1
PROBE_RATE = 0.5
EPSILON = 1e-06

PS = 384
HALF = 192
TH = 512
TW = 512
PMAX = 6
EH = TH + PS
EW = TW + 512
CANVAS = 1280
USED = 108
BLOCKS = 112
STEP = 128
BAND = 96
PART = 64
EDGE = 4
F32 = jnp.float32
BF16 = jnp.bfloat16


def dft_blocks():
    index = np.arange(PS)
    product = (index[:, None] * index[None, :]) % PS
    angles = product.astype(np.float32) * np.float32(2.0 * np.pi / PS)
    norm = np.float32(1.0) / np.sqrt(np.float32(PS))
    cos = (np.cos(angles) * norm).astype(ml_dtypes.bfloat16)
    sin = (-np.sin(angles) * norm).astype(ml_dtypes.bfloat16)
    forward = np.block([[cos, sin], [-sin, cos]])
    order = np.arange(2 * PS).reshape(2, 3, 128).transpose(1, 0, 2).reshape(-1)
    return forward[:, order]


def lane_parts(column):
    block = column // 128
    return block, column - block * 128


def center_of(positions, row, col, slot):
    at = (row * PMAX + slot) * 2
    return positions[at, col], positions[at + 1, col]


def rolled_out(blocks, shift, lanes):
    turned = [pltpu.roll(b, shift, axis=1) for b in blocks]
    keep = lanes >= shift
    zero = jnp.zeros_like(turned[0])
    return [
        jnp.where(keep, turned[0], zero),
        jnp.where(keep, turned[1], turned[0]),
        jnp.where(keep, turned[2], turned[1]),
        jnp.where(keep, zero, turned[2]),
    ]


def rolled_in(blocks, shift, lanes):
    turned = [pltpu.roll(b, (128 - shift) % 128, axis=1) for b in blocks]
    keep = lanes < 128 - shift
    return [jnp.where(keep, turned[k], turned[k + 1]) for k in range(3)]


def illumination_kernel(positions, counts, probe, earlier, out, canvas, power):
    del earlier
    my_row, my_col = lax.axis_index("row"), lax.axis_index("col")
    for j in range(3):
        cols = pl.ds(j * 128, 128)
        power[j] = probe[0, :, cols] * probe[0, :, cols] + probe[1, :, cols] * probe[1, :, cols]
    first, last = PS // 128, (PS + TW) // 128
    for j in range(first, last):
        canvas[j, pl.ds(PS, TH), :] = jnp.zeros((TH, 128), F32)
    lanes = lax.broadcasted_iota(jnp.int32, (BAND, 128), 1)
    grid_r, grid_c = 8, 32

    def tile(k, carry):
        down, across = k // 3 - 1, k % 3 - 1
        row, col = my_row + down, my_col + across
        inside = (row >= 0) & (row < grid_r) & (col >= 0) & (col < grid_c)
        row, col = jnp.where(inside, row, 0), jnp.where(inside, col, 0)
        count = jnp.where(inside, counts[row, col], 0)

        def slot(s, inner):
            top, left = center_of(positions, row, col, s)
            top = top + down * TH - HALF + PS
            left = left + across * TW - HALF + PS
            meets = (top > 0) & (top < PS + TH) & (left > 0) & (left < PS + TW)

            @pl.when(meets)
            def _():
                block, shift = lane_parts(left)
                low = jnp.maximum(PS - top, 0) // BAND
                high = (jnp.minimum(PS + TH - top, PS) + BAND - 1) // BAND

                def band(c, deep):
                    rows = pl.ds(pl.multiple_of(c * BAND, BAND), BAND)
                    parts = rolled_out([power[j, rows, :] for j in range(3)], shift, lanes)
                    for j in range(4):
                        canvas[block + j, pl.ds(top + c * BAND, BAND), :] += parts[j]
                    return deep

                lax.fori_loop(low, high, band, 0)

            return inner

        return lax.fori_loop(0, count, slot, carry)

    lax.fori_loop(0, 9, tile, 0)
    floor = OBJECT_REG * jnp.max(power[...])
    for j in range(TW // 128):
        out[:, pl.ds(j * 128, 128)] = 1.0 / (canvas[first + j, pl.ds(PS, TH), :] + floor)


def main_kernel(
    positions, counts, center, across_in, above_in, below_in, before_in, after_in,
    corners_before_in, corners_after_in, probe_in, intensity_in, forward_in,
    field, rim_before, rim_after, rim_above, rim_below, kept, given,
    extended, total, wave, halfway, residual, returning, turned, window, probe_sum,
    probe, intensity, forward, adjoint, above, below, before, after, corners_before, corners_after,
    copied, slot_copied,
):
    my_row, my_col = lax.axis_index("row"), lax.axis_index("col")
    count = counts[my_row, my_col]

    def inward(s):
        return pltpu.make_async_copy(intensity_in.at[s], intensity.at[s], slot_copied.at[s])

    pairs = [(before_in, before), (after_in, after)]
    pairs += [(corners_before_in, corners_before), (corners_after_in, corners_after)]
    pairs += [(probe_in, probe), (forward_in, forward)]
    for p in range(2):
        for j in range(4):
            pairs.append((center.at[p, :, pl.ds(j * 128, 128)], extended.at[p, j + 2, pl.ds(HALF, TH), :]))
    copies = [pltpu.make_async_copy(a, b, copied.at[k]) for k, (a, b) in enumerate(pairs)]
    rims = ((above_in, above, my_row == EDGE), (below_in, below, my_row == EDGE - 1))
    for k, (rim_in, rim, from_across) in enumerate(rims):
        near = pltpu.make_async_copy(rim_in, rim, copied.at[14 + k])
        pl.when(from_across)(pltpu.make_async_copy(across_in, rim, copied.at[14 + k]).start)
        pl.when(jnp.logical_not(from_across))(near.start)
        copies.insert(0, near)
    for copy in copies[2:]:
        copy.start()
    lax.fori_loop(0, count, lambda s, carry: (inward(s).start(), carry)[1], 0)
    total[...] = jnp.zeros_like(total)
    probe_sum[...] = jnp.zeros_like(probe_sum)
    for copy in copies[:6]:
        copy.wait()
    for p in range(2):
        for j in range(EW // 128):
            if 2 <= j < 6:
                cols = pl.ds((j - 2) * 128, 128)
                over, under, low = above, below, 0
            else:
                cols = pl.ds(j % 2 * 128, 128)
                middle, over = (before, corners_before) if j < 2 else (after, corners_after)
                under, low = over, HALF
                extended[p, j, pl.ds(HALF, TH), :] = middle[p, :, cols].astype(F32)
            extended[p, j, pl.ds(0, HALF), :] = over[p, pl.ds(0, HALF), cols].astype(F32)
            extended[p, j, pl.ds(HALF + TH, HALF), :] = under[p, pl.ds(low, HALF), cols].astype(F32)
    for copy in copies[6:]:
        copy.wait()
    for k in range(2):
        for j in range(6):
            here = (pl.ds(k * PS, PS), pl.ds(j * 128, 128))
            adjoint[here] = forward[here] if k == j % 2 else -forward[here]

    def place_of(s):
        top, left = center_of(positions, my_row, my_col, s)
        return (top,) + lane_parts(left + 64)

    def leave(s, k):
        top, block, shift = place_of(s)
        lanes = lax.broadcasted_iota(jnp.int32, (PART, 128), 1)
        for at in range(k * 128, (k + 1) * 128, PART):
            rows = pl.ds(at, PART)
            cells = []
            for p in range(2):
                found = [extended[p, block + j, pl.ds(top + at, PART), :] for j in range(4)]
                cells.append(jnp.concatenate(rolled_in(found, shift, lanes), axis=1))
                window[s % 2, p, rows, :] = cells[p]
            pr, pi = probe[0, rows, :], probe[1, rows, :]
            wave[pl.ds(k * 128 + at, PART), :] = (pr * cells[0] - pi * cells[1]).astype(BF16)
            wave[pl.ds(k * 128 + at + 128, PART), :] = (pr * cells[1] + pi * cells[0]).astype(BF16)

    for k in range(3):
        leave(0, k)

    def slot(s, carry):
        top, block, shift = place_of(s)
        half = jnp.dot(adjoint[...], wave[...], preferred_element_type=F32).astype(BF16)
        halfway[:, pl.ds(0, PS)] = half[:PS]
        halfway[:, pl.ds(PS, PS)] = half[PS:]
        inward(s).wait()
        for j in range(3):
            cols = pl.ds(j * 128, 128)
            far = jnp.dot(halfway[...], forward[:, pl.ds(j * 256, 256)], preferred_element_type=F32)
            far_r, far_i = far[:, :128], far[:, 128:]
            misfit = far_r * far_r + far_i * far_i - intensity[s, :, cols].astype(F32)
            real, imaginary = (misfit * far_r).astype(BF16), (misfit * far_i).astype(BF16)
            for k in range(3):
                residual[pl.ds(k * 256, 128), cols] = real[k * 128 : (k + 1) * 128]
                residual[pl.ds(k * 256 + 128, 128), cols] = imaginary[k * 128 : (k + 1) * 128]
            leave(jnp.minimum(s + 1, count - 1), j)
        back = jnp.dot(forward[...], residual[...], preferred_element_type=F32).astype(BF16)
        returning[:, pl.ds(0, PS)] = back[:PS]
        returning[:, pl.ds(PS, PS)] = back[PS:]
        lanes = lax.broadcasted_iota(jnp.int32, (PART, 128), 1)
        for j in range(3):
            cols = pl.ds(j * 128, 128)
            gradient = jnp.dot(returning[...], adjoint[:, pl.ds(j * 256, 256)], preferred_element_type=F32)
            for k in range(PS // PART):
                rows = pl.ds(k * PART, PART)
                gr, gi = gradient[k * PART : (k + 1) * PART, :128], gradient[k * PART : (k + 1) * PART, 128:]
                pr, pi = probe[0, rows, cols], probe[1, rows, cols]
                wr, wi = window[s % 2, 0, rows, cols], window[s % 2, 1, rows, cols]
                for p, term in ((0, pr * gr + pi * gi), (1, pr * gi - pi * gr)):
                    term = pltpu.roll(term, shift, axis=1)
                    past = turned[p, rows, :] if j else jnp.zeros_like(term)
                    total[p, block + j, pl.ds(top + k * PART, PART), :] += jnp.where(lanes >= shift, term, past)
                    if j < 2:
                        turned[p, rows, :] = term
                    else:
                        total[p, block + 3, pl.ds(top + k * PART, PART), :] += jnp.where(lanes < shift, term, 0.0)
                probe_sum[0, rows, cols] += wr * gr + wi * gi
                probe_sum[1, rows, cols] += wr * gi - wi * gr
                probe_sum[2, rows, cols] += wr * wr + wi * wi
        return carry

    lax.fori_loop(0, count, slot, 0)
    pairs = []
    for p in range(2):
        for j in range(4):
            cols = pl.ds(j * 128, 128)
            pairs.append((total.at[p, j + 2, pl.ds(HALF, TH), :], field.at[p, :, cols]))
    copies = [pltpu.make_async_copy(a, b, copied.at[k]) for k, (a, b) in enumerate(pairs)]
    for copy in copies:
        copy.start()
    for p in range(2):
        for j in range(EW // 128):
            cols = pl.ds(j % 2 * 128, 128)
            if 2 <= j < 6:
                cols = pl.ds((j - 2) * 128, 128)
                rim_above[p, :, cols] = total[p, j, pl.ds(0, HALF), :].astype(BF16)
                rim_below[p, :, cols] = total[p, j, pl.ds(HALF + TH, HALF), :].astype(BF16)
            else:
                rim = rim_before if j < 2 else rim_after
                rim[p, :, cols] = total[p, j].astype(BF16)
    for core in range(2):

        @pl.when(my_col % 2 == core)
        def _():
            for ref, half, kind in ((kept, core, BF16), (given, 1 - core, BF16)):
                for at in range(BLOCKS):
                    if at < USED:
                        found = half * USED + at
                        p, k, j = found // 72, found // 3 % 24, found % 3
                        ref[at] = probe_sum[p, pl.ds(k * 16, 16), pl.ds(j * 128, 128)].astype(kind)
                    else:
                        ref[at] = jnp.zeros((16, 128), kind)

    for copy in copies:
        copy.wait()


def total_kernel(pieces, out):
    total = pieces[0].astype(F32)
    for k in range(1, pieces.shape[0]):
        total = total + pieces[k].astype(F32)
    for k in range(out.shape[0]):
        out[k] = total.astype(BF16)


def object_kernel(center, field, from_before, from_after, across, from_above, from_below, weight, out):
    my_row = lax.axis_index("row")
    for k in range(TH // 64):
        rows = pl.ds(k * 64, 64)
        outer = pl.ds(HALF + k * 64, 64)
        for p in range(2):
            cells = field[p, rows, :]
            sides = [from_before[p, outer, :], from_after[p, outer, :]]
            cells = cells + jnp.concatenate(sides, axis=1).astype(F32)
            if k * 64 < HALF:
                near, far = from_above[p, rows, :].astype(F32), across[p, rows, :].astype(F32)
                cells = cells + jnp.where(my_row == EDGE, far, near)
            if k * 64 >= TH - HALF:
                there = pl.ds(k * 64 - TH + HALF, 64)
                near, far = from_below[p, there, :].astype(F32), across[p, there, :].astype(F32)
                cells = cells + jnp.where(my_row == EDGE - 1, far, near)
            out[p, rows, :] = center[p, rows, :] - cells * weight[rows, :]


def probe_kernel(half, other, probe, out, sums, planes):
    core = lax.axis_index("col") % 2
    sums[core] = half[...]
    sums[1 - core] = other[...]
    for found in range(2 * USED):
        p, k, j = found // 72, found // 3 % 24, found % 3
        planes[p, pl.ds(k * 16, 16), pl.ds(j * 128, 128)] = sums[found // USED, found % USED].astype(F32)
    floor = PROBE_REG * jnp.max(planes[2])
    square = jnp.zeros((STEP, PS), F32)
    for k in range(PS // STEP):
        rows = pl.ds(k * STEP, STEP)
        weight = 1.0 / (planes[2, rows, :] + floor)
        for p in range(2):
            direction = planes[p, rows, :] * weight
            planes[p, rows, :] = direction
            square = square + direction * direction
    spread = jnp.sqrt(jnp.sum(square) / (PS * PS) + EPSILON)
    for p in range(2):
        out[p] = probe[p] - PROBE_RATE * planes[p] / spread


SMEM = pl.BlockSpec(memory_space=pltpu.SMEM)
VMEM = pl.BlockSpec(memory_space=pltpu.VMEM)
ANY = pl.BlockSpec(memory_space=pl.ANY)


def params(mib):
    return pltpu.CompilerParams(vmem_limit_bytes=mib << 20)


def shifted(value, axis, step):
    size = lax.axis_size(axis)
    low, high = max(0, -step), min(size, size - step)
    return lax.ppermute(value, axis, [(k, k + step) for k in range(low, high)])


def slots_call(*arrays):
    like = jax.ShapeDtypeStruct
    forward = dft_blocks()
    return pl.pallas_call(
        main_kernel,
        out_shape=(
            like((2, TH, TW), F32),
            like((2, EH, 256), BF16),
            like((2, EH, 256), BF16),
            like((2, HALF, TW), BF16),
            like((2, HALF, TW), BF16),
            like((BLOCKS, 16, 128), BF16),
            like((BLOCKS, 16, 128), BF16),
        ),
        in_specs=[SMEM] * 2 + [ANY] * 11,
        out_specs=(ANY,) + (VMEM,) * 6,
        scratch_shapes=[
            pltpu.VMEM((2, EW // 128, EH, 128), F32),
            pltpu.VMEM((2, EW // 128, EH, 128), F32),
            pltpu.VMEM((2 * PS, PS), BF16),
            pltpu.VMEM((PS, 2 * PS), BF16),
            pltpu.VMEM((2 * PS, PS), BF16),
            pltpu.VMEM((PS, 2 * PS), BF16),
            pltpu.VMEM((2, PS, 128), F32),
            pltpu.VMEM((2, 2, PS, PS), F32),
            pltpu.VMEM((3, PS, PS), F32),
            pltpu.VMEM((2, PS, PS), F32),
            pltpu.VMEM((PMAX, PS, PS), BF16),
            pltpu.VMEM((2 * PS, 2 * PS), BF16),
            pltpu.VMEM((2 * PS, 2 * PS), BF16),
            pltpu.VMEM((2, HALF, TW), BF16),
            pltpu.VMEM((2, HALF, TW), BF16),
            pltpu.VMEM((2, TH, 256), BF16),
            pltpu.VMEM((2, TH, 256), BF16),
            pltpu.VMEM((2, PS, 256), BF16),
            pltpu.VMEM((2, PS, 256), BF16),
            pltpu.SemaphoreType.DMA((16,)),
            pltpu.SemaphoreType.DMA((PMAX,)),
        ],
        compiler_params=params(60),
        name="slots",
    )(*arrays, jnp.asarray(forward))


def across_edge(value):
    return lax.ppermute(value, "row", [(EDGE - 1, EDGE), (EDGE, EDGE - 1)])


def within_halves(value, step):
    rows = [k for k in range(lax.axis_size("row")) if k // EDGE == (k + step) // EDGE]
    return lax.ppermute(value, "row", [(k, k + step) for k in rows])


def on_device(object_field, probe_field, intensities, positions, tile_counts):
    my_row = lax.axis_index("row")
    where = positions.transpose(0, 2, 3, 1).reshape(-1, positions.shape[1])
    head, tail = object_field[:, :HALF, :].astype(BF16), object_field[:, TH - HALF :, :].astype(BF16)
    across = across_edge(jnp.where(my_row == EDGE, head, tail))
    above = within_halves(tail, 1)
    below = within_halves(head, -1)
    before = shifted(object_field[:, :, TW - 256 :].astype(BF16), "col", 1)
    after = shifted(object_field[:, :, :256].astype(BF16), "col", -1)
    corners = jnp.concatenate(
        [jnp.where(my_row == EDGE, across, above), jnp.where(my_row == EDGE - 1, across, below)], axis=1
    )
    corners_before = shifted(corners[:, :, TW - 256 :], "col", 1)
    corners_after = shifted(corners[:, :, :256], "col", -1)
    like = jax.ShapeDtypeStruct
    field, rim_before, rim_after, rim_above, rim_below, kept, given = slots_call(
        where, tile_counts, object_field, across, above, below, before, after,
        corners_before, corners_after, probe_field, intensities.reshape(PMAX, PS, PS),
    )
    cols, rows = lax.axis_size("col"), lax.axis_size("row")
    device = np.arange(rows * cols).reshape(2, 4, 4, 4, 2)
    plane = device.transpose(0, 2, 4, 1, 3).reshape(-1, 16).tolist()
    line = device.transpose(1, 3, 4, 0, 2).reshape(-1, 8).tolist()
    partner = [(k, k ^ 1) for k in range(cols)]

    def exchanged(pieces, groups):
        return lax.all_to_all(pieces, ("row", "col"), 0, 0, axis_index_groups=groups)

    def total_of(pieces, times):
        return pl.pallas_call(
            total_kernel,
            out_shape=like((times,) + pieces.shape[1:], BF16),
            in_specs=[VMEM],
            out_specs=VMEM,
            cost_estimate=pl.CostEstimate(flops=3_000_000_000, bytes_accessed=0, transcendentals=0),
            name="total",
        )(pieces)

    arrived = lax.ppermute(given, "col", partner)
    mine = (kept.astype(F32) + arrived.astype(F32)).astype(BF16)
    mine, rim_before, rim_after = lax.optimization_barrier((mine, rim_before, rim_after))
    from_before = shifted(rim_after, "col", 1)
    from_after = shifted(rim_before, "col", -1)
    parts = exchanged(mine.reshape(16, -1, 16, 128), plane)
    sums = total_of(parts, 8)
    parts = exchanged(sums, line)
    sides = jnp.concatenate([from_before, from_after], axis=2).astype(F32)
    up = (rim_above.astype(F32) + sides[:, :HALF]).astype(BF16)
    down = (rim_below.astype(F32) + sides[:, HALF + TH :]).astype(BF16)
    across = across_edge(jnp.where(my_row == EDGE, up, down))
    from_below = within_halves(up, -1)
    from_above = within_halves(down, 1)
    sums = total_of(parts, 16)
    weight = pl.pallas_call(
        illumination_kernel,
        out_shape=like((TH, TW), F32),
        in_specs=[SMEM, SMEM, VMEM, ANY],
        out_specs=VMEM,
        scratch_shapes=[pltpu.VMEM((CANVAS // 128, CANVAS, 128), F32), pltpu.VMEM((3, PS, 128), F32)],
        compiler_params=params(60),
        cost_estimate=pl.CostEstimate(flops=20_000_000, bytes_accessed=20_000_000, transcendentals=0),
        name="illumination",
    )(where, tile_counts, probe_field, sums)
    half = exchanged(sums, plane).reshape(BLOCKS, 16, 128)
    new_object = pl.pallas_call(
        object_kernel,
        out_shape=like((2, TH, TW), F32),
        in_specs=[VMEM] * 8,
        out_specs=VMEM,
        compiler_params=params(60),
        cost_estimate=pl.CostEstimate(flops=40_000_000_000, bytes_accessed=12_000_000, transcendentals=0),
        name="new_object",
    )(object_field, field, from_before, from_after, across, from_above, from_below, weight)
    half, new_object = lax.optimization_barrier((half, new_object))
    other = lax.ppermute(half, "col", partner)
    new_probe = pl.pallas_call(
        probe_kernel,
        out_shape=like((2, PS, PS), F32),
        in_specs=[VMEM] * 3,
        out_specs=VMEM,
        scratch_shapes=[pltpu.VMEM((2, BLOCKS, 16, 128), BF16), pltpu.VMEM((3, PS, PS), F32)],
        compiler_params=params(60),
        name="new_probe",
    )(half, other, probe_field)
    return (new_object, new_probe)


def solution(mesh):
    placed = (P(None, "row", "col"), P(), P("row", "col", None, None, None), P(), P())
    return jax.shard_map(
        on_device,
        mesh=mesh,
        in_specs=placed,
        out_specs=(P(None, "row", "col"), P()),
        check_vma=False,
    )
```

```python
import functools

import jax
import jax.numpy as jnp
import ml_dtypes
import numpy as np
from jax import lax
from jax.experimental import pallas as pl
from jax.experimental.pallas import tpu as pltpu
from jax.sharding import PartitionSpec as P

OBJECT_REG = 0.1
PROBE_REG = 0.1
PROBE_RATE = 0.5
EPSILON = 1e-06

PS = 384
HALF = 192
TH = 512
TW = 512
PMAX = 6
EH = TH + PS
EW = TW + 512
CANVAS = 1280
USED = 108
BLOCKS = 112
STEP = 128
BAND = 96
PART = 64
EDGE = 4
F32 = jnp.float32
BF16 = jnp.bfloat16


def dft_blocks():
    index = np.arange(PS)
    product = (index[:, None] * index[None, :]) % PS
    angles = product.astype(np.float32) * np.float32(2.0 * np.pi / PS)
    norm = np.float32(1.0) / np.sqrt(np.float32(PS))
    cos = (np.cos(angles) * norm).astype(ml_dtypes.bfloat16)
    sin = (-np.sin(angles) * norm).astype(ml_dtypes.bfloat16)
    forward = np.block([[cos, sin], [-sin, cos]])
    order = np.arange(2 * PS).reshape(2, 3, 128).transpose(1, 0, 2).reshape(-1)
    return forward[:, order]


def lane_parts(column):
    block = column // 128
    return block, column - block * 128


def center_of(positions, row, col, slot):
    at = (row * PMAX + slot) * 2
    return positions[at, col], positions[at + 1, col]


def rolled_out(blocks, shift, lanes):
    turned = [pltpu.roll(b, shift, axis=1) for b in blocks]
    keep = lanes >= shift
    zero = jnp.zeros_like(turned[0])
    return [
        jnp.where(keep, turned[0], zero),
        jnp.where(keep, turned[1], turned[0]),
        jnp.where(keep, turned[2], turned[1]),
        jnp.where(keep, zero, turned[2]),
    ]


def rolled_in(blocks, shift, lanes):
    turned = [pltpu.roll(b, (128 - shift) % 128, axis=1) for b in blocks]
    keep = lanes < 128 - shift
    return [jnp.where(keep, turned[k], turned[k + 1]) for k in range(3)]


def illumination_kernel(positions, counts, probe, out, canvas, power):
    my_row, my_col = lax.axis_index("row"), lax.axis_index("col")
    for j in range(3):
        cols = pl.ds(j * 128, 128)
        power[j] = probe[0, :, cols] * probe[0, :, cols] + probe[1, :, cols] * probe[1, :, cols]
    first, last = PS // 128, (PS + TW) // 128
    for j in range(first, last):
        canvas[j, pl.ds(PS, TH), :] = jnp.zeros((TH, 128), F32)
    lanes = lax.broadcasted_iota(jnp.int32, (BAND, 128), 1)
    grid_r, grid_c = 8, 32

    def tile(k, carry):
        down, across = k // 3 - 1, k % 3 - 1
        row, col = my_row + down, my_col + across
        inside = (row >= 0) & (row < grid_r) & (col >= 0) & (col < grid_c)
        row, col = jnp.where(inside, row, 0), jnp.where(inside, col, 0)
        count = jnp.where(inside, counts[row, col], 0)

        def slot(s, inner):
            top, left = center_of(positions, row, col, s)
            top = top + down * TH - HALF + PS
            left = left + across * TW - HALF + PS
            meets = (top > 0) & (top < PS + TH) & (left > 0) & (left < PS + TW)

            @pl.when(meets)
            def _():
                block, shift = lane_parts(left)
                low = jnp.maximum(PS - top, 0) // BAND
                high = (jnp.minimum(PS + TH - top, PS) + BAND - 1) // BAND

                def band(c, deep):
                    rows = pl.ds(pl.multiple_of(c * BAND, BAND), BAND)
                    parts = rolled_out([power[j, rows, :] for j in range(3)], shift, lanes)
                    for j in range(4):
                        canvas[block + j, pl.ds(top + c * BAND, BAND), :] += parts[j]
                    return deep

                lax.fori_loop(low, high, band, 0)

            return inner

        return lax.fori_loop(0, count, slot, carry)

    lax.fori_loop(0, 9, tile, 0)
    floor = OBJECT_REG * jnp.max(power[...])
    for j in range(TW // 128):
        out[:, pl.ds(j * 128, 128)] = 1.0 / (canvas[first + j, pl.ds(PS, TH), :] + floor)


def main_kernel(
    positions, counts, center, across_in, above_in, below_in, before_in, after_in,
    corners_before_in, corners_after_in, probe_in, intensity_in, forward_in,
    field, rim_before, rim_after, rim_above, rim_below, kept, given,
    extended, total, wave, halfway, residual, returning, turned, window, probe_sum,
    probe, intensity, forward, adjoint, above, below, before, after, corners_before, corners_after,
    copied, slot_copied,
):
    my_row, my_col = lax.axis_index("row"), lax.axis_index("col")
    count = counts[my_row, my_col]

    def inward(s):
        return pltpu.make_async_copy(intensity_in.at[s], intensity.at[s], slot_copied.at[s])

    pairs = [(before_in, before), (after_in, after)]
    pairs += [(corners_before_in, corners_before), (corners_after_in, corners_after)]
    pairs += [(probe_in, probe), (forward_in, forward)]
    for p in range(2):
        for j in range(4):
            pairs.append((center.at[p, :, pl.ds(j * 128, 128)], extended.at[p, j + 2, pl.ds(HALF, TH), :]))
    copies = [pltpu.make_async_copy(a, b, copied.at[k]) for k, (a, b) in enumerate(pairs)]
    rims = ((above_in, above, my_row == EDGE), (below_in, below, my_row == EDGE - 1))
    for k, (rim_in, rim, from_across) in enumerate(rims):
        near = pltpu.make_async_copy(rim_in, rim, copied.at[14 + k])
        pl.when(from_across)(pltpu.make_async_copy(across_in, rim, copied.at[14 + k]).start)
        pl.when(jnp.logical_not(from_across))(near.start)
        copies.insert(0, near)
    for copy in copies[2:]:
        copy.start()
    lax.fori_loop(0, count, lambda s, carry: (inward(s).start(), carry)[1], 0)
    total[...] = jnp.zeros_like(total)
    probe_sum[...] = jnp.zeros_like(probe_sum)
    for copy in copies[:6]:
        copy.wait()
    for p in range(2):
        for j in range(EW // 128):
            if 2 <= j < 6:
                cols = pl.ds((j - 2) * 128, 128)
                over, under, low = above, below, 0
            else:
                cols = pl.ds(j % 2 * 128, 128)
                middle, over = (before, corners_before) if j < 2 else (after, corners_after)
                under, low = over, HALF
                extended[p, j, pl.ds(HALF, TH), :] = middle[p, :, cols].astype(F32)
            extended[p, j, pl.ds(0, HALF), :] = over[p, pl.ds(0, HALF), cols].astype(F32)
            extended[p, j, pl.ds(HALF + TH, HALF), :] = under[p, pl.ds(low, HALF), cols].astype(F32)
    for copy in copies[6:]:
        copy.wait()
    for k in range(2):
        for j in range(6):
            here = (pl.ds(k * PS, PS), pl.ds(j * 128, 128))
            adjoint[here] = forward[here] if k == j % 2 else -forward[here]

    def place_of(s):
        top, left = center_of(positions, my_row, my_col, s)
        return (top,) + lane_parts(left + 64)

    def leave(s, k):
        top, block, shift = place_of(s)
        lanes = lax.broadcasted_iota(jnp.int32, (PART, 128), 1)
        for at in range(k * 128, (k + 1) * 128, PART):
            rows = pl.ds(at, PART)
            cells = []
            for p in range(2):
                found = [extended[p, block + j, pl.ds(top + at, PART), :] for j in range(4)]
                cells.append(jnp.concatenate(rolled_in(found, shift, lanes), axis=1))
                window[s % 2, p, rows, :] = cells[p]
            pr, pi = probe[0, rows, :], probe[1, rows, :]
            wave[pl.ds(k * 128 + at, PART), :] = (pr * cells[0] - pi * cells[1]).astype(BF16)
            wave[pl.ds(k * 128 + at + 128, PART), :] = (pr * cells[1] + pi * cells[0]).astype(BF16)

    for k in range(3):
        leave(0, k)

    def slot(s, carry):
        top, block, shift = place_of(s)
        half = jnp.dot(adjoint[...], wave[...], preferred_element_type=F32).astype(BF16)
        halfway[:, pl.ds(0, PS)] = half[:PS]
        halfway[:, pl.ds(PS, PS)] = half[PS:]
        inward(s).wait()
        for j in range(3):
            cols = pl.ds(j * 128, 128)
            far = jnp.dot(halfway[...], forward[:, pl.ds(j * 256, 256)], preferred_element_type=F32)
            far_r, far_i = far[:, :128], far[:, 128:]
            misfit = far_r * far_r + far_i * far_i - intensity[s, :, cols].astype(F32)
            real, imaginary = (misfit * far_r).astype(BF16), (misfit * far_i).astype(BF16)
            for k in range(3):
                residual[pl.ds(k * 256, 128), cols] = real[k * 128 : (k + 1) * 128]
                residual[pl.ds(k * 256 + 128, 128), cols] = imaginary[k * 128 : (k + 1) * 128]
            leave(jnp.minimum(s + 1, count - 1), j)
        back = jnp.dot(forward[...], residual[...], preferred_element_type=F32).astype(BF16)
        returning[:, pl.ds(0, PS)] = back[:PS]
        returning[:, pl.ds(PS, PS)] = back[PS:]
        lanes = lax.broadcasted_iota(jnp.int32, (PART, 128), 1)
        for j in range(3):
            cols = pl.ds(j * 128, 128)
            gradient = jnp.dot(returning[...], adjoint[:, pl.ds(j * 256, 256)], preferred_element_type=F32)
            for k in range(PS // PART):
                rows = pl.ds(k * PART, PART)
                gr, gi = gradient[k * PART : (k + 1) * PART, :128], gradient[k * PART : (k + 1) * PART, 128:]
                pr, pi = probe[0, rows, cols], probe[1, rows, cols]
                wr, wi = window[s % 2, 0, rows, cols], window[s % 2, 1, rows, cols]
                for p, term in ((0, pr * gr + pi * gi), (1, pr * gi - pi * gr)):
                    term = pltpu.roll(term, shift, axis=1)
                    past = turned[p, rows, :] if j else jnp.zeros_like(term)
                    total[p, block + j, pl.ds(top + k * PART, PART), :] += jnp.where(lanes >= shift, term, past)
                    if j < 2:
                        turned[p, rows, :] = term
                    else:
                        total[p, block + 3, pl.ds(top + k * PART, PART), :] += jnp.where(lanes < shift, term, 0.0)
                probe_sum[0, rows, cols] += wr * gr + wi * gi
                probe_sum[1, rows, cols] += wr * gi - wi * gr
                probe_sum[2, rows, cols] += wr * wr + wi * wi
        return carry

    lax.fori_loop(0, count, slot, 0)
    pairs = []
    for p in range(2):
        for j in range(4):
            cols = pl.ds(j * 128, 128)
            pairs.append((total.at[p, j + 2, pl.ds(HALF, TH), :], field.at[p, :, cols]))
    copies = [pltpu.make_async_copy(a, b, copied.at[k]) for k, (a, b) in enumerate(pairs)]
    for copy in copies:
        copy.start()
    for p in range(2):
        for j in range(EW // 128):
            cols = pl.ds(j % 2 * 128, 128)
            if 2 <= j < 6:
                cols = pl.ds((j - 2) * 128, 128)
                rim_above[p, :, cols] = total[p, j, pl.ds(0, HALF), :].astype(BF16)
                rim_below[p, :, cols] = total[p, j, pl.ds(HALF + TH, HALF), :].astype(BF16)
            else:
                rim = rim_before if j < 2 else rim_after
                rim[p, :, cols] = total[p, j].astype(BF16)
    for core in range(2):

        @pl.when(my_col % 2 == core)
        def _():
            for ref, half, kind in ((kept, core, BF16), (given, 1 - core, BF16)):
                for at in range(BLOCKS):
                    if at < USED:
                        found = half * USED + at
                        p, k, j = found // 72, found // 3 % 24, found % 3
                        ref[at] = probe_sum[p, pl.ds(k * 16, 16), pl.ds(j * 128, 128)].astype(kind)
                    else:
                        ref[at] = jnp.zeros((16, 128), kind)

    for copy in copies:
        copy.wait()


def total_kernel(pieces, out):
    total = pieces[0].astype(F32)
    for k in range(1, pieces.shape[0]):
        total = total + pieces[k].astype(F32)
    for k in range(out.shape[0]):
        out[k] = total.astype(BF16)


def object_kernel(center, field, from_before, from_after, across, from_above, from_below, weight, out):
    my_row = lax.axis_index("row")
    for k in range(TH // 64):
        rows = pl.ds(k * 64, 64)
        outer = pl.ds(HALF + k * 64, 64)
        for p in range(2):
            cells = field[p, rows, :]
            sides = [from_before[p, outer, :], from_after[p, outer, :]]
            cells = cells + jnp.concatenate(sides, axis=1).astype(F32)
            if k * 64 < HALF:
                near, far = from_above[p, rows, :].astype(F32), across[p, rows, :].astype(F32)
                cells = cells + jnp.where(my_row == EDGE, far, near)
            if k * 64 >= TH - HALF:
                there = pl.ds(k * 64 - TH + HALF, 64)
                near, far = from_below[p, there, :].astype(F32), across[p, there, :].astype(F32)
                cells = cells + jnp.where(my_row == EDGE - 1, far, near)
            out[p, rows, :] = center[p, rows, :] - cells * weight[rows, :]


def probe_kernel(half, other, probe, out, sums, planes):
    core = lax.axis_index("col") % 2
    sums[core] = half[...]
    sums[1 - core] = other[...]
    for found in range(2 * USED):
        p, k, j = found // 72, found // 3 % 24, found % 3
        planes[p, pl.ds(k * 16, 16), pl.ds(j * 128, 128)] = sums[found // USED, found % USED].astype(F32)
    floor = PROBE_REG * jnp.max(planes[2])
    square = jnp.zeros((STEP, PS), F32)
    for k in range(PS // STEP):
        rows = pl.ds(k * STEP, STEP)
        weight = 1.0 / (planes[2, rows, :] + floor)
        for p in range(2):
            direction = planes[p, rows, :] * weight
            planes[p, rows, :] = direction
            square = square + direction * direction
    spread = jnp.sqrt(jnp.sum(square) / (PS * PS) + EPSILON)
    for p in range(2):
        out[p] = probe[p] - PROBE_RATE * planes[p] / spread


SMEM = pl.BlockSpec(memory_space=pltpu.SMEM)
VMEM = pl.BlockSpec(memory_space=pltpu.VMEM)
ANY = pl.BlockSpec(memory_space=pl.ANY)


def params(mib):
    return pltpu.CompilerParams(vmem_limit_bytes=mib << 20)


def shifted(value, axis, step):
    size = lax.axis_size(axis)
    low, high = max(0, -step), min(size, size - step)
    return lax.ppermute(value, axis, [(k, k + step) for k in range(low, high)])


def slots_call(*arrays):
    like = jax.ShapeDtypeStruct
    forward = dft_blocks()
    return pl.pallas_call(
        main_kernel,
        out_shape=(
            like((2, TH, TW), F32),
            like((2, EH, 256), BF16),
            like((2, EH, 256), BF16),
            like((2, HALF, TW), BF16),
            like((2, HALF, TW), BF16),
            like((BLOCKS, 16, 128), BF16),
            like((BLOCKS, 16, 128), BF16),
        ),
        in_specs=[SMEM] * 2 + [ANY] * 11,
        out_specs=(ANY,) + (VMEM,) * 6,
        scratch_shapes=[
            pltpu.VMEM((2, EW // 128, EH, 128), F32),
            pltpu.VMEM((2, EW // 128, EH, 128), F32),
            pltpu.VMEM((2 * PS, PS), BF16),
            pltpu.VMEM((PS, 2 * PS), BF16),
            pltpu.VMEM((2 * PS, PS), BF16),
            pltpu.VMEM((PS, 2 * PS), BF16),
            pltpu.VMEM((2, PS, 128), F32),
            pltpu.VMEM((2, 2, PS, PS), F32),
            pltpu.VMEM((3, PS, PS), F32),
            pltpu.VMEM((2, PS, PS), F32),
            pltpu.VMEM((PMAX, PS, PS), BF16),
            pltpu.VMEM((2 * PS, 2 * PS), BF16),
            pltpu.VMEM((2 * PS, 2 * PS), BF16),
            pltpu.VMEM((2, HALF, TW), BF16),
            pltpu.VMEM((2, HALF, TW), BF16),
            pltpu.VMEM((2, TH, 256), BF16),
            pltpu.VMEM((2, TH, 256), BF16),
            pltpu.VMEM((2, PS, 256), BF16),
            pltpu.VMEM((2, PS, 256), BF16),
            pltpu.SemaphoreType.DMA((16,)),
            pltpu.SemaphoreType.DMA((PMAX,)),
        ],
        compiler_params=params(60),
        name="slots",
    )(*arrays, jnp.asarray(forward))


def across_edge(value):
    return lax.ppermute(value, "row", [(EDGE - 1, EDGE), (EDGE, EDGE - 1)])


def within_halves(value, step):
    rows = [k for k in range(lax.axis_size("row")) if k // EDGE == (k + step) // EDGE]
    return lax.ppermute(value, "row", [(k, k + step) for k in rows])


def on_device(object_field, probe_field, intensities, positions, tile_counts):
    like = jax.ShapeDtypeStruct
    my_row = lax.axis_index("row")
    where = positions.transpose(0, 2, 3, 1).reshape(-1, positions.shape[1])
    head, tail = object_field[:, :HALF, :].astype(BF16), object_field[:, TH - HALF :, :].astype(BF16)
    across = across_edge(jnp.where(my_row == EDGE, head, tail))
    above = within_halves(tail, 1)
    below = within_halves(head, -1)
    before = shifted(object_field[:, :, TW - 256 :].astype(BF16), "col", 1)
    after = shifted(object_field[:, :, :256].astype(BF16), "col", -1)
    weight = pl.pallas_call(
        illumination_kernel,
        out_shape=like((TH, TW), F32),
        in_specs=[SMEM, SMEM, VMEM],
        out_specs=VMEM,
        scratch_shapes=[pltpu.VMEM((CANVAS // 128, CANVAS, 128), F32), pltpu.VMEM((3, PS, 128), F32)],
        compiler_params=params(60),
        cost_estimate=pl.CostEstimate(flops=20_000_000, bytes_accessed=20_000_000, transcendentals=0),
        name="illumination",
    )(where, tile_counts, probe_field)
    across, above, below, weight = lax.optimization_barrier((across, above, below, weight))
    corners = jnp.concatenate(
        [jnp.where(my_row == EDGE, across, above), jnp.where(my_row == EDGE - 1, across, below)], axis=1
    )
    corners_before = shifted(corners[:, :, TW - 256 :], "col", 1)
    corners_after = shifted(corners[:, :, :256], "col", -1)
    field, rim_before, rim_after, rim_above, rim_below, kept, given = slots_call(
        where, tile_counts, object_field, across, above, below, before, after,
        corners_before, corners_after, probe_field, intensities.reshape(PMAX, PS, PS),
    )
    cols, rows = lax.axis_size("col"), lax.axis_size("row")
    device = np.arange(rows * cols).reshape(2, 4, 4, 4, 2)
    plane = device.transpose(0, 2, 4, 1, 3).reshape(-1, 16).tolist()
    line = device.transpose(1, 3, 4, 0, 2).reshape(-1, 8).tolist()
    partner = [(k, k ^ 1) for k in range(cols)]

    def exchanged(pieces, groups):
        return lax.all_to_all(pieces, ("row", "col"), 0, 0, axis_index_groups=groups)

    def total_of(pieces, times, flops):
        return pl.pallas_call(
            total_kernel,
            out_shape=like((times,) + pieces.shape[1:], BF16),
            in_specs=[VMEM],
            out_specs=VMEM,
            cost_estimate=pl.CostEstimate(flops=flops, bytes_accessed=0, transcendentals=0),
            name="total",
        )(pieces)

    arrived = lax.ppermute(given, "col", partner)
    mine = (kept.astype(F32) + arrived.astype(F32)).astype(BF16)
    mine, rim_before, rim_after = lax.optimization_barrier((mine, rim_before, rim_after))
    from_before = shifted(rim_after, "col", 1)
    from_after = shifted(rim_before, "col", -1)
    parts = exchanged(mine.reshape(16, -1, 16, 128), plane)
    sums = total_of(parts, 8, 10_000_000_000)
    parts = exchanged(sums, line)
    sides = jnp.concatenate([from_before, from_after], axis=2).astype(F32)
    up = (rim_above.astype(F32) + sides[:, :HALF]).astype(BF16)
    down = (rim_below.astype(F32) + sides[:, HALF + TH :]).astype(BF16)
    across = across_edge(jnp.where(my_row == EDGE, up, down))
    from_below = within_halves(up, -1)
    from_above = within_halves(down, 1)
    sums = total_of(parts, 16, 1_000_000_000)
    half = exchanged(sums, plane).reshape(BLOCKS, 16, 128)
    new_object = pl.pallas_call(
        object_kernel,
        out_shape=like((2, TH, TW), F32),
        in_specs=[VMEM] * 8,
        out_specs=VMEM,
        compiler_params=params(60),
        cost_estimate=pl.CostEstimate(flops=40_000_000_000, bytes_accessed=12_000_000, transcendentals=0),
        name="new_object",
    )(object_field, field, from_before, from_after, across, from_above, from_below, weight)
    half, new_object = lax.optimization_barrier((half, new_object))
    other = lax.ppermute(half, "col", partner)
    new_probe = pl.pallas_call(
        probe_kernel,
        out_shape=like((2, PS, PS), F32),
        in_specs=[VMEM] * 3,
        out_specs=VMEM,
        scratch_shapes=[pltpu.VMEM((2, BLOCKS, 16, 128), BF16), pltpu.VMEM((3, PS, PS), F32)],
        compiler_params=params(60),
        name="new_probe",
    )(half, other, probe_field)
    return (new_object, new_probe)


def solution(mesh):
    placed = (P(None, "row", "col"), P(), P("row", "col", None, None, None), P(), P())
    return jax.shard_map(
        on_device,
        mesh=mesh,
        in_specs=placed,
        out_specs=(P(None, "row", "col"), P()),
        check_vma=False,
    )
```

```python
import functools

import jax
import jax.numpy as jnp
import ml_dtypes
import numpy as np
from jax import lax
from jax.experimental import pallas as pl
from jax.experimental.pallas import tpu as pltpu
from jax.sharding import PartitionSpec as P

OBJECT_REG = 0.1
PROBE_REG = 0.1
PROBE_RATE = 0.5
EPSILON = 1e-06

PS = 384
HALF = 192
TH = 512
TW = 512
PMAX = 6
EH = TH + PS
EW = TW + 512
CANVAS = 1280
USED = 108
BLOCKS = 112
STEP = 128
BAND = 96
PART = 64
EDGE = 4
F32 = jnp.float32
BF16 = jnp.bfloat16


def dft_blocks():
    index = np.arange(PS)
    product = (index[:, None] * index[None, :]) % PS
    angles = product.astype(np.float32) * np.float32(2.0 * np.pi / PS)
    norm = np.float32(1.0) / np.sqrt(np.float32(PS))
    cos = (np.cos(angles) * norm).astype(ml_dtypes.bfloat16)
    sin = (-np.sin(angles) * norm).astype(ml_dtypes.bfloat16)
    forward = np.block([[cos, sin], [-sin, cos]])
    order = np.arange(2 * PS).reshape(2, 3, 128).transpose(1, 0, 2).reshape(-1)
    return forward[:, order]


def lane_parts(column):
    block = column // 128
    return block, column - block * 128


def center_of(positions, row, col, slot):
    at = (row * PMAX + slot) * 2
    return positions[at, col], positions[at + 1, col]


def rolled_out(blocks, shift, lanes):
    turned = [pltpu.roll(b, shift, axis=1) for b in blocks]
    keep = lanes >= shift
    zero = jnp.zeros_like(turned[0])
    return [
        jnp.where(keep, turned[0], zero),
        jnp.where(keep, turned[1], turned[0]),
        jnp.where(keep, turned[2], turned[1]),
        jnp.where(keep, zero, turned[2]),
    ]


def rolled_in(blocks, shift, lanes):
    turned = [pltpu.roll(b, (128 - shift) % 128, axis=1) for b in blocks]
    keep = lanes < 128 - shift
    return [jnp.where(keep, turned[k], turned[k + 1]) for k in range(3)]


def illumination_kernel(positions, counts, probe, out, canvas, power):
    my_row, my_col = lax.axis_index("row"), lax.axis_index("col")
    for j in range(3):
        cols = pl.ds(j * 128, 128)
        power[j] = probe[0, :, cols] * probe[0, :, cols] + probe[1, :, cols] * probe[1, :, cols]
    first, last = PS // 128, (PS + TW) // 128
    for j in range(first, last):
        canvas[j, pl.ds(PS, TH), :] = jnp.zeros((TH, 128), F32)
    lanes = lax.broadcasted_iota(jnp.int32, (BAND, 128), 1)
    grid_r, grid_c = 8, 32

    def tile(k, carry):
        down, across = k // 3 - 1, k % 3 - 1
        row, col = my_row + down, my_col + across
        inside = (row >= 0) & (row < grid_r) & (col >= 0) & (col < grid_c)
        row, col = jnp.where(inside, row, 0), jnp.where(inside, col, 0)
        count = jnp.where(inside, counts[row, col], 0)

        def slot(s, inner):
            top, left = center_of(positions, row, col, s)
            top = top + down * TH - HALF + PS
            left = left + across * TW - HALF + PS
            meets = (top > 0) & (top < PS + TH) & (left > 0) & (left < PS + TW)

            @pl.when(meets)
            def _():
                block, shift = lane_parts(left)
                low = jnp.maximum(PS - top, 0) // BAND
                high = (jnp.minimum(PS + TH - top, PS) + BAND - 1) // BAND

                def band(c, deep):
                    rows = pl.ds(pl.multiple_of(c * BAND, BAND), BAND)
                    parts = rolled_out([power[j, rows, :] for j in range(3)], shift, lanes)
                    for j in range(4):
                        canvas[block + j, pl.ds(top + c * BAND, BAND), :] += parts[j]
                    return deep

                lax.fori_loop(low, high, band, 0)

            return inner

        return lax.fori_loop(0, count, slot, carry)

    lax.fori_loop(0, 9, tile, 0)
    floor = OBJECT_REG * jnp.max(power[...])
    for j in range(TW // 128):
        out[:, pl.ds(j * 128, 128)] = 1.0 / (canvas[first + j, pl.ds(PS, TH), :] + floor)


def main_kernel(
    positions, counts, center, across_in, above_in, below_in, before_in, after_in,
    corners_before_in, corners_after_in, probe_in, intensity_in, forward_in,
    field, rim_before, rim_after, rim_above, rim_below, kept, given,
    extended, total, wave, halfway, residual, returning, turned, window, probe_sum,
    probe, intensity, forward, adjoint, above, below, before, after, corners_before, corners_after,
    copied, slot_copied,
):
    my_row, my_col = lax.axis_index("row"), lax.axis_index("col")
    count = counts[my_row, my_col]

    def inward(s):
        return pltpu.make_async_copy(intensity_in.at[s], intensity.at[s], slot_copied.at[s])

    pairs = [(before_in, before), (after_in, after)]
    pairs += [(corners_before_in, corners_before), (corners_after_in, corners_after)]
    pairs += [(probe_in, probe), (forward_in, forward)]
    for p in range(2):
        for j in range(4):
            pairs.append((center.at[p, :, pl.ds(j * 128, 128)], extended.at[p, j + 2, pl.ds(HALF, TH), :]))
    copies = [pltpu.make_async_copy(a, b, copied.at[k]) for k, (a, b) in enumerate(pairs)]
    rims = ((above_in, above, my_row == EDGE), (below_in, below, my_row == EDGE - 1))
    for k, (rim_in, rim, from_across) in enumerate(rims):
        near = pltpu.make_async_copy(rim_in, rim, copied.at[14 + k])
        pl.when(from_across)(pltpu.make_async_copy(across_in, rim, copied.at[14 + k]).start)
        pl.when(jnp.logical_not(from_across))(near.start)
        copies.insert(0, near)
    for copy in copies[2:]:
        copy.start()
    lax.fori_loop(0, count, lambda s, carry: (inward(s).start(), carry)[1], 0)
    total[...] = jnp.zeros_like(total)
    probe_sum[...] = jnp.zeros_like(probe_sum)
    for copy in copies[:6]:
        copy.wait()
    for p in range(2):
        for j in range(EW // 128):
            if 2 <= j < 6:
                cols = pl.ds((j - 2) * 128, 128)
                over, under, low = above, below, 0
            else:
                cols = pl.ds(j % 2 * 128, 128)
                middle, over = (before, corners_before) if j < 2 else (after, corners_after)
                under, low = over, HALF
                extended[p, j, pl.ds(HALF, TH), :] = middle[p, :, cols].astype(F32)
            extended[p, j, pl.ds(0, HALF), :] = over[p, pl.ds(0, HALF), cols].astype(F32)
            extended[p, j, pl.ds(HALF + TH, HALF), :] = under[p, pl.ds(low, HALF), cols].astype(F32)
    for copy in copies[6:]:
        copy.wait()
    for k in range(2):
        for j in range(6):
            here = (pl.ds(k * PS, PS), pl.ds(j * 128, 128))
            adjoint[here] = forward[here] if k == j % 2 else -forward[here]

    def place_of(s):
        top, left = center_of(positions, my_row, my_col, s)
        return (top,) + lane_parts(left + 64)

    def leave(s, k):
        top, block, shift = place_of(s)
        lanes = lax.broadcasted_iota(jnp.int32, (PART, 128), 1)
        for at in range(k * 128, (k + 1) * 128, PART):
            rows = pl.ds(at, PART)
            cells = []
            for p in range(2):
                found = [extended[p, block + j, pl.ds(top + at, PART), :] for j in range(4)]
                cells.append(jnp.concatenate(rolled_in(found, shift, lanes), axis=1))
                window[s % 2, p, rows, :] = cells[p]
            pr, pi = probe[0, rows, :], probe[1, rows, :]
            wave[pl.ds(k * 128 + at, PART), :] = (pr * cells[0] - pi * cells[1]).astype(BF16)
            wave[pl.ds(k * 128 + at + 128, PART), :] = (pr * cells[1] + pi * cells[0]).astype(BF16)

    for k in range(3):
        leave(0, k)

    def slot(s, carry):
        top, block, shift = place_of(s)
        half = jnp.dot(adjoint[...], wave[...], preferred_element_type=F32).astype(BF16)
        halfway[:, pl.ds(0, PS)] = half[:PS]
        halfway[:, pl.ds(PS, PS)] = half[PS:]
        inward(s).wait()
        for j in range(3):
            cols = pl.ds(j * 128, 128)
            far = jnp.dot(halfway[...], forward[:, pl.ds(j * 256, 256)], preferred_element_type=F32)
            far_r, far_i = far[:, :128], far[:, 128:]
            misfit = far_r * far_r + far_i * far_i - intensity[s, :, cols].astype(F32)
            real, imaginary = (misfit * far_r).astype(BF16), (misfit * far_i).astype(BF16)
            for k in range(3):
                residual[pl.ds(k * 256, 128), cols] = real[k * 128 : (k + 1) * 128]
                residual[pl.ds(k * 256 + 128, 128), cols] = imaginary[k * 128 : (k + 1) * 128]
            leave(jnp.minimum(s + 1, count - 1), j)
        back = jnp.dot(forward[...], residual[...], preferred_element_type=F32).astype(BF16)
        returning[:, pl.ds(0, PS)] = back[:PS]
        returning[:, pl.ds(PS, PS)] = back[PS:]
        lanes = lax.broadcasted_iota(jnp.int32, (PART, 128), 1)
        for j in range(3):
            cols = pl.ds(j * 128, 128)
            gradient = jnp.dot(returning[...], adjoint[:, pl.ds(j * 256, 256)], preferred_element_type=F32)
            for k in range(PS // PART):
                rows = pl.ds(k * PART, PART)
                gr, gi = gradient[k * PART : (k + 1) * PART, :128], gradient[k * PART : (k + 1) * PART, 128:]
                pr, pi = probe[0, rows, cols], probe[1, rows, cols]
                wr, wi = window[s % 2, 0, rows, cols], window[s % 2, 1, rows, cols]
                for p, term in ((0, pr * gr + pi * gi), (1, pr * gi - pi * gr)):
                    term = pltpu.roll(term, shift, axis=1)
                    past = turned[p, rows, :] if j else jnp.zeros_like(term)
                    total[p, block + j, pl.ds(top + k * PART, PART), :] += jnp.where(lanes >= shift, term, past)
                    if j < 2:
                        turned[p, rows, :] = term
                    else:
                        total[p, block + 3, pl.ds(top + k * PART, PART), :] += jnp.where(lanes < shift, term, 0.0)
                probe_sum[0, rows, cols] += wr * gr + wi * gi
                probe_sum[1, rows, cols] += wr * gi - wi * gr
                probe_sum[2, rows, cols] += wr * wr + wi * wi
        return carry

    lax.fori_loop(0, count, slot, 0)
    pairs = []
    for p in range(2):
        for j in range(4):
            cols = pl.ds(j * 128, 128)
            pairs.append((total.at[p, j + 2, pl.ds(HALF, TH), :], field.at[p, :, cols]))
    copies = [pltpu.make_async_copy(a, b, copied.at[k]) for k, (a, b) in enumerate(pairs)]
    for copy in copies:
        copy.start()
    for p in range(2):
        for j in range(EW // 128):
            cols = pl.ds(j % 2 * 128, 128)
            if 2 <= j < 6:
                cols = pl.ds((j - 2) * 128, 128)
                rim_above[p, :, cols] = total[p, j, pl.ds(0, HALF), :].astype(BF16)
                rim_below[p, :, cols] = total[p, j, pl.ds(HALF + TH, HALF), :].astype(BF16)
            else:
                rim = rim_before if j < 2 else rim_after
                rim[p, :, cols] = total[p, j].astype(BF16)
    for core in range(2):

        @pl.when(my_col % 2 == core)
        def _():
            for ref, half, kind in ((kept, core, BF16), (given, 1 - core, BF16)):
                for at in range(BLOCKS):
                    if at < USED:
                        found = half * USED + at
                        p, k, j = found // 72, found // 3 % 24, found % 3
                        ref[at] = probe_sum[p, pl.ds(k * 16, 16), pl.ds(j * 128, 128)].astype(kind)
                    else:
                        ref[at] = jnp.zeros((16, 128), kind)

    for copy in copies:
        copy.wait()


def total_kernel(pieces, out):
    total = pieces[0].astype(F32)
    for k in range(1, pieces.shape[0]):
        total = total + pieces[k].astype(F32)
    for k in range(out.shape[0]):
        out[k] = total.astype(BF16)


def cut_kernel(cells, out, piece, copied):
    first = jnp.where(lax.axis_index("row") == EDGE, 0, TH - HALF)
    copy = pltpu.make_async_copy(cells.at[:, pl.ds(pl.multiple_of(first, 64), HALF), :], piece, copied)
    copy.start()
    copy.wait()
    out[...] = piece[...].astype(BF16)


def object_kernel(center, field, from_before, from_after, weight, out):
    for k in range(TH // 64):
        rows = pl.ds(k * 64, 64)
        outer = pl.ds(HALF + k * 64, 64)
        for p in range(2):
            sides = [from_before[p, outer, :], from_after[p, outer, :]]
            cells = field[p, rows, :] + jnp.concatenate(sides, axis=1).astype(F32)
            out[p, rows, :] = center[p, rows, :] - cells * weight[rows, :]


def rims_kernel(base, weight_in, across, from_above, from_below, out, cells, weight, arrived, left):
    my_row = lax.axis_index("row")
    places = (pl.ds(0, HALF), pl.ds(TH - HALF, HALF))
    inward, outward = [], []
    for k, rows in enumerate(places):
        inward.append(pltpu.make_async_copy(base.at[:, rows, :], cells.at[k], arrived.at[k]))
        inward.append(pltpu.make_async_copy(weight_in.at[rows, :], weight.at[k], arrived.at[2 + k]))
        outward.append(pltpu.make_async_copy(cells.at[k], out.at[:, rows, :], left.at[k]))
    for copy in inward:
        copy.start()
    for k, (near, edge) in enumerate(((from_above, EDGE), (from_below, EDGE - 1))):
        inward[2 * k].wait()
        inward[2 * k + 1].wait()
        for p in range(2):
            rim = jnp.where(my_row == edge, across[p].astype(F32), near[p].astype(F32))
            cells[k, p] = cells[k, p] - rim * weight[k]
        outward[k].start()
    for copy in outward:
        copy.wait()


def probe_kernel(half, other, probe, out, sums, planes):
    core = lax.axis_index("col") % 2
    sums[core] = half[...]
    sums[1 - core] = other[...]
    for found in range(2 * USED):
        p, k, j = found // 72, found // 3 % 24, found % 3
        planes[p, pl.ds(k * 16, 16), pl.ds(j * 128, 128)] = sums[found // USED, found % USED].astype(F32)
    floor = PROBE_REG * jnp.max(planes[2])
    square = jnp.zeros((STEP, PS), F32)
    for k in range(PS // STEP):
        rows = pl.ds(k * STEP, STEP)
        weight = 1.0 / (planes[2, rows, :] + floor)
        for p in range(2):
            direction = planes[p, rows, :] * weight
            planes[p, rows, :] = direction
            square = square + direction * direction
    spread = jnp.sqrt(jnp.sum(square) / (PS * PS) + EPSILON)
    for p in range(2):
        out[p] = probe[p] - PROBE_RATE * planes[p] / spread


SMEM = pl.BlockSpec(memory_space=pltpu.SMEM)
VMEM = pl.BlockSpec(memory_space=pltpu.VMEM)
ANY = pl.BlockSpec(memory_space=pl.ANY)


def params(mib):
    return pltpu.CompilerParams(vmem_limit_bytes=mib << 20)


def shifted(value, axis, step):
    size = lax.axis_size(axis)
    low, high = max(0, -step), min(size, size - step)
    return lax.ppermute(value, axis, [(k, k + step) for k in range(low, high)])


def slots_call(*arrays):
    like = jax.ShapeDtypeStruct
    forward = dft_blocks()
    return pl.pallas_call(
        main_kernel,
        out_shape=(
            like((2, TH, TW), F32),
            like((2, EH, 256), BF16),
            like((2, EH, 256), BF16),
            like((2, HALF, TW), BF16),
            like((2, HALF, TW), BF16),
            like((BLOCKS, 16, 128), BF16),
            like((BLOCKS, 16, 128), BF16),
        ),
        in_specs=[SMEM] * 2 + [ANY] * 11,
        out_specs=(ANY,) + (VMEM,) * 6,
        scratch_shapes=[
            pltpu.VMEM((2, EW // 128, EH, 128), F32),
            pltpu.VMEM((2, EW // 128, EH, 128), F32),
            pltpu.VMEM((2 * PS, PS), BF16),
            pltpu.VMEM((PS, 2 * PS), BF16),
            pltpu.VMEM((2 * PS, PS), BF16),
            pltpu.VMEM((PS, 2 * PS), BF16),
            pltpu.VMEM((2, PS, 128), F32),
            pltpu.VMEM((2, 2, PS, PS), F32),
            pltpu.VMEM((3, PS, PS), F32),
            pltpu.VMEM((2, PS, PS), F32),
            pltpu.VMEM((PMAX, PS, PS), BF16),
            pltpu.VMEM((2 * PS, 2 * PS), BF16),
            pltpu.VMEM((2 * PS, 2 * PS), BF16),
            pltpu.VMEM((2, HALF, TW), BF16),
            pltpu.VMEM((2, HALF, TW), BF16),
            pltpu.VMEM((2, TH, 256), BF16),
            pltpu.VMEM((2, TH, 256), BF16),
            pltpu.VMEM((2, PS, 256), BF16),
            pltpu.VMEM((2, PS, 256), BF16),
            pltpu.SemaphoreType.DMA((16,)),
            pltpu.SemaphoreType.DMA((PMAX,)),
        ],
        compiler_params=params(60),
        name="slots",
    )(*arrays, jnp.asarray(forward))


def across_edge(value):
    return lax.ppermute(value, "row", [(EDGE - 1, EDGE), (EDGE, EDGE - 1)])


def within_halves(value, step):
    rows = [k for k in range(lax.axis_size("row")) if k // EDGE == (k + step) // EDGE]
    return lax.ppermute(value, "row", [(k, k + step) for k in rows])


def on_device(object_field, probe_field, intensities, positions, tile_counts):
    like = jax.ShapeDtypeStruct
    my_row = lax.axis_index("row")
    where = positions.transpose(0, 2, 3, 1).reshape(-1, positions.shape[1])
    head, tail = object_field[:, :HALF, :].astype(BF16), object_field[:, TH - HALF :, :].astype(BF16)
    piece = pl.pallas_call(
        cut_kernel,
        out_shape=like((2, HALF, TW), BF16),
        in_specs=[ANY],
        out_specs=VMEM,
        scratch_shapes=[pltpu.VMEM((2, HALF, TW), F32), pltpu.SemaphoreType.DMA],
        compiler_params=params(60),
        cost_estimate=pl.CostEstimate(flops=400_000, bytes_accessed=1_200_000, transcendentals=0),
        name="cut",
    )(object_field)
    across = across_edge(piece)
    above = within_halves(tail, 1)
    below = within_halves(head, -1)
    before = shifted(object_field[:, :, TW - 256 :].astype(BF16), "col", 1)
    after = shifted(object_field[:, :, :256].astype(BF16), "col", -1)
    weight = pl.pallas_call(
        illumination_kernel,
        out_shape=like((TH, TW), F32),
        in_specs=[SMEM, SMEM, VMEM],
        out_specs=VMEM,
        scratch_shapes=[pltpu.VMEM((CANVAS // 128, CANVAS, 128), F32), pltpu.VMEM((3, PS, 128), F32)],
        compiler_params=params(60),
        cost_estimate=pl.CostEstimate(flops=20_000_000, bytes_accessed=20_000_000, transcendentals=0),
        name="illumination",
    )(where, tile_counts, probe_field)
    across, above, below, weight = lax.optimization_barrier((across, above, below, weight))
    corners = jnp.concatenate(
        [jnp.where(my_row == EDGE, across, above), jnp.where(my_row == EDGE - 1, across, below)], axis=1
    )
    corners_before = shifted(corners[:, :, TW - 256 :], "col", 1)
    corners_after = shifted(corners[:, :, :256], "col", -1)
    field, rim_before, rim_after, rim_above, rim_below, kept, given = slots_call(
        where, tile_counts, object_field, across, above, below, before, after,
        corners_before, corners_after, probe_field, intensities.reshape(PMAX, PS, PS),
    )
    cols, rows = lax.axis_size("col"), lax.axis_size("row")
    device = np.arange(rows * cols).reshape(2, 4, 4, 4, 2)
    plane = device.transpose(0, 2, 4, 1, 3).reshape(-1, 16).tolist()
    line = device.transpose(1, 3, 4, 0, 2).reshape(-1, 8).tolist()
    partner = [(k, k ^ 1) for k in range(cols)]

    def exchanged(pieces, groups):
        return lax.all_to_all(pieces, ("row", "col"), 0, 0, axis_index_groups=groups)

    def total_of(pieces, times, flops):
        return pl.pallas_call(
            total_kernel,
            out_shape=like((times,) + pieces.shape[1:], BF16),
            in_specs=[VMEM],
            out_specs=VMEM,
            compiler_params=params(8),
            cost_estimate=pl.CostEstimate(flops=flops, bytes_accessed=0, transcendentals=0),
            name="total",
        )(pieces)

    arrived = lax.ppermute(given, "col", partner)
    mine = (kept.astype(F32) + arrived.astype(F32)).astype(BF16)
    mine, rim_before, rim_after = lax.optimization_barrier((mine, rim_before, rim_after))
    from_before = shifted(rim_after, "col", 1)
    from_after = shifted(rim_before, "col", -1)
    parts = exchanged(mine.reshape(16, -1, 16, 128), plane)
    sums = total_of(parts, 8, 10_000_000_000)
    parts = exchanged(sums, line)
    sides = jnp.concatenate([from_before, from_after], axis=2).astype(F32)
    up = (rim_above.astype(F32) + sides[:, :HALF]).astype(BF16)
    down = (rim_below.astype(F32) + sides[:, HALF + TH :]).astype(BF16)
    across = across_edge(jnp.where(my_row == EDGE, up, down))
    from_below = within_halves(up, -1)
    from_above = within_halves(down, 1)
    sums = total_of(parts, 16, 1_000_000_000)
    half = exchanged(sums, plane).reshape(BLOCKS, 16, 128)
    new_object = pl.pallas_call(
        object_kernel,
        out_shape=like((2, TH, TW), F32),
        in_specs=[VMEM] * 5,
        out_specs=VMEM,
        compiler_params=params(60),
        cost_estimate=pl.CostEstimate(flops=4_000_000, bytes_accessed=12_000_000, transcendentals=0),
        name="new_object",
    )(object_field, field, from_before, from_after, weight)
    new_object = pl.pallas_call(
        rims_kernel,
        out_shape=like((2, TH, TW), F32),
        in_specs=[ANY, ANY, VMEM, VMEM, VMEM],
        out_specs=ANY,
        scratch_shapes=[
            pltpu.VMEM((2, 2, HALF, TW), F32),
            pltpu.VMEM((2, HALF, TW), F32),
            pltpu.SemaphoreType.DMA((4,)),
            pltpu.SemaphoreType.DMA((2,)),
        ],
        input_output_aliases={0: 0},
        compiler_params=params(16),
        cost_estimate=pl.CostEstimate(flops=40_000_000_000, bytes_accessed=4_000_000, transcendentals=0),
        name="rims",
    )(new_object, weight, across, from_above, from_below)
    half, new_object = lax.optimization_barrier((half, new_object))
    other = lax.ppermute(half, "col", partner)
    new_probe = pl.pallas_call(
        probe_kernel,
        out_shape=like((2, PS, PS), F32),
        in_specs=[VMEM] * 3,
        out_specs=VMEM,
        scratch_shapes=[pltpu.VMEM((2, BLOCKS, 16, 128), BF16), pltpu.VMEM((3, PS, PS), F32)],
        compiler_params=params(24),
        name="new_probe",
    )(half, other, probe_field)
    return (new_object, new_probe)


def solution(mesh):
    placed = (P(None, "row", "col"), P(), P("row", "col", None, None, None), P(), P())
    return jax.shard_map(
        on_device,
        mesh=mesh,
        in_specs=placed,
        out_specs=(P(None, "row", "col"), P()),
        check_vma=False,
    )
```

```python
import functools

import jax
import jax.numpy as jnp
import ml_dtypes
import numpy as np
from jax import lax
from jax.experimental import pallas as pl
from jax.experimental.pallas import tpu as pltpu
from jax.sharding import PartitionSpec as P

OBJECT_REG = 0.1
PROBE_REG = 0.1
PROBE_RATE = 0.5
EPSILON = 1e-06

PS = 384
HALF = 192
TH = 512
TW = 512
PMAX = 6
EH = TH + PS
EW = TW + 512
CANVAS = 1280
USED = 108
BLOCKS = 112
STEP = 128
BAND = 96
PART = 64
EDGE = 4
F32 = jnp.float32
BF16 = jnp.bfloat16


def dft_blocks():
    index = np.arange(PS)
    product = (index[:, None] * index[None, :]) % PS
    angles = product.astype(np.float32) * np.float32(2.0 * np.pi / PS)
    norm = np.float32(1.0) / np.sqrt(np.float32(PS))
    cos = (np.cos(angles) * norm).astype(ml_dtypes.bfloat16)
    sin = (-np.sin(angles) * norm).astype(ml_dtypes.bfloat16)
    forward = np.block([[cos, sin], [-sin, cos]])
    order = np.arange(2 * PS).reshape(2, 3, 128).transpose(1, 0, 2).reshape(-1)
    return forward[:, order]


def lane_parts(column):
    block = column // 128
    return block, column - block * 128


def center_of(positions, row, col, slot):
    at = (row * PMAX + slot) * 2
    return positions[at, col], positions[at + 1, col]


def rolled_out(blocks, shift, lanes):
    turned = [pltpu.roll(b, shift, axis=1) for b in blocks]
    keep = lanes >= shift
    zero = jnp.zeros_like(turned[0])
    return [
        jnp.where(keep, turned[0], zero),
        jnp.where(keep, turned[1], turned[0]),
        jnp.where(keep, turned[2], turned[1]),
        jnp.where(keep, zero, turned[2]),
    ]


def rolled_in(blocks, shift, lanes):
    turned = [pltpu.roll(b, (128 - shift) % 128, axis=1) for b in blocks]
    keep = lanes < 128 - shift
    return [jnp.where(keep, turned[k], turned[k + 1]) for k in range(3)]


def illumination_kernel(positions, counts, probe, out, canvas, power):
    my_row, my_col = lax.axis_index("row"), lax.axis_index("col")
    for j in range(3):
        cols = pl.ds(j * 128, 128)
        power[j] = probe[0, :, cols] * probe[0, :, cols] + probe[1, :, cols] * probe[1, :, cols]
    first, last = PS // 128, (PS + TW) // 128
    for j in range(first, last):
        canvas[j, pl.ds(PS, TH), :] = jnp.zeros((TH, 128), F32)
    lanes = lax.broadcasted_iota(jnp.int32, (BAND, 128), 1)
    grid_r, grid_c = 8, 32

    def tile(k, carry):
        down, across = k // 3 - 1, k % 3 - 1
        row, col = my_row + down, my_col + across
        inside = (row >= 0) & (row < grid_r) & (col >= 0) & (col < grid_c)
        row, col = jnp.where(inside, row, 0), jnp.where(inside, col, 0)
        count = jnp.where(inside, counts[row, col], 0)

        def slot(s, inner):
            top, left = center_of(positions, row, col, s)
            top = top + down * TH - HALF + PS
            left = left + across * TW - HALF + PS
            meets = (top > 0) & (top < PS + TH) & (left > 0) & (left < PS + TW)

            @pl.when(meets)
            def _():
                block, shift = lane_parts(left)
                low = jnp.maximum(PS - top, 0) // BAND
                high = (jnp.minimum(PS + TH - top, PS) + BAND - 1) // BAND

                def band(c, deep):
                    rows = pl.ds(pl.multiple_of(c * BAND, BAND), BAND)
                    parts = rolled_out([power[j, rows, :] for j in range(3)], shift, lanes)
                    for j in range(4):
                        canvas[block + j, pl.ds(top + c * BAND, BAND), :] += parts[j]
                    return deep

                lax.fori_loop(low, high, band, 0)

            return inner

        return lax.fori_loop(0, count, slot, carry)

    lax.fori_loop(0, 9, tile, 0)
    floor = OBJECT_REG * jnp.max(power[...])
    for j in range(TW // 128):
        out[:, pl.ds(j * 128, 128)] = 1.0 / (canvas[first + j, pl.ds(PS, TH), :] + floor)


def main_kernel(
    positions, counts, center, across_in, above_in, below_in, before_in, after_in,
    corners_before_in, corners_after_in, probe_in, intensity_in, forward_in,
    field, rim_before, rim_after, rim_above, rim_below, kept, given,
    extended, total, wave, halfway, residual, returning, turned, window, probe_sum,
    probe, intensity, forward, adjoint, above, below, before, after, corners_before, corners_after,
    copied, slot_copied,
):
    my_row, my_col = lax.axis_index("row"), lax.axis_index("col")
    count = counts[my_row, my_col]

    def inward(s):
        return pltpu.make_async_copy(intensity_in.at[s], intensity.at[s], slot_copied.at[s])

    pairs = [(before_in, before), (after_in, after)]
    pairs += [(corners_before_in, corners_before), (corners_after_in, corners_after)]
    pairs += [(probe_in, probe), (forward_in, forward)]
    for p in range(2):
        for j in range(4):
            pairs.append((center.at[p, :, pl.ds(j * 128, 128)], extended.at[p, j + 2, pl.ds(HALF, TH), :]))
    copies = [pltpu.make_async_copy(a, b, copied.at[k]) for k, (a, b) in enumerate(pairs)]
    rims = ((above_in, above, my_row == EDGE), (below_in, below, my_row == EDGE - 1))
    for k, (rim_in, rim, from_across) in enumerate(rims):
        near = pltpu.make_async_copy(rim_in, rim, copied.at[14 + k])
        pl.when(from_across)(pltpu.make_async_copy(across_in, rim, copied.at[14 + k]).start)
        pl.when(jnp.logical_not(from_across))(near.start)
        copies.insert(0, near)
    for copy in copies[2:]:
        copy.start()
    lax.fori_loop(0, count, lambda s, carry: (inward(s).start(), carry)[1], 0)
    total[...] = jnp.zeros_like(total)
    probe_sum[...] = jnp.zeros_like(probe_sum)
    for copy in copies[:6]:
        copy.wait()
    for p in range(2):
        for j in range(EW // 128):
            if 2 <= j < 6:
                cols = pl.ds((j - 2) * 128, 128)
                over, under, low = above, below, 0
            else:
                cols = pl.ds(j % 2 * 128, 128)
                middle, over = (before, corners_before) if j < 2 else (after, corners_after)
                under, low = over, HALF
                extended[p, j, pl.ds(HALF, TH), :] = middle[p, :, cols].astype(F32)
            extended[p, j, pl.ds(0, HALF), :] = over[p, pl.ds(0, HALF), cols].astype(F32)
            extended[p, j, pl.ds(HALF + TH, HALF), :] = under[p, pl.ds(low, HALF), cols].astype(F32)
    for copy in copies[6:]:
        copy.wait()
    for k in range(2):
        for j in range(6):
            here = (pl.ds(k * PS, PS), pl.ds(j * 128, 128))
            adjoint[here] = forward[here] if k == j % 2 else -forward[here]

    def place_of(s):
        top, left = center_of(positions, my_row, my_col, s)
        return (top,) + lane_parts(left + 64)

    def leave(s, k):
        top, block, shift = place_of(s)
        lanes = lax.broadcasted_iota(jnp.int32, (PART, 128), 1)
        for at in range(k * 128, (k + 1) * 128, PART):
            rows = pl.ds(at, PART)
            cells = []
            for p in range(2):
                found = [extended[p, block + j, pl.ds(top + at, PART), :] for j in range(4)]
                cells.append(jnp.concatenate(rolled_in(found, shift, lanes), axis=1))
                window[s % 2, p, rows, :] = cells[p]
            pr, pi = probe[0, rows, :], probe[1, rows, :]
            wave[pl.ds(k * 128 + at, PART), :] = (pr * cells[0] - pi * cells[1]).astype(BF16)
            wave[pl.ds(k * 128 + at + 128, PART), :] = (pr * cells[1] + pi * cells[0]).astype(BF16)

    for k in range(3):
        leave(0, k)

    def slot(s, carry):
        top, block, shift = place_of(s)
        half = jnp.dot(adjoint[...], wave[...], preferred_element_type=F32).astype(BF16)
        halfway[:, pl.ds(0, PS)] = half[:PS]
        halfway[:, pl.ds(PS, PS)] = half[PS:]
        inward(s).wait()
        for j in range(3):
            cols = pl.ds(j * 128, 128)
            far = jnp.dot(halfway[...], forward[:, pl.ds(j * 256, 256)], preferred_element_type=F32)
            far_r, far_i = far[:, :128], far[:, 128:]
            misfit = far_r * far_r + far_i * far_i - intensity[s, :, cols].astype(F32)
            real, imaginary = (misfit * far_r).astype(BF16), (misfit * far_i).astype(BF16)
            for k in range(3):
                residual[pl.ds(k * 256, 128), cols] = real[k * 128 : (k + 1) * 128]
                residual[pl.ds(k * 256 + 128, 128), cols] = imaginary[k * 128 : (k + 1) * 128]
            leave(jnp.minimum(s + 1, count - 1), j)
        back = jnp.dot(forward[...], residual[...], preferred_element_type=F32).astype(BF16)
        returning[:, pl.ds(0, PS)] = back[:PS]
        returning[:, pl.ds(PS, PS)] = back[PS:]
        lanes = lax.broadcasted_iota(jnp.int32, (PART, 128), 1)
        for j in range(3):
            cols = pl.ds(j * 128, 128)
            gradient = jnp.dot(returning[...], adjoint[:, pl.ds(j * 256, 256)], preferred_element_type=F32)
            for k in range(PS // PART):
                rows = pl.ds(k * PART, PART)
                gr, gi = gradient[k * PART : (k + 1) * PART, :128], gradient[k * PART : (k + 1) * PART, 128:]
                pr, pi = probe[0, rows, cols], probe[1, rows, cols]
                wr, wi = window[s % 2, 0, rows, cols], window[s % 2, 1, rows, cols]
                for p, term in ((0, pr * gr + pi * gi), (1, pr * gi - pi * gr)):
                    term = pltpu.roll(term, shift, axis=1)
                    past = turned[p, rows, :] if j else jnp.zeros_like(term)
                    total[p, block + j, pl.ds(top + k * PART, PART), :] += jnp.where(lanes >= shift, term, past)
                    if j < 2:
                        turned[p, rows, :] = term
                    else:
                        total[p, block + 3, pl.ds(top + k * PART, PART), :] += jnp.where(lanes < shift, term, 0.0)
                probe_sum[0, rows, cols] += wr * gr + wi * gi
                probe_sum[1, rows, cols] += wr * gi - wi * gr
                probe_sum[2, rows, cols] += wr * wr + wi * wi
        return carry

    lax.fori_loop(0, count, slot, 0)
    pairs = []
    for p in range(2):
        for j in range(4):
            cols = pl.ds(j * 128, 128)
            pairs.append((total.at[p, j + 2, pl.ds(HALF, TH), :], field.at[p, :, cols]))
    copies = [pltpu.make_async_copy(a, b, copied.at[k]) for k, (a, b) in enumerate(pairs)]
    for copy in copies:
        copy.start()
    for p in range(2):
        for j in range(EW // 128):
            cols = pl.ds(j % 2 * 128, 128)
            if 2 <= j < 6:
                cols = pl.ds((j - 2) * 128, 128)
                rim_above[p, :, cols] = total[p, j, pl.ds(0, HALF), :].astype(BF16)
                rim_below[p, :, cols] = total[p, j, pl.ds(HALF + TH, HALF), :].astype(BF16)
            else:
                rim = rim_before if j < 2 else rim_after
                rim[p, :, cols] = total[p, j].astype(BF16)
    for core in range(2):

        @pl.when(my_col % 2 == core)
        def _():
            for ref, half, kind in ((kept, core, BF16), (given, 1 - core, BF16)):
                for at in range(BLOCKS):
                    if at < USED:
                        found = half * USED + at
                        p, k, j = found // 72, found // 3 % 24, found % 3
                        ref[at] = probe_sum[p, pl.ds(k * 16, 16), pl.ds(j * 128, 128)].astype(kind)
                    else:
                        ref[at] = jnp.zeros((16, 128), kind)

    for copy in copies:
        copy.wait()


def total_kernel(pieces, out):
    total = pieces[0].astype(F32)
    for k in range(1, pieces.shape[0]):
        total = total + pieces[k].astype(F32)
    for k in range(out.shape[0]):
        out[k] = total.astype(BF16)


def cut_kernel(cells, out, piece, copied):
    first = jnp.where(lax.axis_index("row") == EDGE, 0, TH - HALF)
    copy = pltpu.make_async_copy(cells.at[:, pl.ds(pl.multiple_of(first, 64), HALF), :], piece, copied)
    copy.start()
    copy.wait()
    out[...] = piece[...].astype(BF16)


def object_kernel(center, field, from_before, from_after, weight, out):
    for k in range(TH // 64):
        rows = pl.ds(k * 64, 64)
        outer = pl.ds(HALF + k * 64, 64)
        for p in range(2):
            sides = [from_before[p, outer, :], from_after[p, outer, :]]
            cells = field[p, rows, :] + jnp.concatenate(sides, axis=1).astype(F32)
            out[p, rows, :] = center[p, rows, :] - cells * weight[rows, :]


def rims_kernel(base, weight_in, across, from_above, from_below, out, cells, weight, arrived, left):
    my_row = lax.axis_index("row")
    places = (pl.ds(0, HALF), pl.ds(TH - HALF, HALF))
    inward, outward = [], []
    for k, rows in enumerate(places):
        inward.append(pltpu.make_async_copy(base.at[:, rows, :], cells.at[k], arrived.at[k]))
        inward.append(pltpu.make_async_copy(weight_in.at[rows, :], weight.at[k], arrived.at[2 + k]))
        outward.append(pltpu.make_async_copy(cells.at[k], out.at[:, rows, :], left.at[k]))
    for copy in inward:
        copy.start()
    for k, (near, edge) in enumerate(((from_above, EDGE), (from_below, EDGE - 1))):
        inward[2 * k].wait()
        inward[2 * k + 1].wait()
        for p in range(2):
            rim = jnp.where(my_row == edge, across[p].astype(F32), near[p].astype(F32))
            cells[k, p] = cells[k, p] - rim * weight[k]
        outward[k].start()
    for copy in outward:
        copy.wait()


def probe_kernel(half, other, probe, out, sums, planes):
    core = lax.axis_index("col") % 2
    sums[core] = half[...]
    sums[1 - core] = other[...]
    for found in range(2 * USED):
        p, k, j = found // 72, found // 3 % 24, found % 3
        planes[p, pl.ds(k * 16, 16), pl.ds(j * 128, 128)] = sums[found // USED, found % USED].astype(F32)
    floor = PROBE_REG * jnp.max(planes[2])
    square = jnp.zeros((STEP, PS), F32)
    for k in range(PS // STEP):
        rows = pl.ds(k * STEP, STEP)
        weight = 1.0 / (planes[2, rows, :] + floor)
        for p in range(2):
            direction = planes[p, rows, :] * weight
            planes[p, rows, :] = direction
            square = square + direction * direction
    spread = jnp.sqrt(jnp.sum(square) / (PS * PS) + EPSILON)
    for p in range(2):
        out[p] = probe[p] - PROBE_RATE * planes[p] / spread


SMEM = pl.BlockSpec(memory_space=pltpu.SMEM)
VMEM = pl.BlockSpec(memory_space=pltpu.VMEM)
ANY = pl.BlockSpec(memory_space=pl.ANY)


def params(mib):
    return pltpu.CompilerParams(vmem_limit_bytes=mib << 20)


def shifted(value, axis, step):
    size = lax.axis_size(axis)
    low, high = max(0, -step), min(size, size - step)
    return lax.ppermute(value, axis, [(k, k + step) for k in range(low, high)])


def slots_call(*arrays):
    like = jax.ShapeDtypeStruct
    forward = dft_blocks()
    return pl.pallas_call(
        main_kernel,
        out_shape=(
            pltpu.HBM((2, TH, TW), F32),
            pltpu.HBM((2, EH, 256), BF16),
            pltpu.HBM((2, EH, 256), BF16),
            pltpu.HBM((2, HALF, TW), BF16),
            pltpu.HBM((2, HALF, TW), BF16),
            like((BLOCKS, 16, 128), BF16),
            pltpu.HBM((BLOCKS, 16, 128), BF16),
        ),
        in_specs=[SMEM] * 2 + [ANY] * 11,
        out_specs=(ANY,) + (VMEM,) * 6,
        scratch_shapes=[
            pltpu.VMEM((2, EW // 128, EH, 128), F32),
            pltpu.VMEM((2, EW // 128, EH, 128), F32),
            pltpu.VMEM((2 * PS, PS), BF16),
            pltpu.VMEM((PS, 2 * PS), BF16),
            pltpu.VMEM((2 * PS, PS), BF16),
            pltpu.VMEM((PS, 2 * PS), BF16),
            pltpu.VMEM((2, PS, 128), F32),
            pltpu.VMEM((2, 2, PS, PS), F32),
            pltpu.VMEM((3, PS, PS), F32),
            pltpu.VMEM((2, PS, PS), F32),
            pltpu.VMEM((PMAX, PS, PS), BF16),
            pltpu.VMEM((2 * PS, 2 * PS), BF16),
            pltpu.VMEM((2 * PS, 2 * PS), BF16),
            pltpu.VMEM((2, HALF, TW), BF16),
            pltpu.VMEM((2, HALF, TW), BF16),
            pltpu.VMEM((2, TH, 256), BF16),
            pltpu.VMEM((2, TH, 256), BF16),
            pltpu.VMEM((2, PS, 256), BF16),
            pltpu.VMEM((2, PS, 256), BF16),
            pltpu.SemaphoreType.DMA((16,)),
            pltpu.SemaphoreType.DMA((PMAX,)),
        ],
        compiler_params=params(38),
        name="slots",
    )(*arrays, jnp.asarray(forward))


def across_edge(value):
    return lax.ppermute(value, "row", [(EDGE - 1, EDGE), (EDGE, EDGE - 1)])


def within_halves(value, step):
    rows = [k for k in range(lax.axis_size("row")) if k // EDGE == (k + step) // EDGE]
    return lax.ppermute(value, "row", [(k, k + step) for k in rows])


def on_device(object_field, probe_field, intensities, positions, tile_counts):
    like = jax.ShapeDtypeStruct
    my_row = lax.axis_index("row")
    where = positions.transpose(0, 2, 3, 1).reshape(-1, positions.shape[1])
    head, tail = object_field[:, :HALF, :].astype(BF16), object_field[:, TH - HALF :, :].astype(BF16)
    piece = pl.pallas_call(
        cut_kernel,
        out_shape=like((2, HALF, TW), BF16),
        in_specs=[ANY],
        out_specs=VMEM,
        scratch_shapes=[pltpu.VMEM((2, HALF, TW), F32), pltpu.SemaphoreType.DMA],
        compiler_params=params(60),
        cost_estimate=pl.CostEstimate(flops=400_000, bytes_accessed=1_200_000, transcendentals=0),
        name="cut",
    )(object_field)
    across = across_edge(piece)
    above = within_halves(tail, 1)
    below = within_halves(head, -1)
    before = shifted(object_field[:, :, TW - 256 :].astype(BF16), "col", 1)
    after = shifted(object_field[:, :, :256].astype(BF16), "col", -1)
    weight = pl.pallas_call(
        illumination_kernel,
        out_shape=like((TH, TW), F32),
        in_specs=[SMEM, SMEM, VMEM],
        out_specs=VMEM,
        scratch_shapes=[pltpu.VMEM((CANVAS // 128, CANVAS, 128), F32), pltpu.VMEM((3, PS, 128), F32)],
        compiler_params=params(60),
        cost_estimate=pl.CostEstimate(flops=20_000_000, bytes_accessed=20_000_000, transcendentals=0),
        name="illumination",
    )(where, tile_counts, probe_field)
    across, above, below, weight = lax.optimization_barrier((across, above, below, weight))
    corners = jnp.concatenate(
        [jnp.where(my_row == EDGE, across, above), jnp.where(my_row == EDGE - 1, across, below)], axis=1
    )
    corners_before = shifted(corners[:, :, TW - 256 :], "col", 1)
    corners_after = shifted(corners[:, :, :256], "col", -1)
    field, rim_before, rim_after, rim_above, rim_below, kept, given = slots_call(
        where, tile_counts, object_field, across, above, below, before, after,
        corners_before, corners_after, probe_field, intensities.reshape(PMAX, PS, PS),
    )
    cols, rows = lax.axis_size("col"), lax.axis_size("row")
    device = np.arange(rows * cols).reshape(2, 4, 4, 4, 2)
    plane = device.transpose(0, 2, 4, 1, 3).reshape(-1, 16).tolist()
    line = device.transpose(1, 3, 4, 0, 2).reshape(-1, 8).tolist()
    partner = [(k, k ^ 1) for k in range(cols)]

    def exchanged(pieces, groups):
        return lax.all_to_all(pieces, ("row", "col"), 0, 0, axis_index_groups=groups)

    def total_of(pieces, times, flops):
        return pl.pallas_call(
            total_kernel,
            out_shape=like((times,) + pieces.shape[1:], BF16),
            in_specs=[VMEM],
            out_specs=VMEM,
            compiler_params=params(8),
            cost_estimate=pl.CostEstimate(flops=flops, bytes_accessed=0, transcendentals=0),
            name="total",
        )(pieces)

    arrived = lax.ppermute(given, "col", partner)
    mine = (kept.astype(F32) + arrived.astype(F32)).astype(BF16)
    mine, rim_before, rim_after = lax.optimization_barrier((mine, rim_before, rim_after))
    from_before = shifted(rim_after, "col", 1)
    from_after = shifted(rim_before, "col", -1)
    parts = exchanged(mine.reshape(16, -1, 16, 128), plane)
    sums = total_of(parts, 8, 10_000_000_000)
    parts = exchanged(sums, line)
    sides = jnp.concatenate([from_before, from_after], axis=2).astype(F32)
    up = (rim_above.astype(F32) + sides[:, :HALF]).astype(BF16)
    down = (rim_below.astype(F32) + sides[:, HALF + TH :]).astype(BF16)
    across = across_edge(jnp.where(my_row == EDGE, up, down))
    from_below = within_halves(up, -1)
    from_above = within_halves(down, 1)
    sums = total_of(parts, 16, 1_000_000_000)
    half = exchanged(sums, plane).reshape(BLOCKS, 16, 128)
    new_object = pl.pallas_call(
        object_kernel,
        out_shape=like((2, TH, TW), F32),
        in_specs=[VMEM] * 5,
        out_specs=VMEM,
        compiler_params=params(60),
        cost_estimate=pl.CostEstimate(flops=4_000_000, bytes_accessed=12_000_000, transcendentals=0),
        name="new_object",
    )(object_field, field, from_before, from_after, weight)
    new_object = pl.pallas_call(
        rims_kernel,
        out_shape=like((2, TH, TW), F32),
        in_specs=[ANY, ANY, VMEM, VMEM, VMEM],
        out_specs=ANY,
        scratch_shapes=[
            pltpu.VMEM((2, 2, HALF, TW), F32),
            pltpu.VMEM((2, HALF, TW), F32),
            pltpu.SemaphoreType.DMA((4,)),
            pltpu.SemaphoreType.DMA((2,)),
        ],
        input_output_aliases={0: 0},
        compiler_params=params(16),
        cost_estimate=pl.CostEstimate(flops=40_000_000_000, bytes_accessed=4_000_000, transcendentals=0),
        name="rims",
    )(new_object, weight, across, from_above, from_below)
    half, new_object = lax.optimization_barrier((half, new_object))
    other = lax.ppermute(half, "col", partner)
    new_probe = pl.pallas_call(
        probe_kernel,
        out_shape=like((2, PS, PS), F32),
        in_specs=[VMEM] * 3,
        out_specs=VMEM,
        scratch_shapes=[pltpu.VMEM((2, BLOCKS, 16, 128), BF16), pltpu.VMEM((3, PS, PS), F32)],
        compiler_params=params(24),
        name="new_probe",
    )(half, other, probe_field)
    return (new_object, new_probe)


def solution(mesh):
    placed = (P(None, "row", "col"), P(), P("row", "col", None, None, None), P(), P())
    return jax.shard_map(
        on_device,
        mesh=mesh,
        in_specs=placed,
        out_specs=(P(None, "row", "col"), P()),
        check_vma=False,
    )
```

```python
import functools

import jax
import jax.numpy as jnp
import ml_dtypes
import numpy as np
from jax import lax
from jax.experimental import pallas as pl
from jax.experimental.pallas import tpu as pltpu
from jax.sharding import PartitionSpec as P

OBJECT_REG = 0.1
PROBE_REG = 0.1
PROBE_RATE = 0.5
EPSILON = 1e-06

PS = 384
HALF = 192
TH = 512
TW = 512
PMAX = 6
EH = TH + PS
EW = TW + 512
CANVAS = 1280
USED = 108
BLOCKS = 112
STEP = 128
BAND = 96
PART = 64
EDGE = 4
F32 = jnp.float32
BF16 = jnp.bfloat16


def dft_blocks():
    index = np.arange(PS)
    product = (index[:, None] * index[None, :]) % PS
    angles = product.astype(np.float32) * np.float32(2.0 * np.pi / PS)
    norm = np.float32(1.0) / np.sqrt(np.float32(PS))
    cos = (np.cos(angles) * norm).astype(ml_dtypes.bfloat16)
    sin = (-np.sin(angles) * norm).astype(ml_dtypes.bfloat16)
    forward = np.block([[cos, sin], [-sin, cos]])
    order = np.arange(2 * PS).reshape(2, 3, 128).transpose(1, 0, 2).reshape(-1)
    return forward[:, order]


def lane_parts(column):
    block = column // 128
    return block, column - block * 128


def center_of(positions, row, col, slot):
    at = (row * PMAX + slot) * 2
    return positions[at, col], positions[at + 1, col]


def rolled_out(blocks, shift, lanes):
    turned = [pltpu.roll(b, shift, axis=1) for b in blocks]
    keep = lanes >= shift
    zero = jnp.zeros_like(turned[0])
    return [
        jnp.where(keep, turned[0], zero),
        jnp.where(keep, turned[1], turned[0]),
        jnp.where(keep, turned[2], turned[1]),
        jnp.where(keep, zero, turned[2]),
    ]


def rolled_in(blocks, shift, lanes):
    turned = [pltpu.roll(b, (128 - shift) % 128, axis=1) for b in blocks]
    keep = lanes < 128 - shift
    return [jnp.where(keep, turned[k], turned[k + 1]) for k in range(3)]


def illumination_kernel(positions, counts, probe, out, canvas, power):
    my_row, my_col = lax.axis_index("row"), lax.axis_index("col")
    for j in range(3):
        cols = pl.ds(j * 128, 128)
        power[j] = probe[0, :, cols] * probe[0, :, cols] + probe[1, :, cols] * probe[1, :, cols]
    first, last = PS // 128, (PS + TW) // 128
    for j in range(first, last):
        canvas[j, pl.ds(PS, TH), :] = jnp.zeros((TH, 128), F32)
    lanes = lax.broadcasted_iota(jnp.int32, (BAND, 128), 1)
    grid_r, grid_c = 8, 32

    def tile(k, carry):
        down, across = k // 3 - 1, k % 3 - 1
        row, col = my_row + down, my_col + across
        inside = (row >= 0) & (row < grid_r) & (col >= 0) & (col < grid_c)
        row, col = jnp.where(inside, row, 0), jnp.where(inside, col, 0)
        count = jnp.where(inside, counts[row, col], 0)

        def slot(s, inner):
            top, left = center_of(positions, row, col, s)
            top = top + down * TH - HALF + PS
            left = left + across * TW - HALF + PS
            meets = (top > 0) & (top < PS + TH) & (left > 0) & (left < PS + TW)

            @pl.when(meets)
            def _():
                block, shift = lane_parts(left)
                low = jnp.maximum(PS - top, 0) // BAND
                high = (jnp.minimum(PS + TH - top, PS) + BAND - 1) // BAND

                def band(c, deep):
                    rows = pl.ds(pl.multiple_of(c * BAND, BAND), BAND)
                    parts = rolled_out([power[j, rows, :] for j in range(3)], shift, lanes)
                    for j in range(4):
                        canvas[block + j, pl.ds(top + c * BAND, BAND), :] += parts[j]
                    return deep

                lax.fori_loop(low, high, band, 0)

            return inner

        return lax.fori_loop(0, count, slot, carry)

    lax.fori_loop(0, 9, tile, 0)
    floor = OBJECT_REG * jnp.max(power[...])
    for j in range(TW // 128):
        out[:, pl.ds(j * 128, 128)] = 1.0 / (canvas[first + j, pl.ds(PS, TH), :] + floor)


def main_kernel(
    positions, counts, center, across_in, above_in, below_in, before_in, after_in,
    corners_before_in, corners_after_in, probe_in, intensity_in, forward_in,
    field, rim_before, rim_after, rim_above, rim_below, kept, given,
    extended, total, wave, halfway, residual, returning, turned, window, probe_sum,
    probe, intensity, forward, adjoint, above, below, before, after, corners_before, corners_after,
    copied, slot_copied,
):
    my_row, my_col = lax.axis_index("row"), lax.axis_index("col")
    count = counts[my_row, my_col]

    def inward(s):
        return pltpu.make_async_copy(intensity_in.at[s], intensity.at[s], slot_copied.at[s])

    pairs = [(before_in, before), (after_in, after)]
    pairs += [(corners_before_in, corners_before), (corners_after_in, corners_after)]
    pairs += [(probe_in, probe), (forward_in, forward)]
    for p in range(2):
        for j in range(4):
            pairs.append((center.at[p, :, pl.ds(j * 128, 128)], extended.at[p, j + 2, pl.ds(HALF, TH), :]))
    copies = [pltpu.make_async_copy(a, b, copied.at[k]) for k, (a, b) in enumerate(pairs)]
    rims = ((above_in, above, my_row == EDGE), (below_in, below, my_row == EDGE - 1))
    for k, (rim_in, rim, from_across) in enumerate(rims):
        near = pltpu.make_async_copy(rim_in, rim, copied.at[14 + k])
        pl.when(from_across)(pltpu.make_async_copy(across_in, rim, copied.at[14 + k]).start)
        pl.when(jnp.logical_not(from_across))(near.start)
        copies.insert(0, near)
    for copy in copies[2:]:
        copy.start()
    lax.fori_loop(0, count, lambda s, carry: (inward(s).start(), carry)[1], 0)
    total[...] = jnp.zeros_like(total)
    probe_sum[...] = jnp.zeros_like(probe_sum)
    for copy in copies[:6]:
        copy.wait()
    for p in range(2):
        for j in range(2, 6):
            cols = pl.ds((j - 2) * 128, 128)
            extended[p, j, pl.ds(0, HALF), :] = above[p, :, cols].astype(F32)
            extended[p, j, pl.ds(HALF + TH, HALF), :] = below[p, :, cols].astype(F32)
        for middle, corners, whole, part in ((before, corners_before, 1, 0), (after, corners_after, 6, 7)):
            extended[p, whole, pl.ds(0, HALF), :] = corners[p, pl.ds(0, HALF), :].astype(F32)
            extended[p, whole, pl.ds(HALF, TH), :] = middle[p, pl.ds(0, TH), :].astype(F32)
            extended[p, whole, pl.ds(HALF + TH, HALF), :] = corners[p, pl.ds(HALF, HALF), :].astype(F32)
            for piece, rows, top, low in ((corners, HALF, 0, HALF + TH), (middle, TH // 2, HALF, HALF + TH // 2)):
                found = piece[p, pl.ds(2 * rows, rows), :].astype(F32)
                turned_half = pltpu.roll(found, 64, axis=1)
                extended[p, part, pl.ds(top, rows), :] = found if part else turned_half
                extended[p, part, pl.ds(low, rows), :] = turned_half if part else found
    for copy in copies[6:]:
        copy.wait()
    for k in range(2):
        for j in range(6):
            here = (pl.ds(k * PS, PS), pl.ds(j * 128, 128))
            adjoint[here] = forward[here] if k == j % 2 else -forward[here]

    def place_of(s):
        top, left = center_of(positions, my_row, my_col, s)
        return (top,) + lane_parts(left + 64)

    def leave(s, k):
        top, block, shift = place_of(s)
        lanes = lax.broadcasted_iota(jnp.int32, (PART, 128), 1)
        for at in range(k * 128, (k + 1) * 128, PART):
            rows = pl.ds(at, PART)
            cells = []
            for p in range(2):
                found = [extended[p, block + j, pl.ds(top + at, PART), :] for j in range(4)]
                cells.append(jnp.concatenate(rolled_in(found, shift, lanes), axis=1))
                window[s % 2, p, rows, :] = cells[p]
            pr, pi = probe[0, rows, :], probe[1, rows, :]
            wave[pl.ds(k * 128 + at, PART), :] = (pr * cells[0] - pi * cells[1]).astype(BF16)
            wave[pl.ds(k * 128 + at + 128, PART), :] = (pr * cells[1] + pi * cells[0]).astype(BF16)

    for k in range(3):
        leave(0, k)

    def slot(s, carry):
        top, block, shift = place_of(s)
        half = jnp.dot(adjoint[...], wave[...], preferred_element_type=F32).astype(BF16)
        halfway[:, pl.ds(0, PS)] = half[:PS]
        halfway[:, pl.ds(PS, PS)] = half[PS:]
        inward(s).wait()
        for j in range(3):
            cols = pl.ds(j * 128, 128)
            far = jnp.dot(halfway[...], forward[:, pl.ds(j * 256, 256)], preferred_element_type=F32)
            far_r, far_i = far[:, :128], far[:, 128:]
            misfit = far_r * far_r + far_i * far_i - intensity[s, :, cols].astype(F32)
            real, imaginary = (misfit * far_r).astype(BF16), (misfit * far_i).astype(BF16)
            for k in range(3):
                residual[pl.ds(k * 256, 128), cols] = real[k * 128 : (k + 1) * 128]
                residual[pl.ds(k * 256 + 128, 128), cols] = imaginary[k * 128 : (k + 1) * 128]
            leave(jnp.minimum(s + 1, count - 1), j)
        back = jnp.dot(forward[...], residual[...], preferred_element_type=F32).astype(BF16)
        returning[:, pl.ds(0, PS)] = back[:PS]
        returning[:, pl.ds(PS, PS)] = back[PS:]
        lanes = lax.broadcasted_iota(jnp.int32, (PART, 128), 1)
        for j in range(3):
            cols = pl.ds(j * 128, 128)
            gradient = jnp.dot(returning[...], adjoint[:, pl.ds(j * 256, 256)], preferred_element_type=F32)
            for k in range(PS // PART):
                rows = pl.ds(k * PART, PART)
                gr, gi = gradient[k * PART : (k + 1) * PART, :128], gradient[k * PART : (k + 1) * PART, 128:]
                pr, pi = probe[0, rows, cols], probe[1, rows, cols]
                wr, wi = window[s % 2, 0, rows, cols], window[s % 2, 1, rows, cols]
                for p, term in ((0, pr * gr + pi * gi), (1, pr * gi - pi * gr)):
                    term = pltpu.roll(term, shift, axis=1)
                    past = turned[p, rows, :] if j else jnp.zeros_like(term)
                    total[p, block + j, pl.ds(top + k * PART, PART), :] += jnp.where(lanes >= shift, term, past)
                    if j < 2:
                        turned[p, rows, :] = term
                    else:
                        total[p, block + 3, pl.ds(top + k * PART, PART), :] += jnp.where(lanes < shift, term, 0.0)
                probe_sum[0, rows, cols] += wr * gr + wi * gi
                probe_sum[1, rows, cols] += wr * gi - wi * gr
                probe_sum[2, rows, cols] += wr * wr + wi * wi
        return carry

    lax.fori_loop(0, count, slot, 0)
    pairs = []
    for p in range(2):
        for j in range(4):
            cols = pl.ds(j * 128, 128)
            pairs.append((total.at[p, j + 2, pl.ds(HALF, TH), :], field.at[p, :, cols]))
    copies = [pltpu.make_async_copy(a, b, copied.at[k]) for k, (a, b) in enumerate(pairs)]
    for copy in copies:
        copy.start()
    lanes = lax.broadcasted_iota(jnp.int32, (EH // 2, 128), 1)
    for p in range(2):
        for j in range(2, 6):
            cols = pl.ds((j - 2) * 128, 128)
            rim_above[p, :, cols] = total[p, j, pl.ds(0, HALF), :].astype(BF16)
            rim_below[p, :, cols] = total[p, j, pl.ds(HALF + TH, HALF), :].astype(BF16)
        for rim, whole, part in ((rim_before, 1, 0), (rim_after, 6, 7)):
            rim[p, pl.ds(0, EH), :] = total[p, whole].astype(BF16)
            upper, lower = total[p, part, pl.ds(0, EH // 2), :], total[p, part, pl.ds(EH // 2, EH // 2), :]
            if part:
                lower = pltpu.roll(lower, 64, axis=1)
            else:
                upper = pltpu.roll(upper, 64, axis=1)
            rim[p, pl.ds(EH, EH // 2), :] = jnp.where(lanes < 64, upper, lower).astype(BF16)
    for core in range(2):

        @pl.when(my_col % 2 == core)
        def _():
            for ref, half, kind in ((kept, core, BF16), (given, 1 - core, BF16)):
                for at in range(BLOCKS):
                    if at < USED:
                        found = half * USED + at
                        p, k, j = found // 72, found // 3 % 24, found % 3
                        ref[at] = probe_sum[p, pl.ds(k * 16, 16), pl.ds(j * 128, 128)].astype(kind)
                    else:
                        ref[at] = jnp.zeros((16, 128), kind)

    for copy in copies:
        copy.wait()


def total_kernel(pieces, out):
    total = pieces[0].astype(F32)
    for k in range(1, pieces.shape[0]):
        total = total + pieces[k].astype(F32)
    for k in range(out.shape[0]):
        out[k] = total.astype(BF16)


def cut_kernel(cells, out, piece, copied):
    first = jnp.where(lax.axis_index("row") == EDGE, 0, TH - HALF)
    copy = pltpu.make_async_copy(cells.at[:, pl.ds(pl.multiple_of(first, 64), HALF), :], piece, copied)
    copy.start()
    copy.wait()
    out[...] = piece[...].astype(BF16)


def beside(upper, lower, from_upper_lanes):
    lanes = lax.broadcasted_iota(jnp.int32, upper.shape, 1)
    if from_upper_lanes:
        return jnp.where(lanes < 64, pltpu.roll(upper, 64, axis=1), lower)
    return jnp.where(lanes < 64, upper, pltpu.roll(lower, 64, axis=1))


def pieces_kernel(cells, head, tail, last, first):
    half = TH // 2
    for p in range(2):
        head[p] = cells[p, pl.ds(0, HALF), :].astype(BF16)
        tail[p] = cells[p, pl.ds(TH - HALF, HALF), :].astype(BF16)
        for out, whole, part in ((last, 384, 256), (first, 0, 128)):
            out[p, pl.ds(0, TH), :] = cells[p, :, pl.ds(whole, 128)].astype(BF16)
            upper, lower = cells[p, pl.ds(0, half), pl.ds(part, 128)], cells[p, pl.ds(half, half), pl.ds(part, 128)]
            out[p, pl.ds(TH, half), :] = beside(upper, lower, part == 256).astype(BF16)


def corners_kernel(across, above, below, last, first):
    my_row = lax.axis_index("row")
    for p in range(2):
        for out, whole, part in ((last, 384, 256), (first, 0, 128)):

            def block(at):
                cols = pl.ds(at, 128)
                far = across[p, :, cols].astype(F32)
                top = jnp.where(my_row == EDGE, far, above[p, :, cols].astype(F32))
                return top, jnp.where(my_row == EDGE - 1, far, below[p, :, cols].astype(F32))

            top, bottom = block(whole)
            out[p, pl.ds(0, HALF), :] = top.astype(BF16)
            out[p, pl.ds(HALF, HALF), :] = bottom.astype(BF16)
            out[p, pl.ds(2 * HALF, HALF), :] = beside(*block(part), part == 256).astype(BF16)


def merge_kernel(from_before, from_after, rim_above, rim_below, swap, up, down):
    my_row = lax.axis_index("row")
    lanes = lax.broadcasted_iota(jnp.int32, (HALF, 128), 1)
    for p in range(2):
        sums = []
        for rim, rows, halves, lower in (
            (rim_above, pl.ds(0, HALF), pl.ds(EH, HALF), False),
            (rim_below, pl.ds(EH - HALF, HALF), pl.ds(EH * 3 // 2 - HALF, HALF), True),
        ):
            left, right = from_before[p, halves, :].astype(F32), from_after[p, halves, :].astype(F32)
            if lower:
                left = pltpu.roll(left, 64, axis=1)
            else:
                right = pltpu.roll(right, 64, axis=1)
            blocks = [
                from_before[p, rows, :].astype(F32),
                jnp.where(lanes < 64, left, 0.0),
                jnp.where(lanes >= 64, right, 0.0),
                from_after[p, rows, :].astype(F32),
            ]
            sums.append(rim[p].astype(F32) + jnp.concatenate(blocks, axis=1))
        up[p] = sums[0].astype(BF16)
        down[p] = sums[1].astype(BF16)
        swap[p] = jnp.where(my_row == EDGE, sums[0], sums[1]).astype(BF16)


def object_kernel(center, field, from_before, from_after, weight, earlier, out):
    del earlier
    lanes = lax.broadcasted_iota(jnp.int32, (64, 128), 1)
    for k in range(TH // 64):
        rows = pl.ds(k * 64, 64)
        outer = pl.ds(HALF + k * 64, 64)
        upper = HALF + k * 64 < EH // 2
        halves = pl.ds(EH + (HALF + k * 64) % (EH // 2), 64)
        for p in range(2):
            left, right = from_before[p, halves, :].astype(F32), from_after[p, halves, :].astype(F32)
            if upper:
                right = pltpu.roll(right, 64, axis=1)
            else:
                left = pltpu.roll(left, 64, axis=1)
            sides = [
                from_before[p, outer, :].astype(F32),
                jnp.where(lanes < 64, left, 0.0),
                jnp.where(lanes >= 64, right, 0.0),
                from_after[p, outer, :].astype(F32),
            ]
            cells = field[p, rows, :] + jnp.concatenate(sides, axis=1)
            out[p, rows, :] = center[p, rows, :] - cells * weight[rows, :]


def rims_kernel(base, weight_in, across, from_above, from_below, out, cells, weight, arrived, left):
    my_row = lax.axis_index("row")
    places = (pl.ds(0, HALF), pl.ds(TH - HALF, HALF))
    inward, outward = [], []
    for k, rows in enumerate(places):
        inward.append(pltpu.make_async_copy(base.at[:, rows, :], cells.at[k], arrived.at[k]))
        inward.append(pltpu.make_async_copy(weight_in.at[rows, :], weight.at[k], arrived.at[2 + k]))
        outward.append(pltpu.make_async_copy(cells.at[k], out.at[:, rows, :], left.at[k]))
    for copy in inward:
        copy.start()
    for k, (near, edge) in enumerate(((from_above, EDGE), (from_below, EDGE - 1))):
        inward[2 * k].wait()
        inward[2 * k + 1].wait()
        for p in range(2):
            rim = jnp.where(my_row == edge, across[p].astype(F32), near[p].astype(F32))
            cells[k, p] = cells[k, p] - rim * weight[k]
        outward[k].start()
    for copy in outward:
        copy.wait()


def probe_kernel(half, other, probe, out, sums, planes):
    core = lax.axis_index("col") % 2
    sums[core] = half[...]
    sums[1 - core] = other[...]
    for found in range(2 * USED):
        p, k, j = found // 72, found // 3 % 24, found % 3
        planes[p, pl.ds(k * 16, 16), pl.ds(j * 128, 128)] = sums[found // USED, found % USED].astype(F32)
    floor = PROBE_REG * jnp.max(planes[2])
    square = jnp.zeros((STEP, PS), F32)
    for k in range(PS // STEP):
        rows = pl.ds(k * STEP, STEP)
        weight = 1.0 / (planes[2, rows, :] + floor)
        for p in range(2):
            direction = planes[p, rows, :] * weight
            planes[p, rows, :] = direction
            square = square + direction * direction
    spread = jnp.sqrt(jnp.sum(square) / (PS * PS) + EPSILON)
    for p in range(2):
        out[p] = probe[p] - PROBE_RATE * planes[p] / spread


SMEM = pl.BlockSpec(memory_space=pltpu.SMEM)
VMEM = pl.BlockSpec(memory_space=pltpu.VMEM)
ANY = pl.BlockSpec(memory_space=pl.ANY)


def params(mib):
    return pltpu.CompilerParams(vmem_limit_bytes=mib << 20)


def shifted(value, axis, step):
    size = lax.axis_size(axis)
    low, high = max(0, -step), min(size, size - step)
    return lax.ppermute(value, axis, [(k, k + step) for k in range(low, high)])


def slots_call(*arrays):
    like = jax.ShapeDtypeStruct
    forward = dft_blocks()
    return pl.pallas_call(
        main_kernel,
        out_shape=(
            like((2, TH, TW), F32),
            like((2, EH * 3 // 2, 128), BF16),
            like((2, EH * 3 // 2, 128), BF16),
            like((2, HALF, TW), BF16),
            like((2, HALF, TW), BF16),
            like((BLOCKS, 16, 128), BF16),
            like((BLOCKS, 16, 128), BF16),
        ),
        in_specs=[SMEM] * 2 + [ANY] * 11,
        out_specs=(ANY,) + (VMEM,) * 6,
        scratch_shapes=[
            pltpu.VMEM((2, EW // 128, EH, 128), F32),
            pltpu.VMEM((2, EW // 128, EH, 128), F32),
            pltpu.VMEM((2 * PS, PS), BF16),
            pltpu.VMEM((PS, 2 * PS), BF16),
            pltpu.VMEM((2 * PS, PS), BF16),
            pltpu.VMEM((PS, 2 * PS), BF16),
            pltpu.VMEM((2, PS, 128), F32),
            pltpu.VMEM((2, 2, PS, PS), F32),
            pltpu.VMEM((3, PS, PS), F32),
            pltpu.VMEM((2, PS, PS), F32),
            pltpu.VMEM((PMAX, PS, PS), BF16),
            pltpu.VMEM((2 * PS, 2 * PS), BF16),
            pltpu.VMEM((2 * PS, 2 * PS), BF16),
            pltpu.VMEM((2, HALF, TW), BF16),
            pltpu.VMEM((2, HALF, TW), BF16),
            pltpu.VMEM((2, TH * 3 // 2, 128), BF16),
            pltpu.VMEM((2, TH * 3 // 2, 128), BF16),
            pltpu.VMEM((2, PS * 3 // 2, 128), BF16),
            pltpu.VMEM((2, PS * 3 // 2, 128), BF16),
            pltpu.SemaphoreType.DMA((16,)),
            pltpu.SemaphoreType.DMA((PMAX,)),
        ],
        compiler_params=params(60),
        name="slots",
    )(*arrays, jnp.asarray(forward))


def across_edge(value):
    return lax.ppermute(value, "row", [(EDGE - 1, EDGE), (EDGE, EDGE - 1)])


def within_halves(value, step):
    rows = [k for k in range(lax.axis_size("row")) if k // EDGE == (k + step) // EDGE]
    return lax.ppermute(value, "row", [(k, k + step) for k in rows])


def on_device(object_field, probe_field, intensities, positions, tile_counts):
    like = jax.ShapeDtypeStruct
    my_row = lax.axis_index("row")
    where = positions.transpose(0, 2, 3, 1).reshape(-1, positions.shape[1])
    piece = pl.pallas_call(
        cut_kernel,
        out_shape=like((2, HALF, TW), BF16),
        in_specs=[ANY],
        out_specs=VMEM,
        scratch_shapes=[pltpu.VMEM((2, HALF, TW), F32), pltpu.SemaphoreType.DMA],
        compiler_params=params(60),
        cost_estimate=pl.CostEstimate(flops=400_000, bytes_accessed=1_200_000, transcendentals=0),
        name="cut",
    )(object_field)
    across = across_edge(piece)
    strip = like((2, TH * 3 // 2, 128), BF16)
    piece, object_cells = lax.optimization_barrier((piece, object_field))
    head, tail, last, first = pl.pallas_call(
        pieces_kernel,
        out_shape=(like((2, HALF, TW), BF16),) * 2 + (strip,) * 2,
        in_specs=[VMEM],
        out_specs=(VMEM,) * 4,
        compiler_params=params(60),
        cost_estimate=pl.CostEstimate(flops=2_000_000, bytes_accessed=4_000_000, transcendentals=0),
        name="pieces",
    )(object_cells)
    above = within_halves(tail, 1)
    below = within_halves(head, -1)
    before = shifted(last, "col", 1)
    after = shifted(first, "col", -1)
    weight = pl.pallas_call(
        illumination_kernel,
        out_shape=like((TH, TW), F32),
        in_specs=[SMEM, SMEM, VMEM],
        out_specs=VMEM,
        scratch_shapes=[pltpu.VMEM((CANVAS // 128, CANVAS, 128), F32), pltpu.VMEM((3, PS, 128), F32)],
        compiler_params=params(60),
        cost_estimate=pl.CostEstimate(flops=20_000_000, bytes_accessed=20_000_000, transcendentals=0),
        name="illumination",
    )(where, tile_counts, probe_field)
    across, above, below, weight = lax.optimization_barrier((across, above, below, weight))
    last, first = pl.pallas_call(
        corners_kernel,
        out_shape=(like((2, PS * 3 // 2, 128), BF16),) * 2,
        in_specs=[VMEM] * 3,
        out_specs=(VMEM,) * 2,
        compiler_params=params(16),
        cost_estimate=pl.CostEstimate(flops=1_000_000, bytes_accessed=2_000_000, transcendentals=0),
        name="corners",
    )(across, above, below)
    corners_before = shifted(last, "col", 1)
    corners_after = shifted(first, "col", -1)
    field, rim_before, rim_after, rim_above, rim_below, kept, given = slots_call(
        where, tile_counts, object_field, across, above, below, before, after,
        corners_before, corners_after, probe_field, intensities.reshape(PMAX, PS, PS),
    )
    cols, rows = lax.axis_size("col"), lax.axis_size("row")
    device = np.arange(rows * cols).reshape(2, 4, 4, 4, 2)
    plane = device.transpose(0, 2, 4, 1, 3).reshape(-1, 16).tolist()
    line = device.transpose(1, 3, 4, 0, 2).reshape(-1, 8).tolist()
    partner = [(k, k ^ 1) for k in range(cols)]

    def exchanged(pieces, groups):
        return lax.all_to_all(pieces, ("row", "col"), 0, 0, axis_index_groups=groups)

    def total_of(pieces, times, flops):
        return pl.pallas_call(
            total_kernel,
            out_shape=like((times,) + pieces.shape[1:], BF16),
            in_specs=[VMEM],
            out_specs=VMEM,
            compiler_params=params(8),
            cost_estimate=pl.CostEstimate(flops=flops, bytes_accessed=0, transcendentals=0),
            name="total",
        )(pieces)

    arrived = lax.ppermute(given, "col", partner)
    mine = (kept.astype(F32) + arrived.astype(F32)).astype(BF16)
    mine, rim_before, rim_after = lax.optimization_barrier((mine, rim_before, rim_after))
    from_before = shifted(rim_after, "col", 1)
    from_after = shifted(rim_before, "col", -1)
    parts = exchanged(mine.reshape(16, -1, 16, 128), plane)
    sums = total_of(parts, 8, 10_000_000_000)
    parts = exchanged(sums, line)
    swap, up, down = pl.pallas_call(
        merge_kernel,
        out_shape=(like((2, HALF, TW), BF16),) * 3,
        in_specs=[VMEM] * 4,
        out_specs=(VMEM,) * 3,
        compiler_params=params(24),
        cost_estimate=pl.CostEstimate(flops=1_000_000, bytes_accessed=2_000_000, transcendentals=0),
        name="merge",
    )(from_before, from_after, rim_above, rim_below)
    across = across_edge(swap)
    from_below = within_halves(up, -1)
    from_above = within_halves(down, 1)
    sums = total_of(parts, 16, 1_000_000_000)
    half = exchanged(sums, plane).reshape(BLOCKS, 16, 128)
    new_object = pl.pallas_call(
        object_kernel,
        out_shape=like((2, TH, TW), F32),
        in_specs=[VMEM] * 5 + [ANY],
        out_specs=VMEM,
        compiler_params=params(60),
        cost_estimate=pl.CostEstimate(flops=4_000_000, bytes_accessed=12_000_000, transcendentals=0),
        name="new_object",
    )(object_field, field, from_before, from_after, weight, sums)
    new_object = pl.pallas_call(
        rims_kernel,
        out_shape=like((2, TH, TW), F32),
        in_specs=[ANY, ANY, VMEM, VMEM, VMEM],
        out_specs=ANY,
        scratch_shapes=[
            pltpu.VMEM((2, 2, HALF, TW), F32),
            pltpu.VMEM((2, HALF, TW), F32),
            pltpu.SemaphoreType.DMA((4,)),
            pltpu.SemaphoreType.DMA((2,)),
        ],
        input_output_aliases={0: 0},
        compiler_params=params(16),
        cost_estimate=pl.CostEstimate(flops=40_000_000_000, bytes_accessed=4_000_000, transcendentals=0),
        name="rims",
    )(new_object, weight, across, from_above, from_below)
    half, new_object = lax.optimization_barrier((half, new_object))
    other = lax.ppermute(half, "col", partner)
    new_probe = pl.pallas_call(
        probe_kernel,
        out_shape=like((2, PS, PS), F32),
        in_specs=[VMEM] * 3,
        out_specs=VMEM,
        scratch_shapes=[pltpu.VMEM((2, BLOCKS, 16, 128), BF16), pltpu.VMEM((3, PS, PS), F32)],
        compiler_params=params(24),
        name="new_probe",
    )(half, other, probe_field)
    return (new_object, new_probe)


def solution(mesh):
    placed = (P(None, "row", "col"), P(), P("row", "col", None, None, None), P(), P())
    return jax.shard_map(
        on_device,
        mesh=mesh,
        in_specs=placed,
        out_specs=(P(None, "row", "col"), P()),
        check_vma=False,
    )
```

```python
import functools

import jax
import jax.numpy as jnp
import ml_dtypes
import numpy as np
from jax import lax
from jax.experimental import pallas as pl
from jax.experimental.pallas import tpu as pltpu
from jax.sharding import PartitionSpec as P

OBJECT_REG = 0.1
PROBE_REG = 0.1
PROBE_RATE = 0.5
EPSILON = 1e-06

PS = 384
HALF = 192
TH = 512
TW = 512
PMAX = 6
EH = TH + PS
EW = TW + 512
CANVAS = 1280
USED = 108
BLOCKS = 112
STEP = 128
BAND = 96
PART = 64
EDGE = 4
F32 = jnp.float32
BF16 = jnp.bfloat16


def dft_blocks():
    index = np.arange(PS)
    product = (index[:, None] * index[None, :]) % PS
    angles = product.astype(np.float32) * np.float32(2.0 * np.pi / PS)
    norm = np.float32(1.0) / np.sqrt(np.float32(PS))
    cos = (np.cos(angles) * norm).astype(ml_dtypes.bfloat16)
    sin = (-np.sin(angles) * norm).astype(ml_dtypes.bfloat16)
    forward = np.block([[cos, sin], [-sin, cos]])
    order = np.arange(2 * PS).reshape(2, 3, 128).transpose(1, 0, 2).reshape(-1)
    return forward[:, order]


def lane_parts(column):
    block = column // 128
    return block, column - block * 128


def center_of(positions, row, col, slot):
    at = (row * PMAX + slot) * 2
    return positions[at, col], positions[at + 1, col]


def rolled_out(blocks, shift, lanes):
    turned = [pltpu.roll(b, shift, axis=1) for b in blocks]
    keep = lanes >= shift
    zero = jnp.zeros_like(turned[0])
    return [
        jnp.where(keep, turned[0], zero),
        jnp.where(keep, turned[1], turned[0]),
        jnp.where(keep, turned[2], turned[1]),
        jnp.where(keep, zero, turned[2]),
    ]


def rolled_in(blocks, shift, lanes):
    turned = [pltpu.roll(b, (128 - shift) % 128, axis=1) for b in blocks]
    keep = lanes < 128 - shift
    return [jnp.where(keep, turned[k], turned[k + 1]) for k in range(3)]


def power_kernel(probe, power):
    for j in range(3):
        cols = pl.ds(j * 128, 128)
        power[j] = probe[0, :, cols] * probe[0, :, cols] + probe[1, :, cols] * probe[1, :, cols]


def illumination_kernel(positions, counts, power, earlier, out, canvas):
    del earlier
    my_row, my_col = lax.axis_index("row"), lax.axis_index("col")
    first, last = PS // 128, (PS + TW) // 128
    for j in range(first, last):
        canvas[j, pl.ds(PS, TH), :] = jnp.zeros((TH, 128), F32)
    lanes = lax.broadcasted_iota(jnp.int32, (BAND, 128), 1)
    grid_r, grid_c = 8, 32

    def tile(k, carry):
        down, across = k // 3 - 1, k % 3 - 1
        row, col = my_row + down, my_col + across
        inside = (row >= 0) & (row < grid_r) & (col >= 0) & (col < grid_c)
        row, col = jnp.where(inside, row, 0), jnp.where(inside, col, 0)
        count = jnp.where(inside, counts[row, col], 0)

        def slot(s, inner):
            top, left = center_of(positions, row, col, s)
            top = top + down * TH - HALF + PS
            left = left + across * TW - HALF + PS
            meets = (top > 0) & (top < PS + TH) & (left > 0) & (left < PS + TW)

            @pl.when(meets)
            def _():
                block, shift = lane_parts(left)
                low = jnp.maximum(PS - top, 0) // BAND
                high = (jnp.minimum(PS + TH - top, PS) + BAND - 1) // BAND

                def band(c, deep):
                    rows = pl.ds(pl.multiple_of(c * BAND, BAND), BAND)
                    parts = rolled_out([power[j, rows, :] for j in range(3)], shift, lanes)
                    for j in range(4):
                        canvas[block + j, pl.ds(top + c * BAND, BAND), :] += parts[j]
                    return deep

                lax.fori_loop(low, high, band, 0)

            return inner

        return lax.fori_loop(0, count, slot, carry)

    lax.fori_loop(0, 9, tile, 0)
    floor = OBJECT_REG * jnp.max(power[...])
    for j in range(TW // 128):
        out[:, pl.ds(j * 128, 128)] = 1.0 / (canvas[first + j, pl.ds(PS, TH), :] + floor)


def main_kernel(
    positions, counts, center, across_in, above_in, below_in, before_in, after_in,
    corners_before_in, corners_after_in, probe_in, intensity_in, forward_in,
    field, rim_before, rim_after, rim_above, rim_below, kept, given,
    extended, total, wave, halfway, residual, returning, turned, window, probe_sum,
    probe, intensity, forward, adjoint, above, below, before, after, corners_before, corners_after,
    copied, slot_copied,
):
    my_row, my_col = lax.axis_index("row"), lax.axis_index("col")
    count = counts[my_row, my_col]

    def inward(s):
        return pltpu.make_async_copy(intensity_in.at[s], intensity.at[s], slot_copied.at[s])

    pairs = [(before_in, before), (after_in, after)]
    pairs += [(corners_before_in, corners_before), (corners_after_in, corners_after)]
    pairs += [(probe_in, probe), (forward_in, forward)]
    for p in range(2):
        for j in range(4):
            pairs.append((center.at[p, :, pl.ds(j * 128, 128)], extended.at[p, j + 2, pl.ds(HALF, TH), :]))
    copies = [pltpu.make_async_copy(a, b, copied.at[k]) for k, (a, b) in enumerate(pairs)]
    rims = ((above_in, above, my_row == EDGE), (below_in, below, my_row == EDGE - 1))
    for k, (rim_in, rim, from_across) in enumerate(rims):
        near = pltpu.make_async_copy(rim_in, rim, copied.at[14 + k])
        pl.when(from_across)(pltpu.make_async_copy(across_in, rim, copied.at[14 + k]).start)
        pl.when(jnp.logical_not(from_across))(near.start)
        copies.insert(0, near)
    for copy in copies[2:]:
        copy.start()
    lax.fori_loop(0, count, lambda s, carry: (inward(s).start(), carry)[1], 0)
    total[...] = jnp.zeros_like(total)
    probe_sum[...] = jnp.zeros_like(probe_sum)
    for copy in copies[:6]:
        copy.wait()
    for p in range(2):
        for j in range(2, 6):
            cols = pl.ds((j - 2) * 128, 128)
            extended[p, j, pl.ds(0, HALF), :] = above[p, :, cols].astype(F32)
            extended[p, j, pl.ds(HALF + TH, HALF), :] = below[p, :, cols].astype(F32)
        for middle, corners, whole, part in ((before, corners_before, 1, 0), (after, corners_after, 6, 7)):
            extended[p, whole, pl.ds(0, HALF), :] = corners[p, pl.ds(0, HALF), :].astype(F32)
            extended[p, whole, pl.ds(HALF, TH), :] = middle[p, pl.ds(0, TH), :].astype(F32)
            extended[p, whole, pl.ds(HALF + TH, HALF), :] = corners[p, pl.ds(HALF, HALF), :].astype(F32)
            for piece, rows, top, low in ((corners, HALF, 0, HALF + TH), (middle, TH // 2, HALF, HALF + TH // 2)):
                found = piece[p, pl.ds(2 * rows, rows), :].astype(F32)
                turned_half = pltpu.roll(found, 64, axis=1)
                extended[p, part, pl.ds(top, rows), :] = found if part else turned_half
                extended[p, part, pl.ds(low, rows), :] = turned_half if part else found
    for copy in copies[6:]:
        copy.wait()
    for k in range(2):
        for j in range(6):
            here = (pl.ds(k * PS, PS), pl.ds(j * 128, 128))
            adjoint[here] = forward[here] if k == j % 2 else -forward[here]

    def place_of(s):
        top, left = center_of(positions, my_row, my_col, s)
        return (top,) + lane_parts(left + 64)

    def leave(s, k):
        top, block, shift = place_of(s)
        lanes = lax.broadcasted_iota(jnp.int32, (PART, 128), 1)
        for at in range(k * 128, (k + 1) * 128, PART):
            rows = pl.ds(at, PART)
            cells = []
            for p in range(2):
                found = [extended[p, block + j, pl.ds(top + at, PART), :] for j in range(4)]
                cells.append(jnp.concatenate(rolled_in(found, shift, lanes), axis=1))
                window[s % 2, p, rows, :] = cells[p]
            pr, pi = probe[0, rows, :], probe[1, rows, :]
            wave[pl.ds(k * 128 + at, PART), :] = (pr * cells[0] - pi * cells[1]).astype(BF16)
            wave[pl.ds(k * 128 + at + 128, PART), :] = (pr * cells[1] + pi * cells[0]).astype(BF16)

    for k in range(3):
        leave(0, k)

    def slot(s, carry):
        top, block, shift = place_of(s)
        half = jnp.dot(adjoint[...], wave[...], preferred_element_type=F32).astype(BF16)
        halfway[:, pl.ds(0, PS)] = half[:PS]
        halfway[:, pl.ds(PS, PS)] = half[PS:]
        inward(s).wait()
        for j in range(3):
            cols = pl.ds(j * 128, 128)
            far = jnp.dot(halfway[...], forward[:, pl.ds(j * 256, 256)], preferred_element_type=F32)
            far_r, far_i = far[:, :128], far[:, 128:]
            misfit = far_r * far_r + far_i * far_i - intensity[s, :, cols].astype(F32)
            real, imaginary = (misfit * far_r).astype(BF16), (misfit * far_i).astype(BF16)
            for k in range(3):
                residual[pl.ds(k * 256, 128), cols] = real[k * 128 : (k + 1) * 128]
                residual[pl.ds(k * 256 + 128, 128), cols] = imaginary[k * 128 : (k + 1) * 128]
            leave(jnp.minimum(s + 1, count - 1), j)
        back = jnp.dot(forward[...], residual[...], preferred_element_type=F32).astype(BF16)
        returning[:, pl.ds(0, PS)] = back[:PS]
        returning[:, pl.ds(PS, PS)] = back[PS:]
        lanes = lax.broadcasted_iota(jnp.int32, (PART, 128), 1)
        for j in range(3):
            cols = pl.ds(j * 128, 128)
            gradient = jnp.dot(returning[...], adjoint[:, pl.ds(j * 256, 256)], preferred_element_type=F32)
            for k in range(PS // PART):
                rows = pl.ds(k * PART, PART)
                gr, gi = gradient[k * PART : (k + 1) * PART, :128], gradient[k * PART : (k + 1) * PART, 128:]
                pr, pi = probe[0, rows, cols], probe[1, rows, cols]
                wr, wi = window[s % 2, 0, rows, cols], window[s % 2, 1, rows, cols]
                for p, term in ((0, pr * gr + pi * gi), (1, pr * gi - pi * gr)):
                    term = pltpu.roll(term, shift, axis=1)
                    past = turned[p, rows, :] if j else jnp.zeros_like(term)
                    total[p, block + j, pl.ds(top + k * PART, PART), :] += jnp.where(lanes >= shift, term, past)
                    if j < 2:
                        turned[p, rows, :] = term
                    else:
                        total[p, block + 3, pl.ds(top + k * PART, PART), :] += jnp.where(lanes < shift, term, 0.0)
                probe_sum[0, rows, cols] += wr * gr + wi * gi
                probe_sum[1, rows, cols] += wr * gi - wi * gr
                probe_sum[2, rows, cols] += wr * wr + wi * wi
        return carry

    lax.fori_loop(0, count, slot, 0)
    pairs = []
    for p in range(2):
        for j in range(4):
            cols = pl.ds(j * 128, 128)
            pairs.append((total.at[p, j + 2, pl.ds(HALF, TH), :], field.at[p, :, cols]))
    copies = [pltpu.make_async_copy(a, b, copied.at[k]) for k, (a, b) in enumerate(pairs)]
    for copy in copies:
        copy.start()
    lanes = lax.broadcasted_iota(jnp.int32, (EH // 2, 128), 1)
    for p in range(2):
        for j in range(2, 6):
            cols = pl.ds((j - 2) * 128, 128)
            rim_above[p, :, cols] = total[p, j, pl.ds(0, HALF), :].astype(BF16)
            rim_below[p, :, cols] = total[p, j, pl.ds(HALF + TH, HALF), :].astype(BF16)
        for rim, whole, part in ((rim_before, 1, 0), (rim_after, 6, 7)):
            rim[p, pl.ds(0, EH), :] = total[p, whole].astype(BF16)
            upper, lower = total[p, part, pl.ds(0, EH // 2), :], total[p, part, pl.ds(EH // 2, EH // 2), :]
            if part:
                lower = pltpu.roll(lower, 64, axis=1)
            else:
                upper = pltpu.roll(upper, 64, axis=1)
            rim[p, pl.ds(EH, EH // 2), :] = jnp.where(lanes < 64, upper, lower).astype(BF16)
    for core in range(2):

        @pl.when(my_col % 2 == core)
        def _():
            for ref, half, kind in ((kept, core, BF16), (given, 1 - core, BF16)):
                for at in range(BLOCKS):
                    if at < USED:
                        found = half * USED + at
                        p, k, j = found // 72, found // 3 % 24, found % 3
                        ref[at] = probe_sum[p, pl.ds(k * 16, 16), pl.ds(j * 128, 128)].astype(kind)
                    else:
                        ref[at] = jnp.zeros((16, 128), kind)

    for copy in copies:
        copy.wait()


def total_kernel(pieces, out):
    total = pieces[0].astype(F32)
    for k in range(1, pieces.shape[0]):
        total = total + pieces[k].astype(F32)
    for k in range(out.shape[0]):
        out[k] = total.astype(BF16)


def cut_kernel(cells, out, piece, copied):
    first = jnp.where(lax.axis_index("row") == EDGE, 0, TH - HALF)
    copy = pltpu.make_async_copy(cells.at[:, pl.ds(pl.multiple_of(first, 64), HALF), :], piece, copied)
    copy.start()
    copy.wait()
    out[...] = piece[...].astype(BF16)


def beside(upper, lower, from_upper_lanes):
    lanes = lax.broadcasted_iota(jnp.int32, upper.shape, 1)
    if from_upper_lanes:
        return jnp.where(lanes < 64, pltpu.roll(upper, 64, axis=1), lower)
    return jnp.where(lanes < 64, upper, pltpu.roll(lower, 64, axis=1))


def pieces_kernel(cells, head, tail, last, first):
    half = TH // 2
    for p in range(2):
        head[p] = cells[p, pl.ds(0, HALF), :].astype(BF16)
        tail[p] = cells[p, pl.ds(TH - HALF, HALF), :].astype(BF16)
        for out, whole, part in ((last, 384, 256), (first, 0, 128)):
            out[p, pl.ds(0, TH), :] = cells[p, :, pl.ds(whole, 128)].astype(BF16)
            upper, lower = cells[p, pl.ds(0, half), pl.ds(part, 128)], cells[p, pl.ds(half, half), pl.ds(part, 128)]
            out[p, pl.ds(TH, half), :] = beside(upper, lower, part == 256).astype(BF16)


def corners_kernel(across, above, below, last, first):
    my_row = lax.axis_index("row")
    for p in range(2):
        for out, whole, part in ((last, 384, 256), (first, 0, 128)):

            def block(at):
                cols = pl.ds(at, 128)
                far = across[p, :, cols].astype(F32)
                top = jnp.where(my_row == EDGE, far, above[p, :, cols].astype(F32))
                return top, jnp.where(my_row == EDGE - 1, far, below[p, :, cols].astype(F32))

            top, bottom = block(whole)
            out[p, pl.ds(0, HALF), :] = top.astype(BF16)
            out[p, pl.ds(HALF, HALF), :] = bottom.astype(BF16)
            out[p, pl.ds(2 * HALF, HALF), :] = beside(*block(part), part == 256).astype(BF16)


def merge_kernel(from_before, from_after, rim_above, rim_below, swap, up, down):
    my_row = lax.axis_index("row")
    lanes = lax.broadcasted_iota(jnp.int32, (HALF, 128), 1)
    for p in range(2):
        sums = []
        for rim, rows, halves, lower in (
            (rim_above, pl.ds(0, HALF), pl.ds(EH, HALF), False),
            (rim_below, pl.ds(EH - HALF, HALF), pl.ds(EH * 3 // 2 - HALF, HALF), True),
        ):
            left, right = from_before[p, halves, :].astype(F32), from_after[p, halves, :].astype(F32)
            if lower:
                left = pltpu.roll(left, 64, axis=1)
            else:
                right = pltpu.roll(right, 64, axis=1)
            blocks = [
                from_before[p, rows, :].astype(F32),
                jnp.where(lanes < 64, left, 0.0),
                jnp.where(lanes >= 64, right, 0.0),
                from_after[p, rows, :].astype(F32),
            ]
            sums.append(rim[p].astype(F32) + jnp.concatenate(blocks, axis=1))
        up[p] = sums[0].astype(BF16)
        down[p] = sums[1].astype(BF16)
        swap[p] = jnp.where(my_row == EDGE, sums[0], sums[1]).astype(BF16)


def object_kernel(center, field, from_before, from_after, weight, earlier, out):
    del earlier
    lanes = lax.broadcasted_iota(jnp.int32, (64, 128), 1)
    for k in range(TH // 64):
        rows = pl.ds(k * 64, 64)
        outer = pl.ds(HALF + k * 64, 64)
        upper = HALF + k * 64 < EH // 2
        halves = pl.ds(EH + (HALF + k * 64) % (EH // 2), 64)
        for p in range(2):
            left, right = from_before[p, halves, :].astype(F32), from_after[p, halves, :].astype(F32)
            if upper:
                right = pltpu.roll(right, 64, axis=1)
            else:
                left = pltpu.roll(left, 64, axis=1)
            sides = [
                from_before[p, outer, :].astype(F32),
                jnp.where(lanes < 64, left, 0.0),
                jnp.where(lanes >= 64, right, 0.0),
                from_after[p, outer, :].astype(F32),
            ]
            cells = field[p, rows, :] + jnp.concatenate(sides, axis=1)
            out[p, rows, :] = center[p, rows, :] - cells * weight[rows, :]


def rims_kernel(base, weight_in, across, from_above, from_below, out, cells, weight, arrived, left):
    my_row = lax.axis_index("row")
    places = (pl.ds(0, HALF), pl.ds(TH - HALF, HALF))
    inward, outward = [], []
    for k, rows in enumerate(places):
        inward.append(pltpu.make_async_copy(base.at[:, rows, :], cells.at[k], arrived.at[k]))
        inward.append(pltpu.make_async_copy(weight_in.at[rows, :], weight.at[k], arrived.at[2 + k]))
        outward.append(pltpu.make_async_copy(cells.at[k], out.at[:, rows, :], left.at[k]))
    for copy in inward:
        copy.start()
    for k, (near, edge) in enumerate(((from_above, EDGE), (from_below, EDGE - 1))):
        inward[2 * k].wait()
        inward[2 * k + 1].wait()
        for p in range(2):
            rim = jnp.where(my_row == edge, across[p].astype(F32), near[p].astype(F32))
            cells[k, p] = cells[k, p] - rim * weight[k]
        outward[k].start()
    for copy in outward:
        copy.wait()


def probe_kernel(half, other, probe, out, sums, planes):
    core = lax.axis_index("col") % 2
    sums[core] = half[...]
    sums[1 - core] = other[...]
    for found in range(2 * USED):
        p, k, j = found // 72, found // 3 % 24, found % 3
        planes[p, pl.ds(k * 16, 16), pl.ds(j * 128, 128)] = sums[found // USED, found % USED].astype(F32)
    floor = PROBE_REG * jnp.max(planes[2])
    square = jnp.zeros((STEP, PS), F32)
    for k in range(PS // STEP):
        rows = pl.ds(k * STEP, STEP)
        weight = 1.0 / (planes[2, rows, :] + floor)
        for p in range(2):
            direction = planes[p, rows, :] * weight
            planes[p, rows, :] = direction
            square = square + direction * direction
    spread = jnp.sqrt(jnp.sum(square) / (PS * PS) + EPSILON)
    for p in range(2):
        out[p] = probe[p] - PROBE_RATE * planes[p] / spread


SMEM = pl.BlockSpec(memory_space=pltpu.SMEM)
VMEM = pl.BlockSpec(memory_space=pltpu.VMEM)
ANY = pl.BlockSpec(memory_space=pl.ANY)


def params(mib):
    return pltpu.CompilerParams(vmem_limit_bytes=mib << 20)


def shifted(value, axis, step):
    size = lax.axis_size(axis)
    low, high = max(0, -step), min(size, size - step)
    return lax.ppermute(value, axis, [(k, k + step) for k in range(low, high)])


def slots_call(*arrays):
    like = jax.ShapeDtypeStruct
    forward = dft_blocks()
    return pl.pallas_call(
        main_kernel,
        out_shape=(
            like((2, TH, TW), F32),
            like((2, EH * 3 // 2, 128), BF16),
            like((2, EH * 3 // 2, 128), BF16),
            like((2, HALF, TW), BF16),
            like((2, HALF, TW), BF16),
            like((BLOCKS, 16, 128), BF16),
            like((BLOCKS, 16, 128), BF16),
        ),
        in_specs=[SMEM] * 2 + [ANY] * 11,
        out_specs=(ANY,) + (VMEM,) * 6,
        scratch_shapes=[
            pltpu.VMEM((2, EW // 128, EH, 128), F32),
            pltpu.VMEM((2, EW // 128, EH, 128), F32),
            pltpu.VMEM((2 * PS, PS), BF16),
            pltpu.VMEM((PS, 2 * PS), BF16),
            pltpu.VMEM((2 * PS, PS), BF16),
            pltpu.VMEM((PS, 2 * PS), BF16),
            pltpu.VMEM((2, PS, 128), F32),
            pltpu.VMEM((2, 2, PS, PS), F32),
            pltpu.VMEM((3, PS, PS), F32),
            pltpu.VMEM((2, PS, PS), F32),
            pltpu.VMEM((PMAX, PS, PS), BF16),
            pltpu.VMEM((2 * PS, 2 * PS), BF16),
            pltpu.VMEM((2 * PS, 2 * PS), BF16),
            pltpu.VMEM((2, HALF, TW), BF16),
            pltpu.VMEM((2, HALF, TW), BF16),
            pltpu.VMEM((2, TH * 3 // 2, 128), BF16),
            pltpu.VMEM((2, TH * 3 // 2, 128), BF16),
            pltpu.VMEM((2, PS * 3 // 2, 128), BF16),
            pltpu.VMEM((2, PS * 3 // 2, 128), BF16),
            pltpu.SemaphoreType.DMA((16,)),
            pltpu.SemaphoreType.DMA((PMAX,)),
        ],
        compiler_params=params(60),
        name="slots",
    )(*arrays, jnp.asarray(forward))


def across_edge(value):
    return lax.ppermute(value, "row", [(EDGE - 1, EDGE), (EDGE, EDGE - 1)])


def within_halves(value, step):
    rows = [k for k in range(lax.axis_size("row")) if k // EDGE == (k + step) // EDGE]
    return lax.ppermute(value, "row", [(k, k + step) for k in rows])


def on_device(object_field, probe_field, intensities, positions, tile_counts):
    like = jax.ShapeDtypeStruct
    my_row = lax.axis_index("row")
    where = positions.transpose(0, 2, 3, 1).reshape(-1, positions.shape[1])
    piece = pl.pallas_call(
        cut_kernel,
        out_shape=like((2, HALF, TW), BF16),
        in_specs=[ANY],
        out_specs=VMEM,
        scratch_shapes=[pltpu.VMEM((2, HALF, TW), F32), pltpu.SemaphoreType.DMA],
        compiler_params=params(60),
        cost_estimate=pl.CostEstimate(flops=400_000, bytes_accessed=1_200_000, transcendentals=0),
        name="cut",
    )(object_field)
    across = across_edge(piece)
    strip = like((2, TH * 3 // 2, 128), BF16)
    piece, object_cells = lax.optimization_barrier((piece, object_field))
    head, tail, last, first = pl.pallas_call(
        pieces_kernel,
        out_shape=(like((2, HALF, TW), BF16),) * 2 + (strip,) * 2,
        in_specs=[VMEM],
        out_specs=(VMEM,) * 4,
        compiler_params=params(60),
        cost_estimate=pl.CostEstimate(flops=2_000_000, bytes_accessed=4_000_000, transcendentals=0),
        name="pieces",
    )(object_cells)
    above = within_halves(tail, 1)
    below = within_halves(head, -1)
    before = shifted(last, "col", 1)
    after = shifted(first, "col", -1)
    power = pl.pallas_call(
        power_kernel,
        out_shape=like((3, PS, 128), F32),
        in_specs=[VMEM],
        out_specs=VMEM,
        compiler_params=params(60),
        cost_estimate=pl.CostEstimate(flops=20_000_000, bytes_accessed=20_000_000, transcendentals=0),
        name="power",
    )(probe_field)
    across, above, below, power = lax.optimization_barrier((across, above, below, power))
    last, first = pl.pallas_call(
        corners_kernel,
        out_shape=(like((2, PS * 3 // 2, 128), BF16),) * 2,
        in_specs=[VMEM] * 3,
        out_specs=(VMEM,) * 2,
        compiler_params=params(16),
        cost_estimate=pl.CostEstimate(flops=1_000_000, bytes_accessed=2_000_000, transcendentals=0),
        name="corners",
    )(across, above, below)
    corners_before = shifted(last, "col", 1)
    corners_after = shifted(first, "col", -1)
    field, rim_before, rim_after, rim_above, rim_below, kept, given = slots_call(
        where, tile_counts, object_field, across, above, below, before, after,
        corners_before, corners_after, probe_field, intensities.reshape(PMAX, PS, PS),
    )
    cols, rows = lax.axis_size("col"), lax.axis_size("row")
    device = np.arange(rows * cols).reshape(2, 4, 4, 4, 2)
    plane = device.transpose(0, 2, 4, 1, 3).reshape(-1, 16).tolist()
    line = device.transpose(1, 3, 4, 0, 2).reshape(-1, 8).tolist()
    partner = [(k, k ^ 1) for k in range(cols)]

    def exchanged(pieces, groups):
        return lax.all_to_all(pieces, ("row", "col"), 0, 0, axis_index_groups=groups)

    def total_of(pieces, times, flops):
        return pl.pallas_call(
            total_kernel,
            out_shape=like((times,) + pieces.shape[1:], BF16),
            in_specs=[VMEM],
            out_specs=VMEM,
            compiler_params=params(8),
            cost_estimate=pl.CostEstimate(flops=flops, bytes_accessed=0, transcendentals=0),
            name="total",
        )(pieces)

    arrived = lax.ppermute(given, "col", partner)
    mine = (kept.astype(F32) + arrived.astype(F32)).astype(BF16)
    mine, rim_before, rim_after = lax.optimization_barrier((mine, rim_before, rim_after))
    from_before = shifted(rim_after, "col", 1)
    from_after = shifted(rim_before, "col", -1)
    parts = exchanged(mine.reshape(16, -1, 16, 128), plane)
    sums = total_of(parts, 8, 10_000_000_000)
    parts = exchanged(sums, line)
    swap, up, down = pl.pallas_call(
        merge_kernel,
        out_shape=(like((2, HALF, TW), BF16),) * 3,
        in_specs=[VMEM] * 4,
        out_specs=(VMEM,) * 3,
        compiler_params=params(24),
        cost_estimate=pl.CostEstimate(flops=1_000_000, bytes_accessed=2_000_000, transcendentals=0),
        name="merge",
    )(from_before, from_after, rim_above, rim_below)
    across = across_edge(swap)
    from_below = within_halves(up, -1)
    from_above = within_halves(down, 1)
    sums = total_of(parts, 16, 1_000_000_000)
    half = exchanged(sums, plane).reshape(BLOCKS, 16, 128)
    weight = pl.pallas_call(
        illumination_kernel,
        out_shape=like((TH, TW), F32),
        in_specs=[SMEM, SMEM, VMEM, ANY],
        out_specs=VMEM,
        scratch_shapes=[pltpu.VMEM((CANVAS // 128, CANVAS, 128), F32)],
        compiler_params=params(60),
        cost_estimate=pl.CostEstimate(flops=20_000_000, bytes_accessed=20_000_000, transcendentals=0),
        name="illumination",
    )(where, tile_counts, power, sums)
    new_object = pl.pallas_call(
        object_kernel,
        out_shape=like((2, TH, TW), F32),
        in_specs=[VMEM] * 5 + [ANY],
        out_specs=VMEM,
        compiler_params=params(60),
        cost_estimate=pl.CostEstimate(flops=4_000_000, bytes_accessed=12_000_000, transcendentals=0),
        name="new_object",
    )(object_field, field, from_before, from_after, weight, sums)
    new_object = pl.pallas_call(
        rims_kernel,
        out_shape=like((2, TH, TW), F32),
        in_specs=[ANY, ANY, VMEM, VMEM, VMEM],
        out_specs=ANY,
        scratch_shapes=[
            pltpu.VMEM((2, 2, HALF, TW), F32),
            pltpu.VMEM((2, HALF, TW), F32),
            pltpu.SemaphoreType.DMA((4,)),
            pltpu.SemaphoreType.DMA((2,)),
        ],
        input_output_aliases={0: 0},
        compiler_params=params(16),
        cost_estimate=pl.CostEstimate(flops=40_000_000_000, bytes_accessed=4_000_000, transcendentals=0),
        name="rims",
    )(new_object, weight, across, from_above, from_below)
    half, new_object = lax.optimization_barrier((half, new_object))
    other = lax.ppermute(half, "col", partner)
    new_probe = pl.pallas_call(
        probe_kernel,
        out_shape=like((2, PS, PS), F32),
        in_specs=[VMEM] * 3,
        out_specs=VMEM,
        scratch_shapes=[pltpu.VMEM((2, BLOCKS, 16, 128), BF16), pltpu.VMEM((3, PS, PS), F32)],
        compiler_params=params(24),
        name="new_probe",
    )(half, other, probe_field)
    return (new_object, new_probe)


def solution(mesh):
    placed = (P(None, "row", "col"), P(), P("row", "col", None, None, None), P(), P())
    return jax.shard_map(
        on_device,
        mesh=mesh,
        in_specs=placed,
        out_specs=(P(None, "row", "col"), P()),
        check_vma=False,
    )
```

```python
import functools

import jax
import jax.numpy as jnp
import ml_dtypes
import numpy as np
from jax import lax
from jax.experimental import pallas as pl
from jax.experimental.pallas import tpu as pltpu
from jax.sharding import PartitionSpec as P

OBJECT_REG = 0.1
PROBE_REG = 0.1
PROBE_RATE = 0.5
EPSILON = 1e-06

PS = 384
HALF = 192
TH = 512
TW = 512
PMAX = 6
EH = TH + PS
EW = TW + 512
CANVAS = 1280
USED = 108
BLOCKS = 112
STEP = 128
BAND = 96
PART = 64
EDGE = 4
F32 = jnp.float32
BF16 = jnp.bfloat16


def dft_blocks():
    index = np.arange(PS)
    product = (index[:, None] * index[None, :]) % PS
    angles = product.astype(np.float32) * np.float32(2.0 * np.pi / PS)
    norm = np.float32(1.0) / np.sqrt(np.float32(PS))
    cos = (np.cos(angles) * norm).astype(ml_dtypes.bfloat16)
    sin = (-np.sin(angles) * norm).astype(ml_dtypes.bfloat16)
    forward = np.block([[cos, sin], [-sin, cos]])
    order = np.arange(2 * PS).reshape(2, 3, 128).transpose(1, 0, 2).reshape(-1)
    return forward[:, order]


def lane_parts(column):
    block = column // 128
    return block, column - block * 128


def center_of(positions, row, col, slot):
    at = (row * PMAX + slot) * 2
    return positions[at, col], positions[at + 1, col]


def rolled_out(blocks, shift, lanes):
    turned = [pltpu.roll(b, shift, axis=1) for b in blocks]
    keep = lanes >= shift
    zero = jnp.zeros_like(turned[0])
    return [
        jnp.where(keep, turned[0], zero),
        jnp.where(keep, turned[1], turned[0]),
        jnp.where(keep, turned[2], turned[1]),
        jnp.where(keep, zero, turned[2]),
    ]


def rolled_in(blocks, shift, lanes):
    turned = [pltpu.roll(b, (128 - shift) % 128, axis=1) for b in blocks]
    keep = lanes < 128 - shift
    return [jnp.where(keep, turned[k], turned[k + 1]) for k in range(3)]


def add_windows(tiles, positions, counts, probe, start, canvas, power):
    my_row, my_col = lax.axis_index("row"), lax.axis_index("col")
    for j in range(3):
        cols = pl.ds(j * 128, 128)
        power[j] = probe[0, :, cols] * probe[0, :, cols] + probe[1, :, cols] * probe[1, :, cols]
    first, last = PS // 128, (PS + TW) // 128
    for j in range(first, last):
        here = jnp.zeros((TH, 128), F32) if start is None else start[:, pl.ds((j - first) * 128, 128)]
        canvas[j, pl.ds(PS, TH), :] = here
    lanes = lax.broadcasted_iota(jnp.int32, (BAND, 128), 1)
    grid_r, grid_c = 8, 32

    def tile(k, carry):
        down, across = k // 3 - 1, k % 3 - 1
        row, col = my_row + down, my_col + across
        inside = (row >= 0) & (row < grid_r) & (col >= 0) & (col < grid_c)
        row, col = jnp.where(inside, row, 0), jnp.where(inside, col, 0)
        count = jnp.where(inside, counts[row, col], 0)

        def slot(s, inner):
            top, left = center_of(positions, row, col, s)
            top = top + down * TH - HALF + PS
            left = left + across * TW - HALF + PS
            meets = (top > 0) & (top < PS + TH) & (left > 0) & (left < PS + TW)

            @pl.when(meets)
            def _():
                block, shift = lane_parts(left)
                low = jnp.maximum(PS - top, 0) // BAND
                high = (jnp.minimum(PS + TH - top, PS) + BAND - 1) // BAND

                def band(c, deep):
                    rows = pl.ds(pl.multiple_of(c * BAND, BAND), BAND)
                    parts = rolled_out([power[j, rows, :] for j in range(3)], shift, lanes)
                    for j in range(4):
                        canvas[block + j, pl.ds(top + c * BAND, BAND), :] += parts[j]
                    return deep

                lax.fori_loop(low, high, band, 0)

            return inner

        return lax.fori_loop(0, count, slot, carry)

    for low_tile, high_tile in tiles:
        lax.fori_loop(low_tile, high_tile, tile, 0)


def early_kernel(positions, counts, probe, out, canvas, power):
    add_windows(((3, 5),), positions, counts, probe, None, canvas, power)
    for j in range(TW // 128):
        out[:, pl.ds(j * 128, 128)] = canvas[PS // 128 + j, pl.ds(PS, TH), :]


def illumination_kernel(positions, counts, probe, start, earlier, out, canvas, power):
    del earlier
    add_windows(((0, 3), (5, 9)), positions, counts, probe, start, canvas, power)
    floor = OBJECT_REG * jnp.max(power[...])
    for j in range(TW // 128):
        out[:, pl.ds(j * 128, 128)] = 1.0 / (canvas[PS // 128 + j, pl.ds(PS, TH), :] + floor)


def main_kernel(
    positions, counts, center, across_in, above_in, below_in, before_in, after_in,
    corners_before_in, corners_after_in, probe_in, intensity_in, forward_in,
    field, rim_before, rim_after, rim_above, rim_below, kept, given,
    extended, total, wave, halfway, residual, returning, turned, window, probe_sum,
    probe, intensity, forward, adjoint, above, below, before, after, corners_before, corners_after,
    copied, slot_copied,
):
    my_row, my_col = lax.axis_index("row"), lax.axis_index("col")
    count = counts[my_row, my_col]

    def inward(s):
        return pltpu.make_async_copy(intensity_in.at[s], intensity.at[s], slot_copied.at[s])

    pairs = [(before_in, before), (after_in, after)]
    pairs += [(corners_before_in, corners_before), (corners_after_in, corners_after)]
    pairs += [(probe_in, probe), (forward_in, forward)]
    for p in range(2):
        for j in range(4):
            pairs.append((center.at[p, :, pl.ds(j * 128, 128)], extended.at[p, j + 2, pl.ds(HALF, TH), :]))
    copies = [pltpu.make_async_copy(a, b, copied.at[k]) for k, (a, b) in enumerate(pairs)]
    rims = ((above_in, above, my_row == EDGE), (below_in, below, my_row == EDGE - 1))
    for k, (rim_in, rim, from_across) in enumerate(rims):
        near = pltpu.make_async_copy(rim_in, rim, copied.at[14 + k])
        pl.when(from_across)(pltpu.make_async_copy(across_in, rim, copied.at[14 + k]).start)
        pl.when(jnp.logical_not(from_across))(near.start)
        copies.insert(0, near)
    for copy in copies[2:]:
        copy.start()
    lax.fori_loop(0, count, lambda s, carry: (inward(s).start(), carry)[1], 0)
    total[...] = jnp.zeros_like(total)
    probe_sum[...] = jnp.zeros_like(probe_sum)
    for copy in copies[:6]:
        copy.wait()
    for p in range(2):
        for j in range(2, 6):
            cols = pl.ds((j - 2) * 128, 128)
            extended[p, j, pl.ds(0, HALF), :] = above[p, :, cols].astype(F32)
            extended[p, j, pl.ds(HALF + TH, HALF), :] = below[p, :, cols].astype(F32)
        for middle, corners, whole, part in ((before, corners_before, 1, 0), (after, corners_after, 6, 7)):
            extended[p, whole, pl.ds(0, HALF), :] = corners[p, pl.ds(0, HALF), :].astype(F32)
            extended[p, whole, pl.ds(HALF, TH), :] = middle[p, pl.ds(0, TH), :].astype(F32)
            extended[p, whole, pl.ds(HALF + TH, HALF), :] = corners[p, pl.ds(HALF, HALF), :].astype(F32)
            for piece, rows, top, low in ((corners, HALF, 0, HALF + TH), (middle, TH // 2, HALF, HALF + TH // 2)):
                found = piece[p, pl.ds(2 * rows, rows), :].astype(F32)
                turned_half = pltpu.roll(found, 64, axis=1)
                extended[p, part, pl.ds(top, rows), :] = found if part else turned_half
                extended[p, part, pl.ds(low, rows), :] = turned_half if part else found
    for copy in copies[6:]:
        copy.wait()
    for k in range(2):
        for j in range(6):
            here = (pl.ds(k * PS, PS), pl.ds(j * 128, 128))
            adjoint[here] = forward[here] if k == j % 2 else -forward[here]

    def place_of(s):
        top, left = center_of(positions, my_row, my_col, s)
        return (top,) + lane_parts(left + 64)

    def leave(s, k):
        top, block, shift = place_of(s)
        lanes = lax.broadcasted_iota(jnp.int32, (PART, 128), 1)
        for at in range(k * 128, (k + 1) * 128, PART):
            rows = pl.ds(at, PART)
            cells = []
            for p in range(2):
                found = [extended[p, block + j, pl.ds(top + at, PART), :] for j in range(4)]
                cells.append(jnp.concatenate(rolled_in(found, shift, lanes), axis=1))
                window[s % 2, p, rows, :] = cells[p]
            pr, pi = probe[0, rows, :], probe[1, rows, :]
            wave[pl.ds(k * 128 + at, PART), :] = (pr * cells[0] - pi * cells[1]).astype(BF16)
            wave[pl.ds(k * 128 + at + 128, PART), :] = (pr * cells[1] + pi * cells[0]).astype(BF16)

    for k in range(3):
        leave(0, k)

    def slot(s, carry):
        top, block, shift = place_of(s)
        half = jnp.dot(adjoint[...], wave[...], preferred_element_type=F32).astype(BF16)
        halfway[:, pl.ds(0, PS)] = half[:PS]
        halfway[:, pl.ds(PS, PS)] = half[PS:]
        inward(s).wait()
        for j in range(3):
            cols = pl.ds(j * 128, 128)
            far = jnp.dot(halfway[...], forward[:, pl.ds(j * 256, 256)], preferred_element_type=F32)
            far_r, far_i = far[:, :128], far[:, 128:]
            misfit = far_r * far_r + far_i * far_i - intensity[s, :, cols].astype(F32)
            real, imaginary = (misfit * far_r).astype(BF16), (misfit * far_i).astype(BF16)
            for k in range(3):
                residual[pl.ds(k * 256, 128), cols] = real[k * 128 : (k + 1) * 128]
                residual[pl.ds(k * 256 + 128, 128), cols] = imaginary[k * 128 : (k + 1) * 128]
            leave(jnp.minimum(s + 1, count - 1), j)
        back = jnp.dot(forward[...], residual[...], preferred_element_type=F32).astype(BF16)
        returning[:, pl.ds(0, PS)] = back[:PS]
        returning[:, pl.ds(PS, PS)] = back[PS:]
        lanes = lax.broadcasted_iota(jnp.int32, (PART, 128), 1)
        for j in range(3):
            cols = pl.ds(j * 128, 128)
            gradient = jnp.dot(returning[...], adjoint[:, pl.ds(j * 256, 256)], preferred_element_type=F32)
            for k in range(PS // PART):
                rows = pl.ds(k * PART, PART)
                gr, gi = gradient[k * PART : (k + 1) * PART, :128], gradient[k * PART : (k + 1) * PART, 128:]
                pr, pi = probe[0, rows, cols], probe[1, rows, cols]
                wr, wi = window[s % 2, 0, rows, cols], window[s % 2, 1, rows, cols]
                for p, term in ((0, pr * gr + pi * gi), (1, pr * gi - pi * gr)):
                    term = pltpu.roll(term, shift, axis=1)
                    past = turned[p, rows, :] if j else jnp.zeros_like(term)
                    total[p, block + j, pl.ds(top + k * PART, PART), :] += jnp.where(lanes >= shift, term, past)
                    if j < 2:
                        turned[p, rows, :] = term
                    else:
                        total[p, block + 3, pl.ds(top + k * PART, PART), :] += jnp.where(lanes < shift, term, 0.0)
                probe_sum[0, rows, cols] += wr * gr + wi * gi
                probe_sum[1, rows, cols] += wr * gi - wi * gr
                probe_sum[2, rows, cols] += wr * wr + wi * wi
        return carry

    lax.fori_loop(0, count, slot, 0)
    pairs = []
    for p in range(2):
        for j in range(4):
            cols = pl.ds(j * 128, 128)
            pairs.append((total.at[p, j + 2, pl.ds(HALF, TH), :], field.at[p, :, cols]))
    copies = [pltpu.make_async_copy(a, b, copied.at[k]) for k, (a, b) in enumerate(pairs)]
    for copy in copies:
        copy.start()
    lanes = lax.broadcasted_iota(jnp.int32, (EH // 2, 128), 1)
    for p in range(2):
        for j in range(2, 6):
            cols = pl.ds((j - 2) * 128, 128)
            rim_above[p, :, cols] = total[p, j, pl.ds(0, HALF), :].astype(BF16)
            rim_below[p, :, cols] = total[p, j, pl.ds(HALF + TH, HALF), :].astype(BF16)
        for rim, whole, part in ((rim_before, 1, 0), (rim_after, 6, 7)):
            rim[p, pl.ds(0, EH), :] = total[p, whole].astype(BF16)
            upper, lower = total[p, part, pl.ds(0, EH // 2), :], total[p, part, pl.ds(EH // 2, EH // 2), :]
            if part:
                lower = pltpu.roll(lower, 64, axis=1)
            else:
                upper = pltpu.roll(upper, 64, axis=1)
            rim[p, pl.ds(EH, EH // 2), :] = jnp.where(lanes < 64, upper, lower).astype(BF16)
    for core in range(2):

        @pl.when(my_col % 2 == core)
        def _():
            for ref, half, kind in ((kept, core, BF16), (given, 1 - core, BF16)):
                for at in range(BLOCKS):
                    if at < USED:
                        found = half * USED + at
                        p, k, j = found // 72, found // 3 % 24, found % 3
                        ref[at] = probe_sum[p, pl.ds(k * 16, 16), pl.ds(j * 128, 128)].astype(kind)
                    else:
                        ref[at] = jnp.zeros((16, 128), kind)

    for copy in copies:
        copy.wait()


def total_kernel(pieces, out):
    total = pieces[0].astype(F32)
    for k in range(1, pieces.shape[0]):
        total = total + pieces[k].astype(F32)
    for k in range(out.shape[0]):
        out[k] = total.astype(BF16)


def cut_kernel(cells, out, piece, copied):
    first = jnp.where(lax.axis_index("row") == EDGE, 0, TH - HALF)
    copy = pltpu.make_async_copy(cells.at[:, pl.ds(pl.multiple_of(first, 64), HALF), :], piece, copied)
    copy.start()
    copy.wait()
    out[...] = piece[...].astype(BF16)


def beside(upper, lower, from_upper_lanes):
    lanes = lax.broadcasted_iota(jnp.int32, upper.shape, 1)
    if from_upper_lanes:
        return jnp.where(lanes < 64, pltpu.roll(upper, 64, axis=1), lower)
    return jnp.where(lanes < 64, upper, pltpu.roll(lower, 64, axis=1))


def pieces_kernel(cells, head, tail, last, first):
    half = TH // 2
    for p in range(2):
        head[p] = cells[p, pl.ds(0, HALF), :].astype(BF16)
        tail[p] = cells[p, pl.ds(TH - HALF, HALF), :].astype(BF16)
        for out, whole, part in ((last, 384, 256), (first, 0, 128)):
            out[p, pl.ds(0, TH), :] = cells[p, :, pl.ds(whole, 128)].astype(BF16)
            upper, lower = cells[p, pl.ds(0, half), pl.ds(part, 128)], cells[p, pl.ds(half, half), pl.ds(part, 128)]
            out[p, pl.ds(TH, half), :] = beside(upper, lower, part == 256).astype(BF16)


def corners_kernel(across, above, below, last, first):
    my_row = lax.axis_index("row")
    for p in range(2):
        for out, whole, part in ((last, 384, 256), (first, 0, 128)):

            def block(at):
                cols = pl.ds(at, 128)
                far = across[p, :, cols].astype(F32)
                top = jnp.where(my_row == EDGE, far, above[p, :, cols].astype(F32))
                return top, jnp.where(my_row == EDGE - 1, far, below[p, :, cols].astype(F32))

            top, bottom = block(whole)
            out[p, pl.ds(0, HALF), :] = top.astype(BF16)
            out[p, pl.ds(HALF, HALF), :] = bottom.astype(BF16)
            out[p, pl.ds(2 * HALF, HALF), :] = beside(*block(part), part == 256).astype(BF16)


def merge_kernel(from_before, from_after, rim_above, rim_below, swap, up, down):
    my_row = lax.axis_index("row")
    lanes = lax.broadcasted_iota(jnp.int32, (HALF, 128), 1)
    for p in range(2):
        sums = []
        for rim, rows, halves, lower in (
            (rim_above, pl.ds(0, HALF), pl.ds(EH, HALF), False),
            (rim_below, pl.ds(EH - HALF, HALF), pl.ds(EH * 3 // 2 - HALF, HALF), True),
        ):
            left, right = from_before[p, halves, :].astype(F32), from_after[p, halves, :].astype(F32)
            if lower:
                left = pltpu.roll(left, 64, axis=1)
            else:
                right = pltpu.roll(right, 64, axis=1)
            blocks = [
                from_before[p, rows, :].astype(F32),
                jnp.where(lanes < 64, left, 0.0),
                jnp.where(lanes >= 64, right, 0.0),
                from_after[p, rows, :].astype(F32),
            ]
            sums.append(rim[p].astype(F32) + jnp.concatenate(blocks, axis=1))
        up[p] = sums[0].astype(BF16)
        down[p] = sums[1].astype(BF16)
        swap[p] = jnp.where(my_row == EDGE, sums[0], sums[1]).astype(BF16)


def object_kernel(center, field, from_before, from_after, weight, earlier, out):
    del earlier
    lanes = lax.broadcasted_iota(jnp.int32, (64, 128), 1)
    for k in range(TH // 64):
        rows = pl.ds(k * 64, 64)
        outer = pl.ds(HALF + k * 64, 64)
        upper = HALF + k * 64 < EH // 2
        halves = pl.ds(EH + (HALF + k * 64) % (EH // 2), 64)
        for p in range(2):
            left, right = from_before[p, halves, :].astype(F32), from_after[p, halves, :].astype(F32)
            if upper:
                right = pltpu.roll(right, 64, axis=1)
            else:
                left = pltpu.roll(left, 64, axis=1)
            sides = [
                from_before[p, outer, :].astype(F32),
                jnp.where(lanes < 64, left, 0.0),
                jnp.where(lanes >= 64, right, 0.0),
                from_after[p, outer, :].astype(F32),
            ]
            cells = field[p, rows, :] + jnp.concatenate(sides, axis=1)
            out[p, rows, :] = center[p, rows, :] - cells * weight[rows, :]


def rims_kernel(base, weight_in, across, from_above, from_below, out, cells, weight, arrived, left):
    my_row = lax.axis_index("row")
    places = (pl.ds(0, HALF), pl.ds(TH - HALF, HALF))
    inward, outward = [], []
    for k, rows in enumerate(places):
        inward.append(pltpu.make_async_copy(base.at[:, rows, :], cells.at[k], arrived.at[k]))
        inward.append(pltpu.make_async_copy(weight_in.at[rows, :], weight.at[k], arrived.at[2 + k]))
        outward.append(pltpu.make_async_copy(cells.at[k], out.at[:, rows, :], left.at[k]))
    for copy in inward:
        copy.start()
    for k, (near, edge) in enumerate(((from_above, EDGE), (from_below, EDGE - 1))):
        inward[2 * k].wait()
        inward[2 * k + 1].wait()
        for p in range(2):
            rim = jnp.where(my_row == edge, across[p].astype(F32), near[p].astype(F32))
            cells[k, p] = cells[k, p] - rim * weight[k]
        outward[k].start()
    for copy in outward:
        copy.wait()


def probe_kernel(half, other, probe, out, sums, planes):
    core = lax.axis_index("col") % 2
    sums[core] = half[...]
    sums[1 - core] = other[...]
    for found in range(2 * USED):
        p, k, j = found // 72, found // 3 % 24, found % 3
        planes[p, pl.ds(k * 16, 16), pl.ds(j * 128, 128)] = sums[found // USED, found % USED].astype(F32)
    floor = PROBE_REG * jnp.max(planes[2])
    square = jnp.zeros((STEP, PS), F32)
    for k in range(PS // STEP):
        rows = pl.ds(k * STEP, STEP)
        weight = 1.0 / (planes[2, rows, :] + floor)
        for p in range(2):
            direction = planes[p, rows, :] * weight
            planes[p, rows, :] = direction
            square = square + direction * direction
    spread = jnp.sqrt(jnp.sum(square) / (PS * PS) + EPSILON)
    for p in range(2):
        out[p] = probe[p] - PROBE_RATE * planes[p] / spread


SMEM = pl.BlockSpec(memory_space=pltpu.SMEM)
VMEM = pl.BlockSpec(memory_space=pltpu.VMEM)
ANY = pl.BlockSpec(memory_space=pl.ANY)


def params(mib):
    return pltpu.CompilerParams(vmem_limit_bytes=mib << 20)


def shifted(value, axis, step):
    size = lax.axis_size(axis)
    low, high = max(0, -step), min(size, size - step)
    return lax.ppermute(value, axis, [(k, k + step) for k in range(low, high)])


def slots_call(*arrays):
    like = jax.ShapeDtypeStruct
    forward = dft_blocks()
    return pl.pallas_call(
        main_kernel,
        out_shape=(
            like((2, TH, TW), F32),
            like((2, EH * 3 // 2, 128), BF16),
            like((2, EH * 3 // 2, 128), BF16),
            like((2, HALF, TW), BF16),
            like((2, HALF, TW), BF16),
            like((BLOCKS, 16, 128), BF16),
            like((BLOCKS, 16, 128), BF16),
        ),
        in_specs=[SMEM] * 2 + [ANY] * 11,
        out_specs=(ANY,) + (VMEM,) * 6,
        scratch_shapes=[
            pltpu.VMEM((2, EW // 128, EH, 128), F32),
            pltpu.VMEM((2, EW // 128, EH, 128), F32),
            pltpu.VMEM((2 * PS, PS), BF16),
            pltpu.VMEM((PS, 2 * PS), BF16),
            pltpu.VMEM((2 * PS, PS), BF16),
            pltpu.VMEM((PS, 2 * PS), BF16),
            pltpu.VMEM((2, PS, 128), F32),
            pltpu.VMEM((2, 2, PS, PS), F32),
            pltpu.VMEM((3, PS, PS), F32),
            pltpu.VMEM((2, PS, PS), F32),
            pltpu.VMEM((PMAX, PS, PS), BF16),
            pltpu.VMEM((2 * PS, 2 * PS), BF16),
            pltpu.VMEM((2 * PS, 2 * PS), BF16),
            pltpu.VMEM((2, HALF, TW), BF16),
            pltpu.VMEM((2, HALF, TW), BF16),
            pltpu.VMEM((2, TH * 3 // 2, 128), BF16),
            pltpu.VMEM((2, TH * 3 // 2, 128), BF16),
            pltpu.VMEM((2, PS * 3 // 2, 128), BF16),
            pltpu.VMEM((2, PS * 3 // 2, 128), BF16),
            pltpu.SemaphoreType.DMA((16,)),
            pltpu.SemaphoreType.DMA((PMAX,)),
        ],
        compiler_params=params(60),
        name="slots",
    )(*arrays, jnp.asarray(forward))


def across_edge(value):
    return lax.ppermute(value, "row", [(EDGE - 1, EDGE), (EDGE, EDGE - 1)])


def within_halves(value, step):
    rows = [k for k in range(lax.axis_size("row")) if k // EDGE == (k + step) // EDGE]
    return lax.ppermute(value, "row", [(k, k + step) for k in rows])


def on_device(object_field, probe_field, intensities, positions, tile_counts):
    like = jax.ShapeDtypeStruct
    my_row = lax.axis_index("row")
    where = positions.transpose(0, 2, 3, 1).reshape(-1, positions.shape[1])
    piece = pl.pallas_call(
        cut_kernel,
        out_shape=like((2, HALF, TW), BF16),
        in_specs=[ANY],
        out_specs=VMEM,
        scratch_shapes=[pltpu.VMEM((2, HALF, TW), F32), pltpu.SemaphoreType.DMA],
        compiler_params=params(60),
        cost_estimate=pl.CostEstimate(flops=400_000, bytes_accessed=1_200_000, transcendentals=0),
        name="cut",
    )(object_field)
    across = across_edge(piece)
    strip = like((2, TH * 3 // 2, 128), BF16)
    piece, object_cells = lax.optimization_barrier((piece, object_field))
    head, tail, last, first = pl.pallas_call(
        pieces_kernel,
        out_shape=(like((2, HALF, TW), BF16),) * 2 + (strip,) * 2,
        in_specs=[VMEM],
        out_specs=(VMEM,) * 4,
        compiler_params=params(60),
        cost_estimate=pl.CostEstimate(flops=2_000_000, bytes_accessed=4_000_000, transcendentals=0),
        name="pieces",
    )(object_cells)
    above = within_halves(tail, 1)
    below = within_halves(head, -1)
    before = shifted(last, "col", 1)
    after = shifted(first, "col", -1)
    windows = [pltpu.VMEM((CANVAS // 128, CANVAS, 128), F32), pltpu.VMEM((3, PS, 128), F32)]
    early = pl.pallas_call(
        early_kernel,
        out_shape=like((TH, TW), F32),
        in_specs=[SMEM, SMEM, VMEM],
        out_specs=VMEM,
        scratch_shapes=windows,
        compiler_params=params(60),
        cost_estimate=pl.CostEstimate(flops=20_000_000, bytes_accessed=20_000_000, transcendentals=0),
        name="early",
    )(where, tile_counts, probe_field)
    across, above, below, early = lax.optimization_barrier((across, above, below, early))
    last, first = pl.pallas_call(
        corners_kernel,
        out_shape=(like((2, PS * 3 // 2, 128), BF16),) * 2,
        in_specs=[VMEM] * 3,
        out_specs=(VMEM,) * 2,
        compiler_params=params(16),
        cost_estimate=pl.CostEstimate(flops=1_000_000, bytes_accessed=2_000_000, transcendentals=0),
        name="corners",
    )(across, above, below)
    corners_before = shifted(last, "col", 1)
    corners_after = shifted(first, "col", -1)
    field, rim_before, rim_after, rim_above, rim_below, kept, given = slots_call(
        where, tile_counts, object_field, across, above, below, before, after,
        corners_before, corners_after, probe_field, intensities.reshape(PMAX, PS, PS),
    )
    cols, rows = lax.axis_size("col"), lax.axis_size("row")
    device = np.arange(rows * cols).reshape(2, 4, 4, 4, 2)
    plane = device.transpose(0, 2, 4, 1, 3).reshape(-1, 16).tolist()
    line = device.transpose(1, 3, 4, 0, 2).reshape(-1, 8).tolist()
    partner = [(k, k ^ 1) for k in range(cols)]

    def exchanged(pieces, groups):
        return lax.all_to_all(pieces, ("row", "col"), 0, 0, axis_index_groups=groups)

    def total_of(pieces, times, flops):
        return pl.pallas_call(
            total_kernel,
            out_shape=like((times,) + pieces.shape[1:], BF16),
            in_specs=[VMEM],
            out_specs=VMEM,
            compiler_params=params(8),
            cost_estimate=pl.CostEstimate(flops=flops, bytes_accessed=0, transcendentals=0),
            name="total",
        )(pieces)

    arrived = lax.ppermute(given, "col", partner)
    mine = (kept.astype(F32) + arrived.astype(F32)).astype(BF16)
    mine, rim_before, rim_after = lax.optimization_barrier((mine, rim_before, rim_after))
    from_before = shifted(rim_after, "col", 1)
    from_after = shifted(rim_before, "col", -1)
    parts = exchanged(mine.reshape(16, -1, 16, 128), plane)
    sums = total_of(parts, 8, 10_000_000_000)
    parts = exchanged(sums, line)
    swap, up, down = pl.pallas_call(
        merge_kernel,
        out_shape=(like((2, HALF, TW), BF16),) * 3,
        in_specs=[VMEM] * 4,
        out_specs=(VMEM,) * 3,
        compiler_params=params(24),
        cost_estimate=pl.CostEstimate(flops=1_000_000, bytes_accessed=2_000_000, transcendentals=0),
        name="merge",
    )(from_before, from_after, rim_above, rim_below)
    across = across_edge(swap)
    from_below = within_halves(up, -1)
    from_above = within_halves(down, 1)
    sums = total_of(parts, 16, 1_000_000_000)
    half = exchanged(sums, plane).reshape(BLOCKS, 16, 128)
    weight = pl.pallas_call(
        illumination_kernel,
        out_shape=like((TH, TW), F32),
        in_specs=[SMEM, SMEM, VMEM, VMEM, ANY],
        out_specs=VMEM,
        scratch_shapes=windows,
        compiler_params=params(60),
        cost_estimate=pl.CostEstimate(flops=20_000_000, bytes_accessed=20_000_000, transcendentals=0),
        name="illumination",
    )(where, tile_counts, probe_field, early, sums)
    new_object = pl.pallas_call(
        object_kernel,
        out_shape=like((2, TH, TW), F32),
        in_specs=[VMEM] * 5 + [ANY],
        out_specs=VMEM,
        compiler_params=params(60),
        cost_estimate=pl.CostEstimate(flops=4_000_000, bytes_accessed=12_000_000, transcendentals=0),
        name="new_object",
    )(object_field, field, from_before, from_after, weight, sums)
    new_object = pl.pallas_call(
        rims_kernel,
        out_shape=like((2, TH, TW), F32),
        in_specs=[ANY, ANY, VMEM, VMEM, VMEM],
        out_specs=ANY,
        scratch_shapes=[
            pltpu.VMEM((2, 2, HALF, TW), F32),
            pltpu.VMEM((2, HALF, TW), F32),
            pltpu.SemaphoreType.DMA((4,)),
            pltpu.SemaphoreType.DMA((2,)),
        ],
        input_output_aliases={0: 0},
        compiler_params=params(16),
        cost_estimate=pl.CostEstimate(flops=40_000_000_000, bytes_accessed=4_000_000, transcendentals=0),
        name="rims",
    )(new_object, weight, across, from_above, from_below)
    half, new_object = lax.optimization_barrier((half, new_object))
    other = lax.ppermute(half, "col", partner)
    new_probe = pl.pallas_call(
        probe_kernel,
        out_shape=like((2, PS, PS), F32),
        in_specs=[VMEM] * 3,
        out_specs=VMEM,
        scratch_shapes=[pltpu.VMEM((2, BLOCKS, 16, 128), BF16), pltpu.VMEM((3, PS, PS), F32)],
        compiler_params=params(24),
        name="new_probe",
    )(half, other, probe_field)
    return (new_object, new_probe)


def solution(mesh):
    placed = (P(None, "row", "col"), P(), P("row", "col", None, None, None), P(), P())
    return jax.shard_map(
        on_device,
        mesh=mesh,
        in_specs=placed,
        out_specs=(P(None, "row", "col"), P()),
        check_vma=False,
    )
```
